32 devices in a mesh: rep: 8 (over y, x, core), shard: 4 (over z).
Axes of the slice: x: 2, y: 2, z: 4, core: 2. Of those that a mesh axis runs over, the one named last changes fastest.
Arguments:
- tokens: bfloat16 [8192, 1024], P(('rep', 'shard')), may hold values from -6 to 6
- cotangent: bfloat16 [8192, 1024], P(('rep', 'shard')), may hold values from -6 to 6
- segment_ids: int32 [8192], P(('rep', 'shard')), may hold values from 0 to 6, as said below
- routes: int32 [8192, 8], P(('rep', 'shard')), may hold values from 0 to 15, all different within a row; in each aligned block of 256 rows (0 to 255, 256 to 511, ...) at most 160 rows name the same one
- attn_gain: bfloat16 [1024], P('shard'), may hold values from 0.5 to 1.5
- query_weight: bfloat16 [1024, 1024], P('shard'), may hold values from -0.1875 to 0.1875
- key_matrix: bfloat16 [1024, 512], P('shard'), may hold values from -0.1875 to 0.1875
- value_weight: bfloat16 [1024, 512], P('shard'), may hold values from -0.1875 to 0.1875
- out_weight: bfloat16 [1024, 1024], P(None, 'shard'), may hold values from -0.75 to 0.75
- ffn_gain: bfloat16 [1024], P('shard'), may hold values from 0.5 to 1.5
- router_weight: bfloat16 [1024, 16], P('shard'), may hold values from -0.09375 to 0.09375
- gate_weight: bfloat16 [16, 1024, 512], P(None, 'shard'), may hold values from -0.1875 to 0.1875
- up_weight: bfloat16 [16, 1024, 512], P(None, 'shard'), may hold values from -0.1875 to 0.1875
- down_weight: bfloat16 [16, 512, 1024], P(None, 'shard'), may hold values from -1 to 1
Outputs:
- output: bfloat16 [8192, 1024], P(('rep', 'shard'))
- input_grad: float32 [8192, 1024], P(('rep', 'shard'))
- attn_gain_grad: float32 [1024], P('shard')
- query_weight_grad: float32 [1024, 1024], P('shard')
- key_weight_grad: float32 [1024, 512], P('shard')
- value_weight_grad: float32 [1024, 512], P('shard')
- out_weight_grad: float32 [1024, 1024], P(None, 'shard')
- ffn_gain_grad: float32 [1024], P('shard')
- router_weight_grad: float32 [1024, 16], P('shard')
- gate_weight_grad: float32 [16, 1024, 512], P(None, 'shard')
- up_weight_grad: float32 [16, 1024, 512], P(None, 'shard')
- down_weight_grad: float32 [16, 512, 1024], P(None, 'shard')
The draws below stay inside these ranges and needn't reach their ends.
Inputs may be any that keep to these rules, and one draw needn't show every extreme that they name: `segment_ids`: within each packed sequence of 1024 tokens the ids start at 0, never fall, and end at 6. `routes`: each row names 8 different experts. Among the rows of one device no expert is named more than 160 times, and in every draw some expert is named exactly 160 times by the rows of some device.
All inputs are finite; a program needn't handle non-finite values.
Results may differ from the reference program's by a relative error of at most 0.022.
Values may be sent and summed in bfloat16 or wider, within the bound.
No kernel may reach another device: no remote copies, remote signals or barrier semaphores. Data moves between devices by JAX's collectives and lax.ppermute only.
A program may use at most 320 MiB of HBM per device.

```python
import math
from functools import partial
import jax
import jax.numpy as jnp
import numpy as np
from jax import lax

D = 1024
QUERY_HEADS = 16
KEY_VALUE_HEADS = 8
HEAD_SIZE = 64
FF = 512
TOP = 8
E = 16
TOK_DEV = 256
SEQ = 1024
TOKENS = 8192
QW = 1024
KVW = 512
CAP = 160


def draw_segment_ids(key, part):
    key = jax.random.fold_in(key, 7)
    keys = jax.random.split(key, 6)
    seq_count = TOKENS // SEQ
    quarter = TOK_DEV // 4
    places = jnp.arange(SEQ, dtype=jnp.int32)[None, :]
    doc_first = jax.random.randint(keys[0], (seq_count, 1), quarter + 1, TOK_DEV // 2 + 1)
    doc_last = jax.random.randint(keys[1], (seq_count, 1), SEQ - TOK_DEV // 2, SEQ - quarter)
    front_mid = doc_first // 2
    back_mid = (doc_last + SEQ) // 2
    cut_one = jax.random.randint(keys[2], (seq_count, 1), 0, 1 << 20) % front_mid + 1
    cut_two = front_mid + 1 + jax.random.randint(keys[3], (seq_count, 1), 0, 1 << 20) % (doc_first - 1 - front_mid)
    cut_three = doc_last + 1 + jax.random.randint(keys[4], (seq_count, 1), 0, 1 << 20) % (back_mid - doc_last)
    cut_four = back_mid + 1 + jax.random.randint(keys[5], (seq_count, 1), 0, 1 << 20) % (SEQ - 1 - back_mid)
    cut_flags = (places == cut_one) | (places == cut_two) | (places == doc_first) | (places == doc_last) | (places == cut_three) | (places == cut_four)
    return jnp.cumsum(cut_flags.astype(jnp.int32), axis=1).astype(jnp.int32).reshape(TOKENS)


def level_of(stream_key, shape, shards, low, high):
    def one(position, shards_of):
        heights = jax.random.uniform(jax.random.fold_in(jax.random.fold_in(stream_key, 6), position), (shards_of,), jnp.float32, low / len(shards), high / len(shards))
        return jnp.repeat(jnp.exp(heights), shape[position] // shards_of).reshape((-1,) + (1,) * (len(shape) - position - 1))

    gain = one(*shards[0])
    for cut in shards[1:]:
        gain = gain * one(*cut)
    return gain


def assign_block(key, own, number, rows, count, top, reach, slope):
    sequence = jax.random.permutation(key, count)
    packed, ordinary = shares(count, rows * top, reach, slope, True), shares(count, rows * top, reach, slope, False)
    places = jnp.arange(count)

    def named(tallies, rotation):
        used = int((tallies > 0).sum())
        fixed = max(1, used // 4)
        shifted = fixed + (places - fixed + rotation * (used - fixed)) % max(1, count - fixed)
        return jnp.zeros((count,), jnp.int32).at[sequence[jnp.where(places < fixed, places, shifted)]].set(jnp.asarray(tallies, jnp.int32))

    tallies = jnp.where(number % 4 == 0, named(packed, number // 4), named(ordinary, number - number // 4 - 1))
    mixed = jax.random.permutation(jax.random.fold_in(own, 3), count)
    source_of, taker = mixed[0:count // 2 * 2:2], mixed[1:count // 2 * 2:2]
    slack = jnp.minimum(tallies[source_of] - 1, reach - tallies[taker]) // 2
    slack = jnp.where((source_of == sequence[0]) | (taker == sequence[0]) | (tallies[taker] == 0), 0, jnp.maximum(slack, 0))
    shifted = jax.random.randint(jax.random.fold_in(own, 4), (count // 2,), 0, 1 << 20) % (slack + 1)
    tallies = tallies.at[source_of].add(-shifted).at[taker].add(shifted)
    items = jnp.searchsorted(jnp.cumsum(tallies), jnp.arange(rows * top), side="right").astype(jnp.int32)
    grid = items.reshape(top, rows).T
    grid = grid[jax.random.permutation(jax.random.fold_in(own, 1), rows)]
    rotation = jax.random.randint(jax.random.fold_in(own, 2), (rows, 1), 0, top)
    return jnp.take_along_axis(grid, (jnp.arange(top)[None, :] + rotation) % top, axis=1)


def shares(count, total, most, slope, full):
    weights = [(1 << 20) // math.isqrt(grade ** slope) + 1 for grade in range(1, count + 1)]
    largest = most if full else min(most, max(-(-total // count), total * weights[0] // sum(weights)))
    least = 1 if total - largest >= count - 1 else 0
    holding, surplus = [largest] + [least] * (count - 1), total - largest - least * (count - 1)
    while surplus > 0:
        free = [i for i in range(1, count) if holding[i] < largest] or [i for i in range(1, count) if holding[i] < most]
        mass, budget = sum([weights[i] for i in free]), surplus
        for i in free:
            addition = min(most - holding[i], max(1, budget * weights[i] // mass), surplus)
            holding[i] = holding[i] + addition
            surplus = surplus - addition
    return np.array(holding)


def scatter_about(stream_key, shape, scale, limit, pieces=(), kind=jnp.bfloat16):
    level = level_of(stream_key, shape, pieces, -0.22, 0.18) if pieces else 1.0
    drawn = jax.random.normal(stream_key, shape, jnp.float32) * scale * level
    return jnp.minimum(jnp.maximum(drawn, -limit), limit).astype(kind)


def setup_inputs(seed: int = 0) -> dict:
    splits = jax.random.split(jax.random.key(seed), 15)
    tokens = scatter_about(splits[0], (TOKENS, D), 1.0, 6.0, ((0, 32),))
    cotangent = scatter_about(splits[1], (TOKENS, D), 1.0, 6.0, ((0, 32),))
    segment_ids = draw_segment_ids(jax.random.fold_in(splits[14], 71), 0)
    routes_keys = jax.random.split(jax.random.fold_in(splits[3], 1), TOKENS // TOK_DEV)
    routes_turns = jax.random.permutation(jax.random.fold_in(splits[3], 3), TOKENS // TOK_DEV)
    routes = jax.vmap(lambda own, number: assign_block(jax.random.fold_in(splits[3], 2), own, number, TOK_DEV, E, TOP, CAP, 0))(routes_keys, routes_turns).reshape((TOKENS, TOP))
    attn_gain = jnp.clip(1.0 + 0.1 * jax.random.normal(splits[4], (D,), jnp.float32), 0.5, 1.5).astype(jnp.bfloat16)
    query_weight = scatter_about(splits[5], (D, QW), D ** -0.5, 0.1875, ((0, 4),))
    key_matrix = scatter_about(splits[6], (D, KVW), D ** -0.5, 0.1875, ((0, 4),))
    value_weight = scatter_about(splits[7], (D, KVW), D ** -0.5, 0.1875, ((0, 4),))
    out_weight = scatter_about(splits[8], (QW, D), (QW // 16) ** -0.5, 0.75, ((1, 4),))
    ffn_gain = jnp.clip(1.0 + 0.1 * jax.random.normal(splits[9], (D,), jnp.float32), 0.5, 1.5).astype(jnp.bfloat16)
    router_weight = scatter_about(splits[10], (D, E), (4 * D) ** -0.5, 0.09375, ((0, 4),))
    gate_weight = scatter_about(splits[11], (E, D, FF), D ** -0.5, 0.1875, ((1, 4),))
    up_weight = scatter_about(splits[12], (E, D, FF), D ** -0.5, 0.1875, ((1, 4),))
    down_weight = scatter_about(splits[13], (E, FF, D), (FF // 16) ** -0.5, 1.0, ((1, 4),))
    return dict(tokens=tokens, cotangent=cotangent, segment_ids=segment_ids, routes=routes, attn_gain=attn_gain, query_weight=query_weight, key_matrix=key_matrix, value_weight=value_weight, out_weight=out_weight, ffn_gain=ffn_gain, router_weight=router_weight, gate_weight=gate_weight, up_weight=up_weight, down_weight=down_weight)


@jax.custom_vjp
def lower_precision(v):
    return lax.optimization_barrier(v.astype(jnp.bfloat16)).astype(jnp.float32)

@jax.custom_vjp
def lower_precision_backward(v):
    return v

def low_keep(v):
    return (lower_precision(v), None)

def low_pass(kept, grad):
    return (grad,)

def back_keep(v):
    return (v, None)

def back_low(kept, grad):
    return (lower_precision(grad),)
lower_precision.defvjp(low_keep, low_pass)
lower_precision_backward.defvjp(back_keep, back_low)
highest_precision = lax.Precision.HIGHEST
eps_norm = 1e-06
score_scale = 0.125
rope_base = 10000.0
masked_score = -1e+30

def rms_gain(values, gain_vec):
    inverse_rms = lax.rsqrt(lax.optimization_barrier(jnp.mean(values * values, axis=-1, keepdims=True)) + eps_norm)
    return values * inverse_rms * gain_vec

def apply_rotary(values, token_positions, head_count):
    row_count = values.shape[0]
    shaped = values.reshape(row_count, head_count, -1)
    half_size = shaped.shape[2] // 2
    frequency = rope_base ** (-jnp.arange(half_size, dtype=jnp.float32) / half_size)
    angles = token_positions.astype(jnp.float32)[:, None] * frequency[None, :]
    cosine = jnp.cos(angles)[:, None, :]
    sine_table = jnp.sin(angles)[:, None, :]
    first_half = shaped[:, :, :half_size]
    second_half = shaped[:, :, half_size:]
    turned = jnp.concatenate([first_half * cosine - second_half * sine_table, second_half * cosine + first_half * sine_table], axis=-1)
    return turned.reshape(row_count, -1)

def attend_sequence(query_rows, projected_keys, projected_values, segments):
    sequence_length = query_rows.shape[0]
    block_length = min(sequence_length, 512)
    key_head_count = projected_keys.reshape(sequence_length, KEY_VALUE_HEADS, HEAD_SIZE)
    value_head_count = projected_values.reshape(sequence_length, KEY_VALUE_HEADS, HEAD_SIZE)
    key_pos = jnp.arange(sequence_length, dtype=jnp.int32)

    def one_block(block_args):
        query_block_rows, seg_block, pos_block = block_args
        query_head_count = query_block_rows.reshape(block_length, KEY_VALUE_HEADS, QUERY_HEADS // KEY_VALUE_HEADS, HEAD_SIZE)
        scores = jnp.einsum('bkgd,skd->kgbs', query_head_count, key_head_count, precision=highest_precision) * score_scale
        scores = lower_precision_backward(scores)
        allowed = (seg_block[:, None] == segments[None, :]) & (key_pos[None, :] <= pos_block[:, None])
        scores = jnp.where(allowed, scores, masked_score)
        top_score = lax.optimization_barrier(jnp.max(scores, axis=-1, keepdims=True))
        log_total = top_score + jnp.log(lax.optimization_barrier(jnp.sum(jnp.exp(scores - top_score), axis=-1, keepdims=True)))
        weights = lower_precision(jnp.where(allowed, jnp.exp(scores - log_total), 0.0))
        mixed_rows = jnp.einsum('kgbs,skd->bkgd', weights, value_head_count, precision=highest_precision)
        return mixed_rows.reshape(block_length, -1)
    blocks = sequence_length // block_length
    mixed_rows = lax.map(jax.checkpoint(one_block), (query_rows.reshape(blocks, block_length, -1), segments.reshape(blocks, block_length), key_pos.reshape(blocks, block_length)))
    return mixed_rows.reshape(sequence_length, -1)

def expert_block(block_args, gate_weight, up_weight, down_weight):
    normed_rows, picked_experts, gate_values = block_args
    tok_count = normed_rows.shape[0]
    expert_count = gate_weight.shape[0]
    flat_picks = picked_experts.reshape(-1).astype(jnp.int32)
    flat_onehot = (flat_picks[:, None] == jnp.arange(expert_count, dtype=jnp.int32)[None, :]).astype(jnp.int32)
    earlier = jnp.cumsum(flat_onehot, axis=0).astype(jnp.int32) - flat_onehot
    slot_ids = lax.optimization_barrier(jnp.sum(earlier * flat_onehot, axis=1)).astype(jnp.int32)
    places = (flat_picks * CAP + slot_ids).astype(jnp.int32)
    repeated = jnp.repeat(normed_rows, TOP, axis=0)
    buffer = jnp.zeros((expert_count * CAP, normed_rows.shape[1]), jnp.float32).at[places].set(repeated)
    buffer = buffer.reshape(expert_count, CAP, -1)
    gate_act = lower_precision_backward(jnp.einsum('ecd,edf->ecf', buffer, gate_weight, precision=highest_precision))
    up_act = lower_precision_backward(jnp.einsum('ecd,edf->ecf', buffer, up_weight, precision=highest_precision))
    inner_act = lower_precision(jax.nn.silu(gate_act) * up_act)
    result = lower_precision(lower_precision_backward(jnp.einsum('ecf,efd->ecd', inner_act, down_weight, precision=highest_precision)))
    picked = result.reshape(expert_count * CAP, -1)[places].reshape(tok_count, TOP, -1)
    return lax.optimization_barrier(jnp.sum(gate_values[:, :, None] * picked, axis=1))

def layer(tokens, attn_gain, query_weight, key_matrix, value_weight, out_weight, ffn_gain, router_weight, gate_weight, up_weight, down_weight, segment_ids, routes):
    token_positions = jnp.tile(jnp.arange(SEQ, dtype=jnp.int32), TOKENS // SEQ)
    normalized_input = lower_precision(rms_gain(tokens, attn_gain))
    query_rows = lower_precision(apply_rotary(lower_precision_backward(jnp.dot(normalized_input, query_weight, precision=highest_precision)), token_positions, QUERY_HEADS))
    projected_keys = lower_precision(apply_rotary(lower_precision_backward(jnp.dot(normalized_input, key_matrix, precision=highest_precision)), token_positions, KEY_VALUE_HEADS))
    projected_values = lower_precision(lower_precision_backward(jnp.dot(normalized_input, value_weight, precision=highest_precision)))

    def one_sequence(state_carry, seq_args):
        return (state_carry, attend_sequence(seq_args[0], seq_args[1], seq_args[2], seq_args[3]))
    seq_count = TOKENS // SEQ
    ignored, attended = lax.scan(one_sequence, jnp.zeros((), jnp.float32), (query_rows.reshape(seq_count, SEQ, -1), projected_keys.reshape(seq_count, SEQ, -1), projected_values.reshape(seq_count, SEQ, -1), segment_ids.reshape(seq_count, SEQ)))
    attended = lower_precision(lower_precision_backward(attended.reshape(TOKENS, -1)))
    hidden = tokens + lower_precision_backward(jnp.dot(attended, out_weight, precision=highest_precision))
    normed2 = lower_precision(rms_gain(hidden, ffn_gain))
    logits = jnp.dot(normed2, router_weight, precision=highest_precision)
    gate_values = jax.nn.softmax(jnp.take_along_axis(logits, routes, axis=1), axis=-1)
    block_count = TOKENS // TOK_DEV
    run_block = jax.checkpoint(partial(expert_block, gate_weight=gate_weight, up_weight=up_weight, down_weight=down_weight))
    expert_mix = lax.map(run_block, (normed2.reshape(block_count, TOK_DEV, -1), routes.reshape(block_count, TOK_DEV, TOP), gate_values.reshape(block_count, TOK_DEV, TOP)))
    return hidden + expert_mix.reshape(TOKENS, -1)

def reference(tokens, cotangent, segment_ids, routes, attn_gain, query_weight, key_matrix, value_weight, out_weight, ffn_gain, router_weight, gate_weight, up_weight, down_weight):

    def forward(*params):
        return layer(*params, segment_ids, routes)
    output, pullback = jax.vjp(forward, tokens.astype(jnp.float32), attn_gain.astype(jnp.float32), query_weight.astype(jnp.float32), key_matrix.astype(jnp.float32), value_weight.astype(jnp.float32), out_weight.astype(jnp.float32), ffn_gain.astype(jnp.float32), router_weight.astype(jnp.float32), gate_weight.astype(jnp.float32), up_weight.astype(jnp.float32), down_weight.astype(jnp.float32))
    grads = pullback(cotangent.astype(jnp.float32))
    return (output.astype(jnp.bfloat16), grads[0], grads[1], grads[2], grads[3], grads[4], grads[5], grads[6], grads[7], grads[8], grads[9], grads[10])
```

```python
import functools
import math

import jax
import jax.numpy as jnp
from jax import lax
from jax.experimental import pallas as pl
from jax.experimental.pallas import tpu as pltpu
from jax.sharding import Mesh
from jax.sharding import PartitionSpec as P

QUERY_HEADS = 16
KEY_VALUE_HEADS = 8
HEAD = 64
LANES = 128

EPS = 1e-06
ROPE_BASE = 10000.0
MASKED = -1e30
F32 = jnp.float32
BF16 = jnp.bfloat16
NT = (((1,), (1,)), ((), ()))
TN = (((0,), (0,)), ((), ()))
VMEM_LIMIT = 60 * 1024 * 1024


def dot(a, b):
    return jnp.dot(a, b, preferred_element_type=F32)


def dot_nt(a, b):
    return lax.dot_general(a, b, NT, preferred_element_type=F32)


def dot_tn(a, b):
    return lax.dot_general(a, b, TN, preferred_element_type=F32)


def split_hi_lo(value):
    high = value.astype(BF16)
    return high, (value - high.astype(F32)).astype(BF16)


def inverse_rms(value):
    return lax.rsqrt(jnp.mean(value * value, axis=-1, keepdims=True) + EPS)


def swap_halves(value):
    width = value.shape[1]
    lane = lax.broadcasted_iota(jnp.int32, value.shape, 1)
    up = pltpu.roll(value, width - HEAD // 2, 1)
    down = pltpu.roll(value, HEAD // 2, 1)
    return jnp.where(lane % HEAD < HEAD // 2, up, down)


def rotate(value, cosine, sine):
    copies = value.shape[1] // LANES
    cosine = jnp.concatenate([cosine] * copies, axis=1)
    sine = jnp.concatenate([sine] * copies, axis=1)
    return value * cosine + swap_halves(value) * sine


def allowed_pairs(seg_col, seg_row, row0, count):
    rows = seg_col.shape[0]
    row = row0 + lax.broadcasted_iota(jnp.int32, (rows, count), 0)
    col = lax.broadcasted_iota(jnp.int32, (rows, count), 1)
    return (seg_col == seg_row) & (col <= row)


def front_kernel(
    block, heads, kv_heads, x_ref, gain_ref, w_ref, cos_ref, sin_ref, segc_ref, segr_ref,
    normed_ref, q_ref, k_ref, v_ref, att_ref, lse_ref, out_s,
):
    seq = x_ref.shape[0]
    blocks = seq // block
    group = heads // kv_heads
    qw, kw = heads * HEAD, kv_heads * HEAD

    def project(i, carry):
        rows = pl.ds(pl.multiple_of(i * block, block), block)
        x = x_ref[rows, :].astype(F32)
        normed = (x * inverse_rms(x) * gain_ref[...]).astype(BF16)
        normed_ref[rows, :] = normed
        qkv = dot(normed, w_ref[...])
        turned = rotate(qkv[:, : qw + kw], cos_ref[rows, :], sin_ref[rows, :])
        for h in range(heads):
            q_ref[h, rows, :] = turned[:, h * HEAD : (h + 1) * HEAD].astype(BF16)
        for h in range(kv_heads):
            k_ref[h, rows, :] = turned[:, qw + h * HEAD : qw + (h + 1) * HEAD].astype(BF16)
            v_ref[h, rows, :] = qkv[:, qw + kw + h * HEAD : qw + kw + (h + 1) * HEAD].astype(BF16)
        return carry

    lax.fori_loop(0, blocks, project, 0)

    def one_head(h, carry):
        kv = h // group
        for i in range(blocks):
            count = (i + 1) * block
            rows = slice(i * block, (i + 1) * block)
            q = q_ref[h, rows, :] * jnp.asarray(0.125, BF16)
            k = k_ref[kv, :count, :]
            v = v_ref[kv, :count, :]
            allowed = allowed_pairs(segc_ref[rows, :], segr_ref[:, :count], i * block, count)
            s = jnp.where(allowed, dot_nt(q, k), MASKED)
            top = jnp.max(s, axis=-1, keepdims=True)
            e = jnp.exp(s - top)
            total = jnp.sum(e, axis=-1, keepdims=True)
            lse_ref[h, rows, :] = top + jnp.log(total)
            p = (e * (1.0 / total)).astype(BF16)
            out_s[h, rows, :] = dot(p, v)
        return carry

    lax.fori_loop(0, heads, one_head, 0)
    for h in range(heads):
        att_ref[:, h * HEAD : (h + 1) * HEAD] = out_s[h].astype(BF16)


def back_kernel(
    block, heads, kv_heads, q_ref, k_ref, v_ref, do_ref, lse_ref, segc_ref, segr_ref, x_ref,
    normed_ref, w_ref, cos_ref, sin_ref, ng_ref, dw_ref, gain_ref, do_s, dq_s, dk_s, dv_s, raw_s, g_s,
):
    seq = x_ref.shape[0]
    blocks = seq // block
    group = heads // kv_heads
    qw, kw = heads * HEAD, kv_heads * HEAD
    for h in range(heads):
        do_s[h] = do_ref[:, h * HEAD : (h + 1) * HEAD]
    dk_s[...] = jnp.zeros_like(dk_s)
    dv_s[...] = jnp.zeros_like(dv_s)

    def one_head(h, carry):
        kv = h // group
        for i in range(blocks):
            count = (i + 1) * block
            rows = slice(i * block, (i + 1) * block)
            q = q_ref[h, rows, :] * jnp.asarray(0.125, BF16)
            k = k_ref[kv, :count, :]
            v = v_ref[kv, :count, :]
            do = do_s[h, rows, :]
            allowed = allowed_pairs(segc_ref[rows, :], segr_ref[:, :count], i * block, count)
            s = jnp.where(allowed, dot_nt(q, k), MASKED)
            prob = jnp.exp(s - lse_ref[h, rows, :])
            grad = dot_nt(do, v)
            inner = jnp.sum(prob * grad, axis=-1, keepdims=True)
            ds = (prob * (grad - inner)).astype(BF16)
            dq_s[h, rows, :] = dot(ds, k) * 0.125
            dk_s[kv, :count, :] += dot_tn(ds, q)
            dv_s[kv, :count, :] += dot_tn(prob.astype(BF16), do)
        return carry

    lax.fori_loop(0, heads, one_head, 0)
    for h in range(heads):
        raw_s[:, h * HEAD : (h + 1) * HEAD] = dq_s[h]
    for h in range(kv_heads):
        raw_s[:, qw + h * HEAD : qw + (h + 1) * HEAD] = dk_s[h]
        raw_s[:, qw + kw + h * HEAD : qw + kw + (h + 1) * HEAD] = dv_s[h]
    gain_ref[...] = jnp.zeros_like(gain_ref)

    def finish(i, carry):
        rows = pl.ds(pl.multiple_of(i * block, block), block)
        g_s[rows, : qw + kw] = rotate(raw_s[rows, : qw + kw], cos_ref[rows, :], -sin_ref[rows, :]).astype(BF16)
        g_s[rows, qw + kw :] = raw_s[rows, qw + kw :].astype(BF16)
        ng = dot_nt(g_s[rows, :], w_ref[...])
        x = x_ref[rows, :].astype(F32)
        gain_ref[...] += jnp.sum(ng * (x * inverse_rms(x)), axis=0, keepdims=True)
        ng_ref[rows, :] = ng.astype(BF16)
        return carry

    lax.fori_loop(0, blocks, finish, 0)
    width = normed_ref.shape[1]
    for c in range(0, width, 256):
        dw_ref[c : c + 256, :] = dot_tn(normed_ref[:, c : c + 256], g_s[...]).astype(BF16)


def softmax_gates(logits, mask):
    shown = jnp.where(mask > 0.0, logits, MASKED)
    e = jnp.where(mask > 0.0, jnp.exp(shown - jnp.max(shown, axis=-1, keepdims=True)), 0.0)
    return e * (1.0 / jnp.sum(e, axis=-1, keepdims=True))


def mid_kernel(x_ref, att_ref, ow_ref, gain_ref, router_ref, mask_ref, hidden_ref, normed_ref, gates_ref):
    parts, width = ow_ref.shape[0], ow_ref.shape[2]
    depth = att_ref.shape[2]
    for j in range(parts):
        cols = slice(j * width, (j + 1) * width)
        total = x_ref[:, cols].astype(F32)
        for i in range(att_ref.shape[0]):
            total = total + dot(att_ref[i], ow_ref[j, i * depth : (i + 1) * depth, :])
        hidden_ref[:, cols] = total
    hidden = hidden_ref[...]
    normed = (hidden * inverse_rms(hidden) * gain_ref[...]).astype(BF16)
    normed_ref[...] = normed
    gates_ref[...] = softmax_gates(dot(normed, router_ref[...]), mask_ref[...])


def mid_back_kernel(
    hidden_ref, nb_ref, dy_ref, gates_ref, mix_ref, normed_ref, router_ref, gain_ref, ow_ref, att_ref,
    hg_ref, ag_ref, owg_ref, fg_ref, rg_ref, aog_s,
):
    gates = gates_ref[...]
    mix = mix_ref[...]
    lg = gates * (mix - jnp.sum(gates * mix, axis=-1, keepdims=True))
    high, low = split_hi_lo(lg)
    normed = normed_ref[...]
    rg_ref[...] = dot_tn(high, normed) + dot_tn(low, normed)
    router = router_ref[...]
    ng = nb_ref[...].astype(F32) + dot_nt(high, router) + dot_nt(low, router)
    hidden = hidden_ref[...]
    inv = inverse_rms(hidden)
    scaled = hidden * inv
    fg_ref[...] = jnp.sum(ng * scaled, axis=0, keepdims=True)
    w = ng * gain_ref[...]
    hg = dy_ref[...].astype(F32) + inv * (w - scaled * jnp.mean(w * scaled, axis=-1, keepdims=True))
    hg_ref[...] = hg
    aog_s[...] = hg.astype(BF16)
    parts, width = ow_ref.shape[0], ow_ref.shape[2]
    groups, _, depth = att_ref.shape
    for i in range(groups):
        rows = slice(i * depth, (i + 1) * depth)
        total = dot_nt(aog_s[:, 0:width], ow_ref[0, rows, :])
        for j in range(1, parts):
            total = total + dot_nt(aog_s[:, j * width : (j + 1) * width], ow_ref[j, rows, :])
        ag_ref[i] = total.astype(BF16)
        for j in range(parts):
            owg_ref[j, rows, :] = dot_tn(att_ref[i], aog_s[:, j * width : (j + 1) * width]).astype(BF16)


def expert_kernel(
    experts, parts, place_ref, n2_ref, dy_ref, mask_ref, router_ref, *refs
):
    weights = refs[: 3 * parts]
    moe_ref, nb_ref, mix_ref, inner_ref, gg_ref, ug_ref = refs[3 * parts : 3 * parts + 6]
    wg_s, wu_s, wd_s, sems = refs[3 * parts + 6 :]
    z = place_ref[0]
    first = place_ref[1]

    @pl.when(pl.program_id(0) == 0)
    def load():
        copies = []
        for m, target in enumerate((wg_s, wu_s, wd_s)):
            for k in range(parts):
                source = weights[m * parts + k]
                size = source.shape[1]
                chunk = lax.rem(z - k + parts, parts)
                at = pl.ds(pl.multiple_of(chunk * size, size), size)
                copies.append(pltpu.make_async_copy(source, target.at[:, at, :], sems.at[m * parts + k]))
        for copy in copies:
            copy.start()
        for copy in copies:
            copy.wait()

    x = n2_ref[...]
    dy = dy_ref[...].astype(F32)
    gates = softmax_gates(dot(x, router_ref[...]), mask_ref[...])
    lane = lax.broadcasted_iota(jnp.int32, gates.shape, 1)
    moe = nb = mix_out = None
    for e in range(experts):
        g = jnp.sum(jnp.where(lane == first + e, gates, 0.0), axis=-1, keepdims=True)
        ga = dot(x, wg_s[e])
        ua = dot(x, wu_s[e])
        sg = jax.nn.sigmoid(ga)
        act = ga * sg
        inner = (act * ua).astype(BF16)
        inner_ref[e] = inner
        eo = dot(inner, wd_s[e]).astype(BF16).astype(F32)
        mix = jnp.sum(dy * eo, axis=-1, keepdims=True)
        part = g * eo
        moe = part if moe is None else moe + part
        row = jnp.where(lane == e, mix, 0.0) + jnp.where(lane == experts + e, g, 0.0)
        mix_out = row if mix_out is None else mix_out + row
        ig = dot_nt((g * dy).astype(BF16), wd_s[e])
        gg = (ig * ua * sg * (1.0 + ga * (1.0 - sg))).astype(BF16)
        ug = (ig * act).astype(BF16)
        gg_ref[e] = gg
        ug_ref[e] = ug
        back = dot_nt(gg, wg_s[e]) + dot_nt(ug, wu_s[e])
        nb = back if nb is None else nb + back
    moe_ref[...] = moe.astype(BF16)
    nb_ref[...] = nb.astype(BF16)
    mix_ref[...] = mix_out


def expert_grad_kernel(
    experts, parts, place_ref, n2_ref, dy_ref, mix_ref, inner_ref, gg_ref, ug_ref,
    dg_ref, du_ref, dd_ref, g_s, u_s, d_s,
):
    e, step = pl.program_id(0), pl.program_id(1)

    @pl.when(step == 0)
    def clear():
        g_s[...] = jnp.zeros_like(g_s)
        u_s[...] = jnp.zeros_like(u_s)
        d_s[...] = jnp.zeros_like(d_s)

    x = n2_ref[...]
    mix = mix_ref[...]
    lane = lax.broadcasted_iota(jnp.int32, mix.shape, 1)
    g = jnp.sum(jnp.where(lane == experts + e, mix, 0.0), axis=-1, keepdims=True)
    og = (g * dy_ref[...].astype(F32)).astype(BF16)
    g_s[...] += dot_tn(x, gg_ref[0])
    u_s[...] += dot_tn(x, ug_ref[0])
    d_s[...] += dot_tn(inner_ref[0], og)

    @pl.when(step == pl.num_programs(1) - 1)
    def store():
        z = place_ref[0]
        for total, out in ((g_s, dg_ref), (u_s, du_ref), (d_s, dd_ref)):
            size = out.shape[2]
            for k in range(parts):
                chunk = lax.rem(z - k + parts, parts)
                out[k, 0] = total[pl.ds(pl.multiple_of(chunk * size, size), size), :].astype(BF16)


def sds(shape, dtype):
    return jax.ShapeDtypeStruct(shape, dtype)


def params():
    return pltpu.CompilerParams(vmem_limit_bytes=VMEM_LIMIT)


def per_device(
    hi, ep, n, tokens, cotangent, segment_ids, routes, attn_gain, query_weight, key_matrix, value_weight,
    out_weight, ffn_gain, router_weight, gate_weight, up_weight, down_weight,
):
    rows, width = tokens.shape
    seq = rows * n
    experts = gate_weight.shape[0]
    own = experts // ep
    heads, kv_heads = QUERY_HEADS // n, KEY_VALUE_HEADS // n
    qw, kw = heads * HEAD, kv_heads * HEAD
    cols = qw + 2 * kw
    slab = width // n
    ff = gate_weight.shape[2]
    z = lax.axis_index("shard").astype(jnp.int32)
    r = lax.axis_index("ep").astype(jnp.int32)
    place = jnp.stack([z, r * own])
    ring = [(i, (i + 1) % n) for i in range(n)]
    everyone = ("hi", "ep", "shard")

    x_all = lax.all_gather(tokens, "shard", axis=0, tiled=True)
    by_dest = jnp.concatenate(
        [
            query_weight.reshape(slab, n, qw),
            key_matrix.reshape(slab, n, kw),
            value_weight.reshape(slab, n, kw),
        ],
        axis=2,
    ).transpose(1, 0, 2)
    w_qkv = lax.all_to_all(by_dest, "shard", 0, 0).reshape(width, cols)

    pack = jnp.concatenate(
        [
            attn_gain[None],
            ffn_gain[None],
            segment_ids.astype(BF16)[None],
            router_weight.T,
        ],
        axis=0,
    )
    packs = lax.all_gather(pack, "shard", axis=0, tiled=False)
    gain1 = packs[:, 0, :].reshape(1, width).astype(F32)
    gain2 = packs[:, 1, :].reshape(1, width).astype(F32)
    segments = packs[:, 2, :].reshape(seq).astype(F32)
    seg_col, seg_row = segments[:, None], segments[None, :]
    router = jnp.pad(packs[:, 3:, :].transpose(0, 2, 1).reshape(width, experts), ((0, 0), (0, LANES - experts)))
    ids = jnp.arange(experts, dtype=jnp.int32)
    routed = jnp.any(routes[:, :, None] == ids[None, None, :], axis=1)
    mask_own = jnp.pad(routed.astype(F32), ((0, 0), (0, LANES - experts)))
    mask_all = lax.all_gather(routed.T.astype(BF16), "ep", axis=0, tiled=False)
    mask_all = mask_all.transpose(0, 2, 1).reshape(ep * rows, experts).astype(F32)
    mask_all = jnp.pad(mask_all, ((0, 0), (0, LANES - experts)))

    positions = jnp.arange(seq, dtype=jnp.int32).astype(F32)
    frequency = ROPE_BASE ** (-jnp.arange(HEAD // 2, dtype=F32) / (HEAD // 2))
    angles = positions[:, None] * frequency[None, :]
    cosine, sine = jnp.cos(angles), jnp.sin(angles)
    cosine = jnp.concatenate([cosine] * 4, axis=1)
    sine = jnp.concatenate([-sine, sine] * 2, axis=1)

    normed, q, k, v, att, lse = pl.pallas_call(
        functools.partial(front_kernel, rows, heads, kv_heads),
        out_shape=(
            sds((seq, width), BF16),
            sds((heads, seq, HEAD), BF16),
            sds((kv_heads, seq, HEAD), BF16),
            sds((kv_heads, seq, HEAD), BF16),
            sds((seq, qw), BF16),
            sds((heads, seq, 1), F32),
        ),
        scratch_shapes=[pltpu.VMEM((heads, seq, HEAD), F32)],
        compiler_params=params(),
        name="front",
    )(x_all, gain1, w_qkv, cosine, sine, seg_col, seg_row)

    ow = lax.all_gather(out_weight, "shard", axis=0, tiled=False)
    dy_all = lax.all_gather(cotangent, "ep", axis=0, tiled=True)
    att = lax.all_to_all(att.reshape(n, rows, qw), "shard", 0, 0)

    mine = [lax.dynamic_slice_in_dim(w, r * own, own, axis=0) for w in (gate_weight, up_weight, down_weight)]
    mine, x_all = lax.optimization_barrier((mine, x_all))
    slabs = []
    for w in mine:
        slabs.append(w)
        for _ in range(n - 1):
            w = lax.ppermute(w, "shard", ring)
            slabs.append(w)

    hidden, normed2, gates_own = pl.pallas_call(
        mid_kernel,
        out_shape=(sds((rows, width), F32), sds((rows, width), BF16), sds((rows, LANES), F32)),
        compiler_params=params(),
        name="mid",
    )(tokens, att, ow, gain2, router, mask_own)

    n2_all = lax.all_gather(normed2, "ep", axis=0, tiled=True)
    total = ep * rows
    block = 512
    moe, nb, mix, inner, gg, ug = pl.pallas_call(
        functools.partial(expert_kernel, own, n),
        grid=(total // block,),
        in_specs=[
            pl.BlockSpec(memory_space=pltpu.SMEM),
            pl.BlockSpec((block, width), lambda i: (i, 0)),
            pl.BlockSpec((block, width), lambda i: (i, 0)),
            pl.BlockSpec((block, LANES), lambda i: (i, 0)),
            pl.BlockSpec((width, LANES), lambda i: (0, 0)),
        ]
        + [pl.BlockSpec(memory_space=pl.ANY)] * (3 * n),
        out_specs=(
            pl.BlockSpec((block, width), lambda i: (i, 0)),
            pl.BlockSpec((block, width), lambda i: (i, 0)),
            pl.BlockSpec((block, LANES), lambda i: (i, 0)),
            pl.BlockSpec((own, block, ff), lambda i: (0, i, 0)),
            pl.BlockSpec((own, block, ff), lambda i: (0, i, 0)),
            pl.BlockSpec((own, block, ff), lambda i: (0, i, 0)),
        ),
        out_shape=(
            sds((total, width), BF16),
            sds((total, width), BF16),
            sds((total, LANES), F32),
            sds((own, total, ff), BF16),
            sds((own, total, ff), BF16),
            sds((own, total, ff), BF16),
        ),
        scratch_shapes=[
            pltpu.VMEM((own, width, ff), BF16),
            pltpu.VMEM((own, width, ff), BF16),
            pltpu.VMEM((own, ff, width), BF16),
            pltpu.SemaphoreType.DMA((3 * n,)),
        ],
        compiler_params=params(),
        name="experts",
    )(place, n2_all, dy_all, mask_all, router, *slabs)

    nb_own = lax.psum_scatter(nb, "ep", scatter_dimension=0, tiled=True)
    mix_sent = mix[:, :own].reshape(ep, rows, own).transpose(0, 2, 1)
    mix_own = lax.all_to_all(mix_sent, "ep", 0, 0).reshape(experts, rows).T
    mix_own = jnp.pad(mix_own, ((0, 0), (0, LANES - experts)))

    ff_slab = ff // n
    dg, du, dd = pl.pallas_call(
        functools.partial(expert_grad_kernel, own, n),
        grid=(own, total // block),
        in_specs=[
            pl.BlockSpec(memory_space=pltpu.SMEM),
            pl.BlockSpec((block, width), lambda e, i: (i, 0)),
            pl.BlockSpec((block, width), lambda e, i: (i, 0)),
            pl.BlockSpec((block, LANES), lambda e, i: (i, 0)),
            pl.BlockSpec((1, block, ff), lambda e, i: (e, i, 0)),
            pl.BlockSpec((1, block, ff), lambda e, i: (e, i, 0)),
            pl.BlockSpec((1, block, ff), lambda e, i: (e, i, 0)),
        ],
        out_specs=(
            pl.BlockSpec((n, 1, slab, ff), lambda e, i: (0, e, 0, 0)),
            pl.BlockSpec((n, 1, slab, ff), lambda e, i: (0, e, 0, 0)),
            pl.BlockSpec((n, 1, ff_slab, width), lambda e, i: (0, e, 0, 0)),
        ),
        out_shape=(
            sds((n, own, slab, ff), BF16),
            sds((n, own, slab, ff), BF16),
            sds((n, own, ff_slab, width), BF16),
        ),
        scratch_shapes=[
            pltpu.VMEM((width, ff), F32),
            pltpu.VMEM((width, ff), F32),
            pltpu.VMEM((ff, width), F32),
        ],
        compiler_params=params(),
        name="expert_grads",
    )(place, n2_all, dy_all, mix, inner, gg, ug)

    hidden_grad, att_grad, ow_grad, ffn_grad, router_grad = pl.pallas_call(
        mid_back_kernel,
        out_shape=(
            sds((rows, width), F32),
            sds((n, rows, qw), BF16),
            sds((n, n * qw, slab), BF16),
            sds((1, width), F32),
            sds((LANES, width), F32),
        ),
        scratch_shapes=[pltpu.VMEM((rows, width), BF16)],
        compiler_params=params(),
        name="mid_back",
    )(hidden, nb_own, cotangent, gates_own, mix_own, normed2, router, gain2, ow, att)

    att_grad = lax.all_to_all(att_grad, "shard", 0, 0).reshape(seq, qw)
    ng, qkv_grad, gain_grad = pl.pallas_call(
        functools.partial(back_kernel, rows, heads, kv_heads),
        out_shape=(sds((seq, width), BF16), sds((width, cols), BF16), sds((1, width), F32)),
        scratch_shapes=[
            pltpu.VMEM((heads, seq, HEAD), BF16),
            pltpu.VMEM((heads, seq, HEAD), F32),
            pltpu.VMEM((kv_heads, seq, HEAD), F32),
            pltpu.VMEM((kv_heads, seq, HEAD), F32),
            pltpu.VMEM((seq, cols), F32),
            pltpu.VMEM((seq, cols), BF16),
        ],
        compiler_params=params(),
        name="back",
    )(q, k, v, att_grad, lse, seg_col, seg_row, x_all, normed, w_qkv, cosine, sine)

    ng_own = lax.psum_scatter(ng, "shard", scatter_dimension=0, tiled=True).astype(F32)
    moe_own = lax.psum_scatter(moe, "ep", scatter_dimension=0, tiled=True)
    output = (hidden + moe_own.astype(F32)).astype(BF16)

    x = tokens.astype(F32)
    inv = inverse_rms(x)
    scaled = x * inv
    w1 = ng_own * gain1
    input_grad = hidden_grad + inv * (w1 - scaled * jnp.mean(w1 * scaled, axis=-1, keepdims=True))

    def expert_sum(parts):
        part = parts[1]
        for step in list(range(2, n)) + [0]:
            part = lax.ppermute(part, "shard", ring).astype(F32) + parts[step].astype(F32)
            if step:
                part = part.astype(BF16)
        if hi > 1:
            part = lax.psum(part, "hi")
        return lax.all_gather(part.astype(BF16), "ep", axis=0, tiled=True).astype(F32)

    gate_grad, up_grad, down_grad = expert_sum(dg), expert_sum(du), expert_sum(dd)

    qkv_part = lax.psum_scatter(qkv_grad.reshape(n, slab, cols), "ep", scatter_dimension=1, tiled=True)
    qkv_part = lax.all_to_all(qkv_part, "shard", 0, 0)
    ow_part = lax.psum_scatter(ow_grad, "ep", scatter_dimension=1, tiled=True)
    ow_part = jnp.sum(lax.all_to_all(ow_part, "shard", 0, 0).astype(F32), axis=0)
    if hi > 1:
        qkv_part = lax.psum(qkv_part.astype(F32), "hi").astype(BF16)
        ow_part = lax.psum(ow_part, "hi")
    qkv_full = lax.all_gather(qkv_part, "ep", axis=1, tiled=True).astype(F32)
    ow_full = lax.all_gather(ow_part.astype(BF16), "ep", axis=0, tiled=True).astype(F32)

    def columns(part):
        return part.transpose(1, 0, 2).reshape(slab, -1)

    small = lax.psum(jnp.concatenate([gain_grad, ffn_grad, router_grad[:experts]], axis=0), everyone)
    small = lax.dynamic_slice_in_dim(small, z * slab, slab, axis=1)
    return (
        output,
        input_grad,
        small[0],
        columns(qkv_full[:, :, :qw]),
        columns(qkv_full[:, :, qw : qw + kw]),
        columns(qkv_full[:, :, qw + kw :]),
        ow_full,
        small[1],
        small[2:].T,
        gate_grad,
        up_grad,
        down_grad,
    )


def solution(mesh):
    rep, n = mesh.shape["rep"], mesh.shape["shard"]
    ep = math.gcd(rep, 8)
    hi = rep // ep
    split = Mesh(mesh.devices.reshape(hi, ep, n), ("hi", "ep", "shard"))
    rows = ("hi", "ep", "shard")
    placed = (
        P(rows, None),
        P(rows, None),
        P(rows),
        P(rows, None),
        P("shard"),
        P("shard", None),
        P("shard", None),
        P("shard", None),
        P(None, "shard"),
        P("shard"),
        P("shard", None),
        P(None, "shard", None),
        P(None, "shard", None),
        P(None, "shard", None),
    )
    return jax.shard_map(
        functools.partial(per_device, hi, ep, n),
        mesh=split,
        in_specs=placed,
        out_specs=(
            P(rows, None),
            P(rows, None),
            P("shard"),
            P("shard", None),
            P("shard", None),
            P("shard", None),
            P(None, "shard"),
            P("shard"),
            P("shard", None),
            P(None, "shard", None),
            P(None, "shard", None),
            P(None, "shard", None),
        ),
        check_vma=False,
    )
```

```python
import functools
import math

import jax
import jax.numpy as jnp
from jax import lax
from jax.experimental import pallas as pl
from jax.experimental.pallas import tpu as pltpu
from jax.sharding import Mesh
from jax.sharding import PartitionSpec as P

QUERY_HEADS = 16
KEY_VALUE_HEADS = 8
HEAD = 64
LANES = 128
MIX_LOW = 64

EPS = 1e-06
ROPE_BASE = 10000.0
MASKED = -1e30
F32 = jnp.float32
BF16 = jnp.bfloat16
NT = (((1,), (1,)), ((), ()))
TN = (((0,), (0,)), ((), ()))
VMEM_LIMIT = 60 * 1024 * 1024


def dot(a, b):
    return jnp.dot(a, b, preferred_element_type=F32)


def dot_nt(a, b):
    return lax.dot_general(a, b, NT, preferred_element_type=F32)


def dot_tn(a, b):
    return lax.dot_general(a, b, TN, preferred_element_type=F32)


def split_hi_lo(value):
    high = value.astype(BF16)
    return high, (value - high.astype(F32)).astype(BF16)


def inverse_rms(value):
    return lax.rsqrt(jnp.mean(value * value, axis=-1, keepdims=True) + EPS)


def swap_halves(value):
    width = value.shape[1]
    lane = lax.broadcasted_iota(jnp.int32, value.shape, 1)
    up = pltpu.roll(value, width - HEAD // 2, 1)
    down = pltpu.roll(value, HEAD // 2, 1)
    return jnp.where(lane % HEAD < HEAD // 2, up, down)


def rotate(value, cosine, sine):
    copies = value.shape[1] // LANES
    cosine = jnp.concatenate([cosine] * copies, axis=1)
    sine = jnp.concatenate([sine] * copies, axis=1)
    return value * cosine + swap_halves(value) * sine


def allowed_pairs(seg_col, seg_row, row0, count):
    rows = seg_col.shape[0]
    row = row0 + lax.broadcasted_iota(jnp.int32, (rows, count), 0)
    col = lax.broadcasted_iota(jnp.int32, (rows, count), 1)
    return (seg_col == seg_row) & (col <= row)


def ring_chunk(z, k, parts):
    return lax.rem(z - k + parts, parts)


def chunk_of(index, size):
    return pl.ds(pl.multiple_of(index * size, size), size)


def front_kernel(
    block, heads, kv_heads, parts, place_ref, *refs
):
    chunks = refs[:parts]
    (gain_ref, wrel_ref, cos_ref, sin_ref, segc_ref, segr_ref,
     x_ref, w_ref, normed_ref, q_ref, k_ref, v_ref, att_ref, lse_ref, out_s, sems) = refs[parts:]
    seq = x_ref.shape[0]
    blocks = seq // block
    group = heads // kv_heads
    qw, kw = heads * HEAD, kv_heads * HEAD
    z = place_ref[0]
    slab = wrel_ref.shape[1]
    copies = []
    for i in range(parts):
        at = chunk_of(ring_chunk(z, i, parts), block)
        copies.append(pltpu.make_async_copy(chunks[i], x_ref.at[at, :], sems.at[i]))
    for copy in copies:
        copy.start()
    for i in range(parts):
        w_ref[chunk_of(ring_chunk(z, i, parts), slab), :] = wrel_ref[i]
    for copy in copies:
        copy.wait()

    def project(i, carry):
        rows = pl.ds(pl.multiple_of(i * block, block), block)
        x = x_ref[rows, :].astype(F32)
        normed = (x * inverse_rms(x) * gain_ref[...]).astype(BF16)
        normed_ref[rows, :] = normed
        qkv = dot(normed, w_ref[...])
        turned = rotate(qkv[:, : qw + kw], cos_ref[rows, :], sin_ref[rows, :])
        for h in range(heads):
            q_ref[h, rows, :] = turned[:, h * HEAD : (h + 1) * HEAD].astype(BF16)
        for h in range(kv_heads):
            k_ref[h, rows, :] = turned[:, qw + h * HEAD : qw + (h + 1) * HEAD].astype(BF16)
            v_ref[h, rows, :] = qkv[:, qw + kw + h * HEAD : qw + kw + (h + 1) * HEAD].astype(BF16)
        return carry

    lax.fori_loop(0, blocks, project, 0)

    def one_head(h, carry):
        kv = h // group
        for i in range(blocks):
            count = (i + 1) * block
            rows = slice(i * block, (i + 1) * block)
            q = q_ref[h, rows, :] * jnp.asarray(0.125, BF16)
            k = k_ref[kv, :count, :]
            v = v_ref[kv, :count, :]
            allowed = allowed_pairs(segc_ref[rows, :], segr_ref[:, :count], i * block, count)
            s = jnp.where(allowed, dot_nt(q, k), MASKED)
            top = jnp.max(s, axis=-1, keepdims=True)
            e = jnp.exp(s - top)
            total = jnp.sum(e, axis=-1, keepdims=True)
            lse_ref[h, rows, :] = top + jnp.log(total)
            p = (e * (1.0 / total)).astype(BF16)
            out_s[h, rows, :] = dot(p, v)
        return carry

    lax.fori_loop(0, heads, one_head, 0)
    for h in range(heads):
        att_ref[:, h * HEAD : (h + 1) * HEAD] = out_s[h].astype(BF16)


def back_kernel(
    block, heads, kv_heads, place_ref, q_ref, k_ref, v_ref, do_ref, lse_ref, segc_ref, segr_ref, x_ref,
    normed_ref, w_ref, cos_ref, sin_ref, ng_ref, dw_ref, gain_ref, do_s, dq_s, dk_s, dv_s, raw_s, g_s,
):
    seq = x_ref.shape[0]
    blocks = seq // block
    group = heads // kv_heads
    qw, kw = heads * HEAD, kv_heads * HEAD
    for h in range(heads):
        do_s[h] = do_ref[:, h * HEAD : (h + 1) * HEAD]
    dk_s[...] = jnp.zeros_like(dk_s)
    dv_s[...] = jnp.zeros_like(dv_s)

    def one_head(h, carry):
        kv = h // group
        for i in range(blocks):
            count = (i + 1) * block
            rows = slice(i * block, (i + 1) * block)
            q = q_ref[h, rows, :] * jnp.asarray(0.125, BF16)
            k = k_ref[kv, :count, :]
            v = v_ref[kv, :count, :]
            do = do_s[h, rows, :]
            allowed = allowed_pairs(segc_ref[rows, :], segr_ref[:, :count], i * block, count)
            s = jnp.where(allowed, dot_nt(q, k), MASKED)
            prob = jnp.exp(s - lse_ref[h, rows, :])
            grad = dot_nt(do, v)
            inner = jnp.sum(prob * grad, axis=-1, keepdims=True)
            ds = (prob * (grad - inner)).astype(BF16)
            dq_s[h, rows, :] = dot(ds, k) * 0.125
            dk_s[kv, :count, :] += dot_tn(ds, q)
            dv_s[kv, :count, :] += dot_tn(prob.astype(BF16), do)
        return carry

    lax.fori_loop(0, heads, one_head, 0)
    for h in range(heads):
        raw_s[:, h * HEAD : (h + 1) * HEAD] = dq_s[h]
    for h in range(kv_heads):
        raw_s[:, qw + h * HEAD : qw + (h + 1) * HEAD] = dk_s[h]
        raw_s[:, qw + kw + h * HEAD : qw + kw + (h + 1) * HEAD] = dv_s[h]
    gain_ref[...] = jnp.zeros_like(gain_ref)

    def finish(i, carry):
        rows = pl.ds(pl.multiple_of(i * block, block), block)
        g_s[rows, : qw + kw] = rotate(raw_s[rows, : qw + kw], cos_ref[rows, :], -sin_ref[rows, :]).astype(BF16)
        g_s[rows, qw + kw :] = raw_s[rows, qw + kw :].astype(BF16)
        ng = dot_nt(g_s[rows, :], w_ref[...])
        x = x_ref[rows, :].astype(F32)
        gain_ref[...] += jnp.sum(ng * (x * inverse_rms(x)), axis=0, keepdims=True)
        ng_ref[ring_chunk(place_ref[0], i, blocks)] = ng.astype(BF16)
        return carry

    lax.fori_loop(0, blocks, finish, 0)
    width = normed_ref.shape[1]
    for c in range(0, width, 256):
        dw_ref[c : c + 256, :] = dot_tn(normed_ref[:, c : c + 256], g_s[...]).astype(BF16)


def softmax_gates(logits, mask):
    shown = jnp.where(mask > 0.0, logits, MASKED)
    e = jnp.where(mask > 0.0, jnp.exp(shown - jnp.max(shown, axis=-1, keepdims=True)), 0.0)
    return e * (1.0 / jnp.sum(e, axis=-1, keepdims=True))


def mid_kernel(place_ref, x_ref, att_ref, ow_ref, gain_ref, router_ref, mask_ref, hidden_ref, normed_ref, gates_ref):
    parts, width = ow_ref.shape[0], ow_ref.shape[2]
    depth = att_ref.shape[2]
    for j in range(parts):
        cols = chunk_of(ring_chunk(place_ref[0], j, parts), width)
        total = x_ref[:, cols].astype(F32)
        for i in range(att_ref.shape[0]):
            total = total + dot(att_ref[i], ow_ref[j, i * depth : (i + 1) * depth, :])
        hidden_ref[:, cols] = total
    hidden = hidden_ref[...]
    normed = (hidden * inverse_rms(hidden) * gain_ref[...]).astype(BF16)
    normed_ref[...] = normed
    gates_ref[...] = softmax_gates(dot(normed, router_ref[...]), mask_ref[...])


def mid_back_kernel(
    place_ref, hidden_ref, nb_ref, dy_ref, gates_ref, normed_ref, router_ref, gain_ref, ow_ref, att_ref,
    hg_ref, ag_ref, owg_ref, fg_ref, rg_ref, aog_s,
):
    gates = gates_ref[...]
    width_all = hidden_ref.shape[1]
    mix = nb_ref[:, width_all:].astype(F32)
    mix = mix + pltpu.roll(mix, LANES - MIX_LOW, 1)
    lg = gates * (mix - jnp.sum(gates * mix, axis=-1, keepdims=True))
    high, low = split_hi_lo(lg)
    normed = normed_ref[...]
    rg_ref[...] = dot_tn(high, normed) + dot_tn(low, normed)
    router = router_ref[...]
    ng = nb_ref[:, :width_all].astype(F32) + dot_nt(high, router) + dot_nt(low, router)
    hidden = hidden_ref[...]
    inv = inverse_rms(hidden)
    scaled = hidden * inv
    fg_ref[...] = jnp.sum(ng * scaled, axis=0, keepdims=True)
    w = ng * gain_ref[...]
    hg = dy_ref[...].astype(F32) + inv * (w - scaled * jnp.mean(w * scaled, axis=-1, keepdims=True))
    hg_ref[...] = hg
    aog_s[...] = hg.astype(BF16)
    parts, width = ow_ref.shape[0], ow_ref.shape[2]
    groups, _, depth = att_ref.shape
    for i in range(groups):
        rows = slice(i * depth, (i + 1) * depth)
        total = None
        for j in range(parts):
            chunk = ring_chunk(place_ref[0], j, parts)
            part = dot_nt(aog_s[:, chunk_of(chunk, width)], ow_ref[j, rows, :])
            total = part if total is None else total + part
        ag_ref[i] = total.astype(BF16)
        for j in range(parts):
            owg_ref[j, rows, :] = dot_tn(att_ref[i], aog_s[:, j * width : (j + 1) * width]).astype(BF16)


def expert_kernel(
    experts, parts, place_ref, n2_ref, dy_ref, mask_ref, router_ref, *refs
):
    weights = refs[: 3 * parts]
    moe_ref, nb_ref, g_ref, inner_ref, gg_ref, ug_ref = refs[3 * parts : 3 * parts + 6]
    wg_s, wu_s, wd_s, sems = refs[3 * parts + 6 :]
    z = place_ref[0]
    first = place_ref[1]

    @pl.when(pl.program_id(0) == 0)
    def load():
        copies = []
        for m, target in enumerate((wg_s, wu_s, wd_s)):
            for k in range(parts):
                source = weights[m * parts + k]
                size = source.shape[1]
                at = chunk_of(ring_chunk(z, k, parts), size)
                copies.append(pltpu.make_async_copy(source, target.at[:, at, :], sems.at[m * parts + k]))
        for copy in copies:
            copy.start()
        for copy in copies:
            copy.wait()

    x = n2_ref[...]
    dy = dy_ref[...].astype(F32)
    gates = softmax_gates(dot(x, router_ref[...]), mask_ref[...])
    lane = lax.broadcasted_iota(jnp.int32, gates.shape, 1)
    moe = nb = mix_out = None
    for e in range(experts):
        g = jnp.sum(jnp.where(lane == first + e, gates, 0.0), axis=-1, keepdims=True)
        ga = dot(x, wg_s[e])
        ua = dot(x, wu_s[e])
        sg = jax.nn.sigmoid(ga)
        act = ga * sg
        inner = (act * ua).astype(BF16)
        inner_ref[e] = inner
        eo = dot(inner, wd_s[e]).astype(BF16).astype(F32)
        mix = jnp.sum(dy * eo, axis=-1, keepdims=True)
        part = g * eo
        moe = part if moe is None else moe + part
        high, low = split_hi_lo(mix)
        row = jnp.where(lane == first + e, high.astype(F32), 0.0)
        row = row + jnp.where(lane == MIX_LOW + first + e, low.astype(F32), 0.0)
        mix_out = row if mix_out is None else mix_out + row
        g_ref[...] = jnp.where(lane == e, g, g_ref[...] if e else 0.0)
        ig = dot_nt((g * dy).astype(BF16), wd_s[e])
        gg = (ig * ua * sg * (1.0 + ga * (1.0 - sg))).astype(BF16)
        ug = (ig * act).astype(BF16)
        gg_ref[e] = gg
        ug_ref[e] = ug
        back = dot_nt(gg, wg_s[e]) + dot_nt(ug, wu_s[e])
        nb = back if nb is None else nb + back
    moe_ref[...] = moe.astype(BF16)
    width = n2_ref.shape[1]
    nb_ref[:, :width] = nb.astype(BF16)
    nb_ref[:, width:] = mix_out.astype(BF16)


def expert_grad_kernel(experts, parts, half, place_ref, *refs):
    halves = (refs[:6], refs[6:12])
    dg_ref, du_ref, dd_ref, g_s, u_s, d_s = refs[12:]
    e, step = pl.program_id(0), pl.program_id(1)

    @pl.when(step == 0)
    def clear():
        g_s[...] = jnp.zeros_like(g_s)
        u_s[...] = jnp.zeros_like(u_s)
        d_s[...] = jnp.zeros_like(d_s)

    def add(n2_ref, dy_ref, g_ref, inner_ref, gg_ref, ug_ref):
        x = n2_ref[...]
        lane = lax.broadcasted_iota(jnp.int32, g_ref.shape, 1)
        g = jnp.sum(jnp.where(lane == e, g_ref[...], 0.0), axis=-1, keepdims=True)
        og = (g * dy_ref[...].astype(F32)).astype(BF16)
        g_s[...] += dot_tn(x, gg_ref[0])
        u_s[...] += dot_tn(x, ug_ref[0])
        d_s[...] += dot_tn(inner_ref[0], og)

    pl.when(step < half)(lambda: add(*halves[0]))
    pl.when(step >= half)(lambda: add(*halves[1]))

    @pl.when(step == pl.num_programs(1) - 1)
    def store():
        z = place_ref[0]
        for total, out in ((g_s, dg_ref), (u_s, du_ref), (d_s, dd_ref)):
            size = out.shape[2]
            for k in range(parts):
                out[k, 0] = total[chunk_of(ring_chunk(z, k, parts), size), :].astype(BF16)


def sds(shape, dtype):
    return jax.ShapeDtypeStruct(shape, dtype)


def params():
    return pltpu.CompilerParams(vmem_limit_bytes=VMEM_LIMIT)


def cost(flops, traffic):
    return pl.CostEstimate(flops=int(flops), bytes_accessed=int(traffic), transcendentals=0)


def per_device(
    hi, yx, n, tokens, cotangent, segment_ids, routes, attn_gain, query_weight, key_matrix, value_weight,
    out_weight, ffn_gain, router_weight, gate_weight, up_weight, down_weight,
):
    rows, width = tokens.shape
    seq = rows * n
    experts = gate_weight.shape[0]
    ep = yx * 2
    own = experts // ep
    heads, kv_heads = QUERY_HEADS // n, KEY_VALUE_HEADS // n
    qw, kw = heads * HEAD, kv_heads * HEAD
    cols = qw + 2 * kw
    slab = width // n
    ff = gate_weight.shape[2]
    z = lax.axis_index("shard").astype(jnp.int32)
    core = lax.axis_index("cr").astype(jnp.int32)
    r = lax.axis_index("yx").astype(jnp.int32) * 2 + core
    place = jnp.stack([z, r * own])
    plane = ("yx", "cr")
    smem = pl.BlockSpec(memory_space=pltpu.SMEM)
    vmem = pl.BlockSpec(memory_space=pltpu.VMEM)
    hbm = pl.BlockSpec(memory_space=pl.ANY)

    def shift(value, k=1):
        return lax.ppermute(value, "shard", [(i, (i + k) % n) for i in range(n)])

    def swap(value):
        return lax.ppermute(value, "cr", [(0, 1), (1, 0)])

    def pick(value, index, axis):
        return lax.dynamic_index_in_dim(value, index, axis, keepdims=False)

    def absolute(parts):
        stacked = jnp.stack(parts)
        return jnp.stack([pick(stacked, lax.rem(z - j + n, n), 0) for j in range(n)])

    pack = jnp.concatenate(
        [attn_gain[None], ffn_gain[None], segment_ids.astype(BF16)[None], router_weight.T], axis=0
    )
    packs = absolute([pack] + [shift(pack, k) for k in range(1, n)])
    gain1 = packs[:, 0, :].reshape(1, width).astype(F32)
    gain2 = packs[:, 1, :].reshape(1, width).astype(F32)
    segments = packs[:, 2, :].reshape(seq).astype(F32)
    seg_col, seg_row = segments[:, None], segments[None, :]
    router = jnp.pad(packs[:, 3:, :].transpose(0, 2, 1).reshape(width, experts), ((0, 0), (0, LANES - experts)))

    part_rows = slab // ep
    by_dest = jnp.concatenate(
        [
            lax.dynamic_slice_in_dim(w, r * part_rows, part_rows, axis=0).reshape(part_rows, n, -1)
            for w in (query_weight, key_matrix, value_weight)
        ],
        axis=2,
    )
    w_rel = jnp.stack(
        [pick(by_dest, z, 1)] + [shift(pick(by_dest, lax.rem(z + k, n), 1), k) for k in range(1, n)]
    )
    w_rel = lax.all_gather(w_rel, plane, axis=1, tiled=True)
    ow_rows = out_weight.shape[0] // ep
    ow_mine = lax.dynamic_slice_in_dim(out_weight, r * ow_rows, ow_rows, axis=0)
    ow = jnp.stack([ow_mine] + [shift(ow_mine, k) for k in range(1, n)])
    ow = lax.all_gather(ow, plane, axis=1, tiled=True)

    chunks = [tokens]
    for _ in range(n - 1):
        chunks.append(shift(chunks[-1]))

    ids = jnp.arange(experts, dtype=jnp.int32)
    routed = jnp.any(routes[:, :, None] == ids[None, None, :], axis=1)
    mask_own = jnp.pad(routed.astype(F32), ((0, 0), (0, LANES - experts)))
    mask_all = lax.all_gather(routed.T.astype(BF16), plane, axis=0, tiled=False).reshape(yx, 2, experts, rows)

    def mask_of(which):
        mask = pick(mask_all, which, 1).transpose(0, 2, 1).reshape(yx * rows, experts).astype(F32)
        return jnp.pad(mask, ((0, 0), (0, LANES - experts)))

    positions = jnp.arange(seq, dtype=jnp.int32).astype(F32)
    frequency = ROPE_BASE ** (-jnp.arange(HEAD // 2, dtype=F32) / (HEAD // 2))
    angles = positions[:, None] * frequency[None, :]
    cosine, sine = jnp.cos(angles), jnp.sin(angles)
    cosine = jnp.concatenate([cosine] * 4, axis=1)
    sine = jnp.concatenate([-sine, sine] * 2, axis=1)

    mine = [lax.dynamic_slice_in_dim(w, r * own, own, axis=0) for w in (gate_weight, up_weight, down_weight)]
    mine, chunks = lax.optimization_barrier((mine, chunks))
    slabs = []
    for w in mine:
        slabs.append(w)
        for _ in range(n - 1):
            w = shift(w)
            slabs.append(w)

    x_all, w_qkv, normed, q, k, v, att, lse = pl.pallas_call(
        functools.partial(front_kernel, rows, heads, kv_heads, n),
        in_specs=[smem] + [hbm] * n + [vmem] * 6,
        out_shape=(
            sds((seq, width), BF16),
            sds((width, cols), BF16),
            sds((seq, width), BF16),
            sds((heads, seq, HEAD), BF16),
            sds((kv_heads, seq, HEAD), BF16),
            sds((kv_heads, seq, HEAD), BF16),
            sds((seq, qw), BF16),
            sds((heads, seq, 1), F32),
        ),
        scratch_shapes=[pltpu.VMEM((heads, seq, HEAD), F32), pltpu.SemaphoreType.DMA((n,))],
        compiler_params=params(),
        cost_estimate=cost(2 * seq * width * cols, 60e6),
        name="front",
    )(place, *chunks, gain1, w_rel, cosine, sine, seg_col, seg_row)

    att = lax.all_to_all(att.reshape(n, rows, qw), "shard", 0, 0)
    hidden, normed2, gates_own = pl.pallas_call(
        mid_kernel,
        in_specs=[smem] + [vmem] * 6,
        out_shape=(sds((rows, width), F32), sds((rows, width), BF16), sds((rows, LANES), F32)),
        compiler_params=params(),
        cost_estimate=cost(2 * rows * width * width, 14e6),
        name="mid",
    )(place, tokens, att, ow, gain2, router, mask_own)

    dy_mine = lax.all_gather(cotangent, "yx", axis=0, tiled=True)
    dy_mate = swap(dy_mine)
    n2_mine = lax.all_gather(normed2, "yx", axis=0, tiled=True)
    n2_mate = swap(n2_mine)

    total = yx * rows
    block = min(512, total)
    steps = total // block

    def run_experts(n2, dy, mask):
        return pl.pallas_call(
            functools.partial(expert_kernel, own, n),
            grid=(steps,),
            in_specs=[
                smem,
                pl.BlockSpec((block, width), lambda i: (i, 0)),
                pl.BlockSpec((block, width), lambda i: (i, 0)),
                pl.BlockSpec((block, LANES), lambda i: (i, 0)),
                pl.BlockSpec((width, LANES), lambda i: (0, 0)),
            ]
            + [hbm] * (3 * n),
            out_specs=(
                pl.BlockSpec((block, width), lambda i: (i, 0)),
                pl.BlockSpec((block, width + LANES), lambda i: (i, 0)),
                pl.BlockSpec((block, LANES), lambda i: (i, 0)),
                pl.BlockSpec((own, block, ff), lambda i: (0, i, 0)),
                pl.BlockSpec((own, block, ff), lambda i: (0, i, 0)),
                pl.BlockSpec((own, block, ff), lambda i: (0, i, 0)),
            ),
            out_shape=(
                sds((total, width), BF16),
                sds((total, width + LANES), BF16),
                sds((total, LANES), F32),
                sds((own, total, ff), BF16),
                sds((own, total, ff), BF16),
                sds((own, total, ff), BF16),
            ),
            scratch_shapes=[
                pltpu.VMEM((own, width, ff), BF16),
                pltpu.VMEM((own, width, ff), BF16),
                pltpu.VMEM((own, ff, width), BF16),
                pltpu.SemaphoreType.DMA((3 * n,)),
            ],
            compiler_params=params(),
            cost_estimate=cost(12 * own * total * width * ff, 70e6),
            name="experts",
        )(place, n2, dy, mask, router, *slabs)

    moe_mate, nb_mate, *saved_mate = run_experts(n2_mate, dy_mate, mask_of(1 - core))
    nb_got = swap(nb_mate)
    moe_got = swap(moe_mate)
    moe, nb, *saved_mine = run_experts(n2_mine, dy_mine, mask_of(core))

    def plus(one, other):
        return (one.astype(F32) + other.astype(F32)).astype(BF16)

    nb_own = lax.psum_scatter(plus(nb, nb_got), "yx", scatter_dimension=0, tiled=True)
    moe_own = lax.psum_scatter(plus(moe, moe_got), "yx", scatter_dimension=0, tiled=True)

    ff_slab = ff // n

    def half_specs(at):
        return [
            pl.BlockSpec((block, width), lambda e, i: (at(i), 0)),
            pl.BlockSpec((block, width), lambda e, i: (at(i), 0)),
            pl.BlockSpec((block, LANES), lambda e, i: (at(i), 0)),
            pl.BlockSpec((1, block, ff), lambda e, i: (e, at(i), 0)),
            pl.BlockSpec((1, block, ff), lambda e, i: (e, at(i), 0)),
            pl.BlockSpec((1, block, ff), lambda e, i: (e, at(i), 0)),
        ]

    dg, du, dd = pl.pallas_call(
        functools.partial(expert_grad_kernel, own, n, steps),
        grid=(own, 2 * steps),
        in_specs=[smem]
        + half_specs(lambda i: jnp.minimum(i, steps - 1))
        + half_specs(lambda i: jnp.maximum(i - steps, 0)),
        out_specs=(
            pl.BlockSpec((n, 1, slab, ff), lambda e, i: (0, e, 0, 0)),
            pl.BlockSpec((n, 1, slab, ff), lambda e, i: (0, e, 0, 0)),
            pl.BlockSpec((n, 1, ff_slab, width), lambda e, i: (0, e, 0, 0)),
        ),
        out_shape=(
            sds((n, own, slab, ff), BF16),
            sds((n, own, slab, ff), BF16),
            sds((n, own, ff_slab, width), BF16),
        ),
        scratch_shapes=[
            pltpu.VMEM((width, ff), F32),
            pltpu.VMEM((width, ff), F32),
            pltpu.VMEM((ff, width), F32),
        ],
        compiler_params=params(),
        cost_estimate=cost(6 * own * 2 * total * width * ff, 80e6),
        name="expert_grads",
    )(place, n2_mate, dy_mate, *saved_mate, n2_mine, dy_mine, *saved_mine)

    def ring_sum(parts):
        part = parts[1]
        for step in list(range(2, n)) + [0]:
            part = shift(part).astype(F32) + parts[step].astype(F32)
            if step:
                part = part.astype(BF16)
        return part

    def expert_sum(parts):
        part = ring_sum(parts)
        if hi > 1:
            part = lax.psum(part, "hi")
        mine = lax.all_gather(part.astype(BF16), "yx", axis=0, tiled=False)
        mate = swap(mine)
        even, odd = jnp.where(core == 0, mine, mate), jnp.where(core == 0, mate, mine)
        return jnp.stack([even, odd], axis=1).reshape((experts,) + part.shape[1:]).astype(F32)

    gate_grad, up_grad, down_grad = expert_sum(dg), expert_sum(du), expert_sum(dd)

    hidden_grad, att_grad, ow_grad, ffn_grad, router_grad = pl.pallas_call(
        mid_back_kernel,
        in_specs=[smem] + [vmem] * 9,
        out_shape=(
            sds((rows, width), F32),
            sds((n, rows, qw), BF16),
            sds((n, n * qw, slab), BF16),
            sds((1, width), F32),
            sds((LANES, width), F32),
        ),
        scratch_shapes=[pltpu.VMEM((rows, width), BF16)],
        compiler_params=params(),
        cost_estimate=cost(4 * rows * width * width, 20e6),
        name="mid_back",
    )(place, hidden, nb_own, cotangent, gates_own, normed2, router, gain2, ow, att)

    att_grad = lax.all_to_all(att_grad, "shard", 0, 0).reshape(seq, qw)
    ng, qkv_grad, gain_grad = pl.pallas_call(
        functools.partial(back_kernel, rows, heads, kv_heads),
        in_specs=[smem] + [vmem] * 12,
        out_shape=(sds((n, rows, width), BF16), sds((width, cols), BF16), sds((1, width), F32)),
        scratch_shapes=[
            pltpu.VMEM((heads, seq, HEAD), BF16),
            pltpu.VMEM((heads, seq, HEAD), F32),
            pltpu.VMEM((kv_heads, seq, HEAD), F32),
            pltpu.VMEM((kv_heads, seq, HEAD), F32),
            pltpu.VMEM((seq, cols), F32),
            pltpu.VMEM((seq, cols), BF16),
        ],
        compiler_params=params(),
        cost_estimate=cost(4 * seq * width * cols, 80e6),
        name="back",
    )(place, q, k, v, att_grad, lse, seg_col, seg_row, x_all, normed, w_qkv, cosine, sine)

    ng_own = ring_sum(ng)
    output = (hidden + moe_own.astype(F32)).astype(BF16)

    x = tokens.astype(F32)
    inv = inverse_rms(x)
    scaled = x * inv
    w1 = ng_own * gain1
    input_grad = hidden_grad + inv * (w1 - scaled * jnp.mean(w1 * scaled, axis=-1, keepdims=True))

    kvw = 2 * kw
    small = jnp.concatenate([gain_grad, ffn_grad, router_grad[:experts]], axis=0)
    small_rows = 16
    small = jnp.pad(small, ((0, ep * small_rows - small.shape[0]), (0, 0)))
    small = small.reshape(ep, small_rows, n, slab).transpose(2, 0, 1, 3).astype(BF16)
    qkv_rows = qkv_grad.reshape(n, ep, part_rows, cols)
    wide = max(slab, qw, kvw)

    def widen(part):
        return jnp.pad(part, ((0, 0),) * 3 + ((0, wide - part.shape[3]),))

    pieces = [widen(ow_grad.reshape(n, ep, ow_rows, slab)), widen(small), widen(qkv_rows[..., :qw]), widen(qkv_rows[..., qw:])]
    dense = jnp.concatenate(pieces, axis=2)
    dense = dense.reshape(n, yx, 2, dense.shape[2], wide).transpose(2, 1, 0, 3, 4)
    dense = plus(pick(dense, core, 0), swap(pick(dense, 1 - core, 0)))
    piece = dense.shape[1:]
    dense = lax.psum_scatter(dense.reshape(-1, wide), "yx", scatter_dimension=0, tiled=True).reshape(piece)
    if hi > 1:
        dense = lax.psum(dense.astype(F32), "hi").astype(BF16)
    dense = lax.all_to_all(dense, "shard", 0, 0)
    cut = ow_rows + small_rows
    summed = jnp.sum(dense[:, :cut].astype(F32), axis=0).astype(BF16)
    kept = dense[:, cut:].reshape(n * 2 * part_rows, wide)
    full = lax.all_gather(jnp.concatenate([summed, kept], axis=0), plane, axis=0, tiled=False)
    ow_full = full[:, :ow_rows, :slab].reshape(-1, slab).astype(F32)
    small_full = full[:, ow_rows:cut, :slab].reshape(-1, slab).astype(F32)
    kept = full[:, cut:].reshape(ep, n, 2, part_rows, wide)

    def columns(which, start, size):
        part = kept[:, :, which, :, start : start + size]
        return part.transpose(0, 2, 1, 3).reshape(slab, n * size).astype(F32)

    return (
        output,
        input_grad,
        small_full[0],
        columns(0, 0, qw),
        columns(1, 0, kw),
        columns(1, kw, kw),
        ow_full,
        small_full[1],
        small_full[2 : 2 + experts].T,
        gate_grad,
        up_grad,
        down_grad,
    )


def solution(mesh):
    rep, n = mesh.shape["rep"], mesh.shape["shard"]
    yx = math.gcd(rep // 2, 4)
    hi = rep // (2 * yx)
    split = Mesh(mesh.devices.reshape(hi, yx, 2, n), ("hi", "yx", "cr", "shard"))
    rows = ("hi", "yx", "cr", "shard")
    placed = (
        P(rows, None),
        P(rows, None),
        P(rows),
        P(rows, None),
        P("shard"),
        P("shard", None),
        P("shard", None),
        P("shard", None),
        P(None, "shard"),
        P("shard"),
        P("shard", None),
        P(None, "shard", None),
        P(None, "shard", None),
        P(None, "shard", None),
    )
    return jax.shard_map(
        functools.partial(per_device, hi, yx, n),
        mesh=split,
        in_specs=placed,
        out_specs=(
            P(rows, None),
            P(rows, None),
            P("shard"),
            P("shard", None),
            P("shard", None),
            P("shard", None),
            P(None, "shard"),
            P("shard"),
            P("shard", None),
            P(None, "shard", None),
            P(None, "shard", None),
            P(None, "shard", None),
        ),
        check_vma=False,
    )
```

```python
import functools
import math

import jax
import jax.numpy as jnp
from jax import lax
from jax.experimental import pallas as pl
from jax.experimental.pallas import tpu as pltpu
from jax.sharding import Mesh
from jax.sharding import PartitionSpec as P

QUERY_HEADS = 16
KEY_VALUE_HEADS = 8
HEAD = 64
LANES = 128
MIX_LOW = 64

EPS = 1e-06
ROPE_BASE = 10000.0
MASKED = -1e30
F32 = jnp.float32
BF16 = jnp.bfloat16
NT = (((1,), (1,)), ((), ()))
TN = (((0,), (0,)), ((), ()))
VMEM_LIMIT = 60 * 1024 * 1024


def dot(a, b):
    return jnp.dot(a, b, preferred_element_type=F32)


def dot_nt(a, b):
    return lax.dot_general(a, b, NT, preferred_element_type=F32)


def dot_tn(a, b):
    return lax.dot_general(a, b, TN, preferred_element_type=F32)


def split_hi_lo(value):
    high = value.astype(BF16)
    return high, (value - high.astype(F32)).astype(BF16)


def inverse_rms(value):
    return lax.rsqrt(jnp.mean(value * value, axis=-1, keepdims=True) + EPS)


def swap_halves(value):
    width = value.shape[1]
    lane = lax.broadcasted_iota(jnp.int32, value.shape, 1)
    up = pltpu.roll(value, width - HEAD // 2, 1)
    down = pltpu.roll(value, HEAD // 2, 1)
    return jnp.where(lane % HEAD < HEAD // 2, up, down)


def rotate(value, cosine, sine):
    copies = value.shape[1] // LANES
    cosine = jnp.concatenate([cosine] * copies, axis=1)
    sine = jnp.concatenate([sine] * copies, axis=1)
    return value * cosine + swap_halves(value) * sine


def allowed_pairs(seg_col, seg_row, row0, count):
    rows = seg_col.shape[0]
    row = row0 + lax.broadcasted_iota(jnp.int32, (rows, count), 0)
    col = lax.broadcasted_iota(jnp.int32, (rows, count), 1)
    return (seg_col == seg_row) & (col <= row)


def ring_chunk(z, k, parts):
    return lax.rem(z - k + parts, parts)


def chunk_of(index, size):
    return pl.ds(pl.multiple_of(index * size, size), size)


def peer(place_ref, c, j):
    return lax.bitwise_xor(place_ref[2], jnp.int32(j)) * 2 + lax.bitwise_xor(place_ref[3], jnp.int32(c))


def front_kernel(
    block, heads, kv_heads, parts, place_ref, *refs
):
    chunks = refs[:parts]
    (gain_ref, mine_ref, mate_ref, cos_ref, sin_ref, segc_ref, segr_ref,
     x_ref, w_ref, normed_ref, q_ref, k_ref, v_ref, att_ref, lse_ref, out_s, sems) = refs[parts:]
    seq = x_ref.shape[0]
    blocks = seq // block
    group = heads // kv_heads
    qw, kw = heads * HEAD, kv_heads * HEAD
    z = place_ref[0]
    slab = w_ref.shape[0] // parts
    part = slab // (2 * mine_ref.shape[0])
    copies = []
    for i in range(parts):
        at = chunk_of(ring_chunk(z, i, parts), block)
        copies.append(pltpu.make_async_copy(chunks[i], x_ref.at[at, :], sems.at[i]))
    for copy in copies:
        copy.start()
    for c, piece_ref in enumerate((mine_ref, mate_ref)):
        for j in range(piece_ref.shape[0]):
            at = peer(place_ref, c, j) * part
            for i in range(parts):
                start = pl.multiple_of(ring_chunk(z, i, parts) * slab + at, part)
                w_ref[pl.ds(start, part), :] = piece_ref[j, i, :part, :]
    for copy in copies:
        copy.wait()

    def project(i, carry):
        rows = pl.ds(pl.multiple_of(i * block, block), block)
        x = x_ref[rows, :].astype(F32)
        normed = (x * inverse_rms(x) * gain_ref[...]).astype(BF16)
        normed_ref[rows, :] = normed
        qkv = dot(normed, w_ref[...])
        turned = rotate(qkv[:, : qw + kw], cos_ref[rows, :], sin_ref[rows, :])
        for h in range(heads):
            q_ref[h, rows, :] = turned[:, h * HEAD : (h + 1) * HEAD].astype(BF16)
        for h in range(kv_heads):
            k_ref[h, rows, :] = turned[:, qw + h * HEAD : qw + (h + 1) * HEAD].astype(BF16)
            v_ref[h, rows, :] = qkv[:, qw + kw + h * HEAD : qw + kw + (h + 1) * HEAD].astype(BF16)
        return carry

    lax.fori_loop(0, blocks, project, 0)

    def one_head(h, carry):
        kv = h // group
        for i in range(blocks):
            count = (i + 1) * block
            rows = slice(i * block, (i + 1) * block)
            q = q_ref[h, rows, :] * jnp.asarray(0.125, BF16)
            k = k_ref[kv, :count, :]
            v = v_ref[kv, :count, :]
            allowed = allowed_pairs(segc_ref[rows, :], segr_ref[:, :count], i * block, count)
            s = jnp.where(allowed, dot_nt(q, k), MASKED)
            top = jnp.max(s, axis=-1, keepdims=True)
            e = jnp.exp(s - top)
            total = jnp.sum(e, axis=-1, keepdims=True)
            lse_ref[h, rows, :] = top + jnp.log(total)
            p = (e * (1.0 / total)).astype(BF16)
            out_s[h, rows, :] = dot(p, v)
        return carry

    lax.fori_loop(0, heads, one_head, 0)
    for h in range(heads):
        att_ref[:, h * HEAD : (h + 1) * HEAD] = out_s[h].astype(BF16)


def back_kernel(
    block, heads, kv_heads, place_ref, q_ref, k_ref, v_ref, do_ref, lse_ref, segc_ref, segr_ref, x_ref,
    normed_ref, w_ref, cos_ref, sin_ref, ng_ref, dw_ref, gain_ref, do_s, dq_s, dk_s, dv_s, raw_s, g_s,
):
    seq = x_ref.shape[0]
    blocks = seq // block
    group = heads // kv_heads
    qw, kw = heads * HEAD, kv_heads * HEAD
    for h in range(heads):
        do_s[h] = do_ref[:, h * HEAD : (h + 1) * HEAD]
    dk_s[...] = jnp.zeros_like(dk_s)
    dv_s[...] = jnp.zeros_like(dv_s)

    def one_head(h, carry):
        kv = h // group
        for i in range(blocks):
            count = (i + 1) * block
            rows = slice(i * block, (i + 1) * block)
            q = q_ref[h, rows, :] * jnp.asarray(0.125, BF16)
            k = k_ref[kv, :count, :]
            v = v_ref[kv, :count, :]
            do = do_s[h, rows, :]
            allowed = allowed_pairs(segc_ref[rows, :], segr_ref[:, :count], i * block, count)
            s = jnp.where(allowed, dot_nt(q, k), MASKED)
            prob = jnp.exp(s - lse_ref[h, rows, :])
            grad = dot_nt(do, v)
            inner = jnp.sum(prob * grad, axis=-1, keepdims=True)
            ds = (prob * (grad - inner)).astype(BF16)
            dq_s[h, rows, :] = dot(ds, k) * 0.125
            dk_s[kv, :count, :] += dot_tn(ds, q)
            dv_s[kv, :count, :] += dot_tn(prob.astype(BF16), do)
        return carry

    lax.fori_loop(0, heads, one_head, 0)
    for h in range(heads):
        raw_s[:, h * HEAD : (h + 1) * HEAD] = dq_s[h]
    for h in range(kv_heads):
        raw_s[:, qw + h * HEAD : qw + (h + 1) * HEAD] = dk_s[h]
        raw_s[:, qw + kw + h * HEAD : qw + kw + (h + 1) * HEAD] = dv_s[h]
    gain_ref[...] = jnp.zeros_like(gain_ref)

    def finish(i, carry):
        rows = pl.ds(pl.multiple_of(i * block, block), block)
        g_s[rows, : qw + kw] = rotate(raw_s[rows, : qw + kw], cos_ref[rows, :], -sin_ref[rows, :]).astype(BF16)
        g_s[rows, qw + kw :] = raw_s[rows, qw + kw :].astype(BF16)
        ng = dot_nt(g_s[rows, :], w_ref[...])
        x = x_ref[rows, :].astype(F32)
        gain_ref[...] += jnp.sum(ng * (x * inverse_rms(x)), axis=0, keepdims=True)
        ng_ref[ring_chunk(place_ref[0], i, blocks)] = ng.astype(BF16)
        return carry

    lax.fori_loop(0, blocks, finish, 0)
    width = normed_ref.shape[1]
    for c in range(0, width, 256):
        dw_ref[c : c + 256, :] = dot_tn(normed_ref[:, c : c + 256], g_s[...]).astype(BF16)


def softmax_gates(logits, mask):
    shown = jnp.where(mask > 0.0, logits, MASKED)
    e = jnp.where(mask > 0.0, jnp.exp(shown - jnp.max(shown, axis=-1, keepdims=True)), 0.0)
    return e * (1.0 / jnp.sum(e, axis=-1, keepdims=True))


def mid_kernel(
    place_ref, x_ref, att_ref, mine_ref, mate_ref, gain_ref, router_ref, mask_ref,
    hidden_ref, normed_ref, gates_ref, ow_ref,
):
    parts, width = ow_ref.shape[0], ow_ref.shape[2]
    share = ow_ref.shape[1] // (2 * mine_ref.shape[0])
    fold = mine_ref.shape[3] // width
    lines = share // fold
    skip = mine_ref.shape[2] - lines
    for c, piece_ref in enumerate((mine_ref, mate_ref)):
        for j in range(piece_ref.shape[0]):
            at = peer(place_ref, c, j) * share
            for k in range(parts):
                for f in range(fold):
                    start = pl.multiple_of(at + f * lines, lines)
                    ow_ref[k, pl.ds(start, lines), :] = piece_ref[j, k, skip:, f * width : (f + 1) * width]
    depth = att_ref.shape[2]
    for j in range(parts):
        cols = chunk_of(ring_chunk(place_ref[0], j, parts), width)
        total = x_ref[:, cols].astype(F32)
        for i in range(att_ref.shape[0]):
            total = total + dot(att_ref[i], ow_ref[j, i * depth : (i + 1) * depth, :])
        hidden_ref[:, cols] = total
    hidden = hidden_ref[...]
    normed = (hidden * inverse_rms(hidden) * gain_ref[...]).astype(BF16)
    normed_ref[...] = normed
    gates_ref[...] = softmax_gates(dot(normed, router_ref[...]), mask_ref[...])


def mid_back_kernel(
    place_ref, hidden_ref, nb0_ref, nb1_ref, nb2_ref, nb3_ref, dy_ref, gates_ref, normed_ref, router_ref, gain_ref, ow_ref, att_ref,
    hg_ref, ag_ref, owg_ref, fg_ref, rg_ref, aog_s,
):
    gates = gates_ref[...]
    width_all = hidden_ref.shape[1]
    nb = sum(ref[...].astype(F32) for ref in (nb1_ref, nb2_ref, nb3_ref)) + nb0_ref[...].astype(F32)
    mix = nb[:, width_all:]
    mix = mix + pltpu.roll(mix, LANES - MIX_LOW, 1)
    lg = gates * (mix - jnp.sum(gates * mix, axis=-1, keepdims=True))
    high, low = split_hi_lo(lg)
    normed = normed_ref[...]
    rg_ref[...] = dot_tn(high, normed) + dot_tn(low, normed)
    router = router_ref[...]
    ng = nb[:, :width_all] + dot_nt(high, router) + dot_nt(low, router)
    hidden = hidden_ref[...]
    inv = inverse_rms(hidden)
    scaled = hidden * inv
    fg_ref[...] = jnp.sum(ng * scaled, axis=0, keepdims=True)
    w = ng * gain_ref[...]
    hg = dy_ref[...].astype(F32) + inv * (w - scaled * jnp.mean(w * scaled, axis=-1, keepdims=True))
    hg_ref[...] = hg
    aog_s[...] = hg.astype(BF16)
    parts, width = ow_ref.shape[0], ow_ref.shape[2]
    groups, _, depth = att_ref.shape
    for i in range(groups):
        rows = slice(i * depth, (i + 1) * depth)
        total = None
        for j in range(parts):
            chunk = ring_chunk(place_ref[0], j, parts)
            part = dot_nt(aog_s[:, chunk_of(chunk, width)], ow_ref[j, rows, :])
            total = part if total is None else total + part
        ag_ref[i] = total.astype(BF16)
        for j in range(parts):
            owg_ref[j, rows, :] = dot_tn(att_ref[i], aog_s[:, j * width : (j + 1) * width]).astype(BF16)


def expert_kernel(parts, e, place_ref, n2_ref, dyx_ref, router_ref, w_ref, *refs):
    previous = refs[:2] if e else ()
    moe_ref, nb_ref, g_ref, inner_ref, gg_ref, ug_ref, wg_s, wu_s, wd_s, sems = refs[len(previous) :]
    width, ff = wg_s.shape
    slab, ff_slab = width // parts, ff // parts

    @pl.when(pl.program_id(0) == 0)
    def load():
        copies = []

        def move(start, count, target):
            copies.append(pltpu.make_async_copy(w_ref.at[start : start + count, :], target, sems.at[len(copies)]))

        for k in range(parts):
            start = k * 3 * slab
            move(start, slab, wg_s.at[k * slab : (k + 1) * slab, :])
            move(start + slab, slab, wu_s.at[k * slab : (k + 1) * slab, :])
            for c in range(width // ff):
                at = start + 2 * slab + c * ff_slab
                move(at, ff_slab, wd_s.at[k * ff_slab : (k + 1) * ff_slab, c * ff : (c + 1) * ff])
        for copy in copies:
            copy.start()
        for copy in copies:
            copy.wait()

    x = n2_ref[...]
    dy = dyx_ref[:, :width].astype(F32)
    gates = softmax_gates(dot(x, router_ref[...]), dyx_ref[:, width:].astype(F32))
    lane = lax.broadcasted_iota(jnp.int32, gates.shape, 1)
    at = place_ref[1] + e
    g = jnp.sum(jnp.where(lane == at, gates, 0.0), axis=-1, keepdims=True)
    ga = dot(x, wg_s[...])
    ua = dot(x, wu_s[...])
    sg = jax.nn.sigmoid(ga)
    act = ga * sg
    inner = (act * ua).astype(BF16)
    inner_ref[...] = inner
    eo = dot(inner, wd_s[...]).astype(BF16).astype(F32)
    moe = g * eo
    high, low = split_hi_lo(jnp.sum(dy * eo, axis=-1, keepdims=True))
    mix = jnp.where(lane == at, high.astype(F32), 0.0) + jnp.where(lane == MIX_LOW + at, low.astype(F32), 0.0)
    g_ref[...] = jnp.where(lane == 0, g, 0.0)
    ig = dot_nt((g * dy).astype(BF16), wd_s[...])
    gg = (ig * ua * sg * (1.0 + ga * (1.0 - sg))).astype(BF16)
    ug = (ig * act).astype(BF16)
    gg_ref[...] = gg
    ug_ref[...] = ug
    nb = dot_nt(gg, wg_s[...]) + dot_nt(ug, wu_s[...])
    if e:
        moe = moe + previous[0][...].astype(F32)
        nb = nb + previous[1][:, :width].astype(F32)
        mix = mix + previous[1][:, width:].astype(F32)
    moe_ref[...] = moe.astype(BF16)
    nb_ref[:, :width] = nb.astype(BF16)
    nb_ref[:, width:] = mix.astype(BF16)


def expert_grad_kernel(parts, half, *refs):
    halves = (refs[:6], refs[6:12])
    out_ref, g_s, u_s, d_s = refs[12:]
    step = pl.program_id(0)
    width, ff = g_s.shape
    slab, ff_slab = width // parts, ff // parts

    @pl.when(step == 0)
    def clear():
        g_s[...] = jnp.zeros_like(g_s)
        u_s[...] = jnp.zeros_like(u_s)
        d_s[...] = jnp.zeros_like(d_s)

    def add(n2_ref, dyx_ref, g_ref, inner_ref, gg_ref, ug_ref):
        x = n2_ref[...]
        g = jnp.sum(g_ref[...], axis=-1, keepdims=True)
        og = (g * dyx_ref[:, :width].astype(F32)).astype(BF16)
        g_s[...] += dot_tn(x, gg_ref[...])
        u_s[...] += dot_tn(x, ug_ref[...])
        d_s[...] += dot_tn(inner_ref[...], og)

    pl.when(step < half)(lambda: add(*halves[0]))
    pl.when(step >= half)(lambda: add(*halves[1]))

    @pl.when(step == pl.num_programs(0) - 1)
    def store():
        for k in range(parts):
            start = k * 3 * slab
            out_ref[start : start + slab, :] = g_s[k * slab : (k + 1) * slab, :].astype(BF16)
            out_ref[start + slab : start + 2 * slab, :] = u_s[k * slab : (k + 1) * slab, :].astype(BF16)
            for c in range(width // ff):
                at = start + 2 * slab + c * ff_slab
                out_ref[at : at + ff_slab, :] = d_s[k * ff_slab : (k + 1) * ff_slab, c * ff : (c + 1) * ff].astype(BF16)


def share_kernel(count, place_ref, *refs):
    gate_ref, up_ref, down_ref = refs[-3:]
    _, _, slab, ff = gate_ref.shape
    ff_slab, width = down_ref.shape[2:]
    for i in range(count):

        @pl.when(pl.program_id(0) == i)
        def copy(piece_ref=refs[i]):
            gate_ref[0, 0] = piece_ref[:slab, :].astype(F32)
            up_ref[0, 0] = piece_ref[slab : 2 * slab, :].astype(F32)
            for c in range(width // ff):
                at = 2 * slab + c * ff_slab
                down_ref[0, 0, :, c * ff : (c + 1) * ff] = piece_ref[at : at + ff_slab, :].astype(F32)


def sds(shape, dtype):
    return jax.ShapeDtypeStruct(shape, dtype)


def params():
    return pltpu.CompilerParams(vmem_limit_bytes=VMEM_LIMIT)


def cost(flops, traffic):
    return pl.CostEstimate(flops=int(flops), bytes_accessed=int(traffic), transcendentals=0)


def per_device(
    hi, yx, n, tokens, cotangent, segment_ids, routes, attn_gain, query_weight, key_matrix, value_weight,
    out_weight, ffn_gain, router_weight, gate_weight, up_weight, down_weight,
):
    rows, width = tokens.shape
    seq = rows * n
    experts = gate_weight.shape[0]
    ep = yx * 2
    own = experts // ep
    heads, kv_heads = QUERY_HEADS // n, KEY_VALUE_HEADS // n
    qw, kw = heads * HEAD, kv_heads * HEAD
    cols = qw + 2 * kw
    slab = width // n
    ff = gate_weight.shape[2]
    z = lax.axis_index("shard").astype(jnp.int32)
    core = lax.axis_index("cr").astype(jnp.int32)
    chip = lax.axis_index("yx").astype(jnp.int32)
    r = chip * 2 + core
    place = jnp.stack([z, r * own, chip, core])
    smem = pl.BlockSpec(memory_space=pltpu.SMEM)
    vmem = pl.BlockSpec(memory_space=pltpu.VMEM)
    hbm = pl.BlockSpec(memory_space=pl.ANY)

    def shift(value, k=1):
        return lax.ppermute(value, "shard", [(i, (i + k) % n) for i in range(n)])

    def swap(value):
        return lax.ppermute(value, "cr", [(0, 1), (1, 0)])

    def flip(value, j):
        return lax.ppermute(value, "yx", [(i, i ^ j) for i in range(yx)])

    def pick(value, index, axis):
        return lax.dynamic_index_in_dim(value, index, axis, keepdims=False)

    def absolute(parts):
        stacked = jnp.stack(parts)
        return jnp.stack([pick(stacked, lax.rem(z - j + n, n), 0) for j in range(n)])

    def around(value):
        return [value] + [flip(value, j) for j in range(1, yx)]

    def plus(one, other):
        return (one.astype(F32) + other.astype(F32)).astype(BF16)

    chunks = [tokens]
    for _ in range(n - 1):
        chunks.append(shift(chunks[-1]))

    pack = jnp.concatenate(
        [attn_gain[None], ffn_gain[None], segment_ids.astype(BF16)[None], router_weight.T], axis=0
    )
    packs = absolute([pack] + [shift(pack, k) for k in range(1, n)])
    gain1 = packs[:, 0, :].reshape(1, width).astype(F32)
    gain2 = packs[:, 1, :].reshape(1, width).astype(F32)
    segments = packs[:, 2, :].reshape(seq).astype(F32)
    seg_col, seg_row = segments[:, None], segments[None, :]
    router = jnp.pad(packs[:, 3:, :].transpose(0, 2, 1).reshape(width, experts), ((0, 0), (0, LANES - experts)))

    part_rows = slab // ep
    by_dest = jnp.concatenate(
        [
            lax.dynamic_slice_in_dim(w, r * part_rows, part_rows, axis=0).reshape(part_rows, n, -1)
            for w in (query_weight, key_matrix, value_weight)
        ],
        axis=2,
    )
    ow_rows = out_weight.shape[0] // ep
    fold = cols // slab
    ow_mine = lax.dynamic_slice_in_dim(out_weight, r * ow_rows, ow_rows, axis=0)
    ow_mine = ow_mine.reshape(fold, ow_rows // fold, slab).transpose(1, 0, 2).reshape(ow_rows // fold, cols)

    def piece(k):
        return jnp.concatenate([pick(by_dest, lax.rem(z + k, n), 1), ow_mine], axis=0)

    dense_mine = jnp.stack([piece(0)] + [shift(piece(k), k) for k in range(1, n)])
    dense_mine = jnp.stack(around(dense_mine))
    dense_mate = swap(dense_mine)

    ids = jnp.arange(experts, dtype=jnp.int32)
    routed = jnp.any(routes[:, :, None] == ids[None, None, :], axis=1)
    mask_own = jnp.pad(routed.astype(F32), ((0, 0), (0, LANES - experts)))
    dyx_mine = jnp.concatenate(around(jnp.concatenate([cotangent, mask_own.astype(BF16)], axis=1)), axis=0)
    dyx_mate = swap(dyx_mine)

    positions = jnp.arange(seq, dtype=jnp.int32).astype(F32)
    frequency = ROPE_BASE ** (-jnp.arange(HEAD // 2, dtype=F32) / (HEAD // 2))
    angles = positions[:, None] * frequency[None, :]
    cosine, sine = jnp.cos(angles), jnp.sin(angles)
    cosine = jnp.concatenate([cosine] * 4, axis=1)
    sine = jnp.concatenate([-sine, sine] * 2, axis=1)

    folds = width // ff
    packed = []
    for e in range(own):
        gate, up, down = (pick(w, r * own + e, 0) for w in (gate_weight, up_weight, down_weight))
        down = [down[:, c * ff : (c + 1) * ff] for c in range(folds)]
        packed.append(jnp.concatenate([gate, up] + down, axis=0))
    packed, chunks = lax.optimization_barrier((packed, chunks))
    weights = [lax.all_gather(w, "shard", axis=0, tiled=True) for w in packed]

    x_all, w_qkv, normed, q, k, v, att, lse = pl.pallas_call(
        functools.partial(front_kernel, rows, heads, kv_heads, n),
        in_specs=[smem] + [hbm] * n + [vmem] * 7,
        out_shape=(
            sds((seq, width), BF16),
            sds((width, cols), BF16),
            sds((seq, width), BF16),
            sds((heads, seq, HEAD), BF16),
            sds((kv_heads, seq, HEAD), BF16),
            sds((kv_heads, seq, HEAD), BF16),
            sds((seq, qw), BF16),
            sds((heads, seq, 1), F32),
        ),
        scratch_shapes=[pltpu.VMEM((heads, seq, HEAD), F32), pltpu.SemaphoreType.DMA((n,))],
        compiler_params=params(),
        cost_estimate=cost(2 * seq * width * cols, 60e6),
        name="front",
    )(place, *chunks, gain1, dense_mine, dense_mate, cosine, sine, seg_col, seg_row)

    att = lax.all_to_all(att.reshape(n, rows, qw), "shard", 0, 0)
    hidden, normed2, gates_own, ow = pl.pallas_call(
        mid_kernel,
        in_specs=[smem] + [vmem] * 7,
        out_shape=(
            sds((rows, width), F32),
            sds((rows, width), BF16),
            sds((rows, LANES), F32),
            sds((n, ep * ow_rows, slab), BF16),
        ),
        compiler_params=params(),
        cost_estimate=cost(2 * rows * width * width, 14e6),
        name="mid",
    )(place, tokens, att, dense_mine, dense_mate, gain2, router, mask_own)

    n2_mine = jnp.concatenate(around(normed2), axis=0)
    n2_mate = swap(n2_mine)

    total = yx * rows
    block = min(512, total)
    steps = total // block

    def by_block(size):
        return pl.BlockSpec((block, size), lambda i: (i, 0))

    def run_expert(e, n2, dyx, previous):
        return pl.pallas_call(
            functools.partial(expert_kernel, n, e),
            grid=(steps,),
            in_specs=[
                smem,
                by_block(width),
                by_block(width + LANES),
                pl.BlockSpec((width, LANES), lambda i: (0, 0)),
                hbm,
            ]
            + ([by_block(width), by_block(width + LANES)] if e else []),
            out_specs=(
                by_block(width),
                by_block(width + LANES),
                by_block(LANES),
                by_block(ff),
                by_block(ff),
                by_block(ff),
            ),
            out_shape=(
                sds((total, width), BF16),
                sds((total, width + LANES), BF16),
                sds((total, LANES), F32),
                sds((total, ff), BF16),
                sds((total, ff), BF16),
                sds((total, ff), BF16),
            ),
            scratch_shapes=[
                pltpu.VMEM((width, ff), BF16),
                pltpu.VMEM((width, ff), BF16),
                pltpu.VMEM((ff, width), BF16),
                pltpu.SemaphoreType.DMA(((2 + folds) * n,)),
            ],
            compiler_params=params(),
            cost_estimate=cost(12 * total * width * ff, 36e6),
            name="expert",
        )(place, n2, dyx, router, weights[e], *previous)

    def half_specs(at):
        sizes = (width, width + LANES, LANES, ff, ff, ff)
        return [pl.BlockSpec((block, size), lambda i: (at(i), 0)) for size in sizes]

    def weight_grads(mate, mine):
        return pl.pallas_call(
            functools.partial(expert_grad_kernel, n, steps),
            grid=(2 * steps,),
            in_specs=half_specs(lambda i: jnp.minimum(i, steps - 1))
            + half_specs(lambda i: jnp.maximum(i - steps, 0)),
            out_specs=pl.BlockSpec((3 * width, ff), lambda i: (0, 0)),
            out_shape=sds((3 * width, ff), BF16),
            scratch_shapes=[
                pltpu.VMEM((width, ff), F32),
                pltpu.VMEM((width, ff), F32),
                pltpu.VMEM((ff, width), F32),
            ],
            compiler_params=params(),
            cost_estimate=cost(12 * total * width * ff, 40e6),
            name="expert_grads",
        )(n2_mate, dyx_mate, *mate, n2_mine, dyx_mine, *mine)

    def spread(value):
        return [value[j * rows : (j + 1) * rows] for j in range(yx)]

    def exchanged(blocks):
        return [blocks[0]] + [flip(blocks[j], j) for j in range(1, yx)]

    previous_mate = previous_mine = ()
    owned = []
    for e in range(own):
        *previous_mate, g_mate, in_mate, gg_mate, ug_mate = run_expert(e, n2_mate, dyx_mate, previous_mate)
        if e == own - 1:
            moe_got, nb_got = swap(previous_mate[0]), swap(previous_mate[1])
        *previous_mine, g_mine, in_mine, gg_mine, ug_mine = run_expert(e, n2_mine, dyx_mine, previous_mine)
        grads = weight_grads((g_mate, in_mate, gg_mate, ug_mate), (g_mine, in_mine, gg_mine, ug_mine))
        if e < own - 1:
            grads, weights[e + 1] = lax.optimization_barrier((grads, weights[e + 1]))
        else:
            nb_parts = exchanged(spread(plus(previous_mine[1], nb_got)))
            moe_sum = plus(previous_mine[0], moe_got)
            nb_parts, moe_sum, grads = lax.optimization_barrier((nb_parts, moe_sum, grads))
        grads = lax.psum_scatter(grads, "shard", scatter_dimension=0, tiled=True)
        if hi > 1:
            grads = lax.psum(grads.astype(F32), "hi").astype(BF16)
        owned.append(grads)

    hidden_grad, att_grad, ow_grad, ffn_grad, router_grad = pl.pallas_call(
        mid_back_kernel,
        in_specs=[smem] + [vmem] * 12,
        out_shape=(
            sds((rows, width), F32),
            sds((n, rows, qw), BF16),
            sds((n, n * qw, slab), BF16),
            sds((1, width), F32),
            sds((LANES, width), F32),
        ),
        scratch_shapes=[pltpu.VMEM((rows, width), BF16)],
        compiler_params=params(),
        cost_estimate=cost(4 * rows * width * width, 20e6),
        name="mid_back",
    )(place, hidden, *nb_parts, cotangent, gates_own, normed2, router, gain2, ow, att)

    att_grad = lax.all_to_all(att_grad, "shard", 0, 0).reshape(seq, qw)
    ng, qkv_grad, gain_grad = pl.pallas_call(
        functools.partial(back_kernel, rows, heads, kv_heads),
        in_specs=[smem] + [vmem] * 12,
        out_shape=(sds((n, rows, width), BF16), sds((width, cols), BF16), sds((1, width), F32)),
        scratch_shapes=[
            pltpu.VMEM((heads, seq, HEAD), BF16),
            pltpu.VMEM((heads, seq, HEAD), F32),
            pltpu.VMEM((kv_heads, seq, HEAD), F32),
            pltpu.VMEM((kv_heads, seq, HEAD), F32),
            pltpu.VMEM((seq, cols), F32),
            pltpu.VMEM((seq, cols), BF16),
        ],
        compiler_params=params(),
        cost_estimate=cost(4 * seq * width * cols, 80e6),
        name="back",
    )(place, q, k, v, att_grad, lse, seg_col, seg_row, x_all, normed, w_qkv, cosine, sine)

    part = ng[1]
    for step in list(range(2, n)) + [0]:
        part = shift(part).astype(F32) + ng[step].astype(F32)
        if step:
            part = part.astype(BF16)
    x = tokens.astype(F32)
    inv = inverse_rms(x)
    scaled = x * inv
    w1 = part * gain1
    input_grad = hidden_grad + inv * (w1 - scaled * jnp.mean(w1 * scaled, axis=-1, keepdims=True))

    moe_parts = exchanged(spread(moe_sum))
    output = (hidden + sum(p.astype(F32) for p in moe_parts)).astype(BF16)

    shared = ()
    for e in range(own):
        mine = around(owned[e])
        pieces = [p for one in mine for p in (one, swap(one))]

        def out_index(j, place_ref, e=e):
            return (peer(place_ref, j % 2, j // 2), e, 0, 0)

        shared = pl.pallas_call(
            functools.partial(share_kernel, ep),
            grid_spec=pltpu.PrefetchScalarGridSpec(
                num_scalar_prefetch=1,
                grid=(ep,),
                in_specs=[pl.BlockSpec((3 * slab, ff), lambda j, place_ref: (0, 0))] * ep + [hbm] * len(shared),
                out_specs=(
                    pl.BlockSpec((1, 1, slab, ff), out_index),
                    pl.BlockSpec((1, 1, slab, ff), out_index),
                    pl.BlockSpec((1, 1, ff // n, width), out_index),
                ),
            ),
            out_shape=(
                sds((ep, own, slab, ff), F32),
                sds((ep, own, slab, ff), F32),
                sds((ep, own, ff // n, width), F32),
            ),
            input_output_aliases={1 + ep + i: i for i in range(len(shared))},
            compiler_params=params(),
            cost_estimate=cost(0, 20e6),
            name="share",
        )(place, *pieces, *shared)
    gate_grad, up_grad, down_grad = (g.reshape((experts,) + g.shape[2:]) for g in shared)

    kvw = 2 * kw
    small = jnp.concatenate([gain_grad, ffn_grad, router_grad[:experts]], axis=0)
    small_rows = 16
    small = jnp.pad(small, ((0, ep * small_rows - small.shape[0]), (0, 0)))
    small = small.reshape(ep, small_rows, n, slab).transpose(2, 0, 1, 3).astype(BF16)
    qkv_rows = qkv_grad.reshape(n, ep, part_rows, cols)
    wide = max(slab, qw, kvw)

    def widen(part):
        return jnp.pad(part, ((0, 0),) * 3 + ((0, wide - part.shape[3]),))

    pieces = [widen(ow_grad.reshape(n, ep, ow_rows, slab)), widen(small), widen(qkv_rows[..., :qw]), widen(qkv_rows[..., qw:])]
    dense = jnp.concatenate(pieces, axis=2)
    dense = dense.reshape(n, yx, 2, dense.shape[2], wide).transpose(2, 1, 0, 3, 4)
    dense = plus(pick(dense, core, 0), swap(pick(dense, 1 - core, 0)))
    dense = exchanged([pick(dense, lax.bitwise_xor(chip, jnp.int32(j)), 0) for j in range(yx)])
    dense = sum(p.astype(F32) for p in dense)
    if hi > 1:
        dense = lax.psum(dense, "hi")
    dense = dense.astype(BF16)
    dense = [pick(dense, z, 0)] + [shift(pick(dense, lax.rem(z + k, n), 0), k) for k in range(1, n)]
    cut = ow_rows + small_rows
    summed = sum(p[:cut].astype(F32) for p in dense).astype(BF16)
    kept = absolute([p[cut:] for p in dense]).reshape(n * 2 * part_rows, wide)
    mine = jnp.stack(around(jnp.concatenate([summed, kept], axis=0)))
    both = jnp.stack([mine, swap(mine)], axis=1).reshape((ep,) + mine.shape[1:])
    full = jnp.stack([pick(both, lax.bitwise_xor(r, jnp.int32(i)), 0) for i in range(ep)])
    ow_full = full[:, :ow_rows, :slab].reshape(-1, slab).astype(F32)
    small_full = full[:, ow_rows:cut, :slab].reshape(-1, slab).astype(F32)
    kept = full[:, cut:].reshape(ep, n, 2, part_rows, wide)

    def columns(which, start, size):
        part = kept[:, :, which, :, start : start + size]
        return part.transpose(0, 2, 1, 3).reshape(slab, n * size).astype(F32)

    return (
        output,
        input_grad,
        small_full[0],
        columns(0, 0, qw),
        columns(1, 0, kw),
        columns(1, kw, kw),
        ow_full,
        small_full[1],
        small_full[2 : 2 + experts].T,
        gate_grad,
        up_grad,
        down_grad,
    )


def solution(mesh):
    rep, n = mesh.shape["rep"], mesh.shape["shard"]
    yx = math.gcd(rep // 2, 4)
    hi = rep // (2 * yx)
    split = Mesh(mesh.devices.reshape(hi, yx, 2, n), ("hi", "yx", "cr", "shard"))
    rows = ("hi", "yx", "cr", "shard")
    placed = (
        P(rows, None),
        P(rows, None),
        P(rows),
        P(rows, None),
        P("shard"),
        P("shard", None),
        P("shard", None),
        P("shard", None),
        P(None, "shard"),
        P("shard"),
        P("shard", None),
        P(None, "shard", None),
        P(None, "shard", None),
        P(None, "shard", None),
    )
    return jax.shard_map(
        functools.partial(per_device, hi, yx, n),
        mesh=split,
        in_specs=placed,
        out_specs=(
            P(rows, None),
            P(rows, None),
            P("shard"),
            P("shard", None),
            P("shard", None),
            P("shard", None),
            P(None, "shard"),
            P("shard"),
            P("shard", None),
            P(None, "shard", None),
            P(None, "shard", None),
            P(None, "shard", None),
        ),
        check_vma=False,
    )
```

```python
import functools
import math

import jax
import jax.numpy as jnp
from jax import lax
from jax.experimental import pallas as pl
from jax.experimental.pallas import tpu as pltpu
from jax.sharding import Mesh
from jax.sharding import PartitionSpec as P

QUERY_HEADS = 16
KEY_VALUE_HEADS = 8
HEAD = 64
LANES = 128
MIX_LOW = 64

EPS = 1e-06
ROPE_BASE = 10000.0
MASKED = -1e30
F32 = jnp.float32
BF16 = jnp.bfloat16
NT = (((1,), (1,)), ((), ()))
TN = (((0,), (0,)), ((), ()))
VMEM_LIMIT = 60 * 1024 * 1024


def dot(a, b):
    return jnp.dot(a, b, preferred_element_type=F32)


def dot_nt(a, b):
    return lax.dot_general(a, b, NT, preferred_element_type=F32)


def dot_tn(a, b):
    return lax.dot_general(a, b, TN, preferred_element_type=F32)


def split_hi_lo(value):
    high = value.astype(BF16)
    return high, (value - high.astype(F32)).astype(BF16)


def inverse_rms(value):
    return lax.rsqrt(jnp.mean(value * value, axis=-1, keepdims=True) + EPS)


def swap_halves(value):
    width = value.shape[1]
    lane = lax.broadcasted_iota(jnp.int32, value.shape, 1)
    up = pltpu.roll(value, width - HEAD // 2, 1)
    down = pltpu.roll(value, HEAD // 2, 1)
    return jnp.where(lane % HEAD < HEAD // 2, up, down)


def rotate(value, cosine, sine):
    copies = value.shape[1] // LANES
    cosine = jnp.concatenate([cosine] * copies, axis=1)
    sine = jnp.concatenate([sine] * copies, axis=1)
    return value * cosine + swap_halves(value) * sine


def allowed_pairs(seg_col, seg_row, row0, count):
    rows = seg_col.shape[0]
    row = row0 + lax.broadcasted_iota(jnp.int32, (rows, count), 0)
    col = lax.broadcasted_iota(jnp.int32, (rows, count), 1)
    return (seg_col == seg_row) & (col <= row)


def ring_chunk(z, k, parts):
    return lax.rem(z - k + parts, parts)


def chunk_of(index, size):
    return pl.ds(pl.multiple_of(index * size, size), size)


def peer(place_ref, c, j):
    return lax.bitwise_xor(place_ref[2], jnp.int32(j)) * 2 + lax.bitwise_xor(place_ref[3], jnp.int32(c))


def front_kernel(
    block, heads, kv_heads, parts, place_ref, *refs
):
    chunks = refs[:parts]
    (gain_ref, mine_ref, mate_ref, cos_ref, sin_ref, segc_ref, segr_ref,
     x_ref, w_ref, normed_ref, q_ref, k_ref, v_ref, att_ref, lse_ref, out_s, sems) = refs[parts:]
    seq = x_ref.shape[0]
    blocks = seq // block
    group = heads // kv_heads
    qw, kw = heads * HEAD, kv_heads * HEAD
    z = place_ref[0]
    slab = w_ref.shape[0] // parts
    part = slab // (2 * mine_ref.shape[0])
    copies = []
    for i in range(parts):
        at = chunk_of(ring_chunk(z, i, parts), block)
        copies.append(pltpu.make_async_copy(chunks[i], x_ref.at[at, :], sems.at[i]))
    for copy in copies:
        copy.start()
    for c, piece_ref in enumerate((mine_ref, mate_ref)):
        for j in range(piece_ref.shape[0]):
            at = peer(place_ref, c, j) * part
            for i in range(parts):
                start = pl.multiple_of(ring_chunk(z, i, parts) * slab + at, part)
                w_ref[pl.ds(start, part), :] = piece_ref[j, i, :part, :]
    for copy in copies:
        copy.wait()

    def project(i, carry):
        rows = pl.ds(pl.multiple_of(i * block, block), block)
        x = x_ref[rows, :].astype(F32)
        normed = (x * inverse_rms(x) * gain_ref[...]).astype(BF16)
        normed_ref[rows, :] = normed
        qkv = dot(normed, w_ref[...])
        turned = rotate(qkv[:, : qw + kw], cos_ref[rows, :], sin_ref[rows, :])
        for h in range(heads):
            q_ref[h, rows, :] = turned[:, h * HEAD : (h + 1) * HEAD].astype(BF16)
        for h in range(kv_heads):
            k_ref[h, rows, :] = turned[:, qw + h * HEAD : qw + (h + 1) * HEAD].astype(BF16)
            v_ref[h, rows, :] = qkv[:, qw + kw + h * HEAD : qw + kw + (h + 1) * HEAD].astype(BF16)
        return carry

    lax.fori_loop(0, blocks, project, 0)

    def one_head(h, carry):
        kv = h // group
        for i in range(blocks):
            count = (i + 1) * block
            rows = slice(i * block, (i + 1) * block)
            q = q_ref[h, rows, :] * jnp.asarray(0.125, BF16)
            k = k_ref[kv, :count, :]
            v = v_ref[kv, :count, :]
            allowed = allowed_pairs(segc_ref[rows, :], segr_ref[:, :count], i * block, count)
            s = jnp.where(allowed, dot_nt(q, k), MASKED)
            top = jnp.max(s, axis=-1, keepdims=True)
            e = jnp.exp(s - top)
            total = jnp.sum(e, axis=-1, keepdims=True)
            lse_ref[h, rows, :] = top + jnp.log(total)
            p = (e * (1.0 / total)).astype(BF16)
            out_s[h, rows, :] = dot(p, v)
        return carry

    lax.fori_loop(0, heads, one_head, 0)
    for h in range(heads):
        att_ref[:, h * HEAD : (h + 1) * HEAD] = out_s[h].astype(BF16)


def back_kernel(
    block, heads, kv_heads, q_ref, k_ref, v_ref, do_ref, lse_ref, segc_ref, segr_ref,
    raw_ref, do_s, dq_s, dk_s, dv_s,
):
    seq = do_ref.shape[0]
    blocks = seq // block
    group = heads // kv_heads
    qw, kw = heads * HEAD, kv_heads * HEAD
    for h in range(heads):
        do_s[h] = do_ref[:, h * HEAD : (h + 1) * HEAD]
    dk_s[...] = jnp.zeros_like(dk_s)
    dv_s[...] = jnp.zeros_like(dv_s)

    def one_head(h, carry):
        kv = h // group
        for i in range(blocks):
            count = (i + 1) * block
            rows = slice(i * block, (i + 1) * block)
            q = q_ref[h, rows, :] * jnp.asarray(0.125, BF16)
            k = k_ref[kv, :count, :]
            v = v_ref[kv, :count, :]
            do = do_s[h, rows, :]
            allowed = allowed_pairs(segc_ref[rows, :], segr_ref[:, :count], i * block, count)
            s = jnp.where(allowed, dot_nt(q, k), MASKED)
            prob = jnp.exp(s - lse_ref[h, rows, :])
            grad = dot_nt(do, v)
            inner = jnp.sum(prob * grad, axis=-1, keepdims=True)
            ds = (prob * (grad - inner)).astype(BF16)
            dq_s[h, rows, :] = dot(ds, k) * 0.125
            dk_s[kv, :count, :] += dot_tn(ds, q)
            dv_s[kv, :count, :] += dot_tn(prob.astype(BF16), do)
        return carry

    lax.fori_loop(0, heads, one_head, 0)
    for h in range(heads):
        raw_ref[:, h * HEAD : (h + 1) * HEAD] = dq_s[h]
    for h in range(kv_heads):
        raw_ref[:, qw + h * HEAD : qw + (h + 1) * HEAD] = dk_s[h]
        raw_ref[:, qw + kw + h * HEAD : qw + kw + (h + 1) * HEAD] = dv_s[h]


def finish_kernel(
    block, turned, place_ref, raw_ref, x_ref, normed_ref, w_ref, cos_ref, sin_ref, ng_ref, dw_ref, gain_ref, g_s,
):
    seq = x_ref.shape[0]
    blocks = seq // block
    gain_ref[...] = jnp.zeros_like(gain_ref)

    def finish(i, carry):
        rows = pl.ds(pl.multiple_of(i * block, block), block)
        g_s[rows, :turned] = rotate(raw_ref[rows, :turned], cos_ref[rows, :], -sin_ref[rows, :]).astype(BF16)
        g_s[rows, turned:] = raw_ref[rows, turned:].astype(BF16)
        ng = dot_nt(g_s[rows, :], w_ref[...])
        x = x_ref[rows, :].astype(F32)
        gain_ref[...] += jnp.sum(ng * (x * inverse_rms(x)), axis=0, keepdims=True)
        ng_ref[ring_chunk(place_ref[0], i, blocks)] = ng.astype(BF16)
        return carry

    lax.fori_loop(0, blocks, finish, 0)
    width = normed_ref.shape[1]
    for c in range(0, width, 256):
        dw_ref[c : c + 256, :] = dot_tn(normed_ref[:, c : c + 256], g_s[...]).astype(BF16)


def softmax_gates(logits, mask):
    shown = jnp.where(mask > 0.0, logits, MASKED)
    e = jnp.where(mask > 0.0, jnp.exp(shown - jnp.max(shown, axis=-1, keepdims=True)), 0.0)
    return e * (1.0 / jnp.sum(e, axis=-1, keepdims=True))


def mid_kernel(
    place_ref, x_ref, att_ref, mine_ref, mate_ref, gain_ref, router_ref, mask_ref,
    hidden_ref, normed_ref, gates_ref, ow_ref,
):
    parts, width = ow_ref.shape[0], ow_ref.shape[2]
    share = ow_ref.shape[1] // (2 * mine_ref.shape[0])
    fold = mine_ref.shape[3] // width
    lines = share // fold
    skip = mine_ref.shape[2] - lines
    for c, piece_ref in enumerate((mine_ref, mate_ref)):
        for j in range(piece_ref.shape[0]):
            at = peer(place_ref, c, j) * share
            for k in range(parts):
                for f in range(fold):
                    start = pl.multiple_of(at + f * lines, lines)
                    ow_ref[k, pl.ds(start, lines), :] = piece_ref[j, k, skip:, f * width : (f + 1) * width]
    depth = att_ref.shape[2]
    for j in range(parts):
        cols = chunk_of(ring_chunk(place_ref[0], j, parts), width)
        total = x_ref[:, cols].astype(F32)
        for i in range(att_ref.shape[0]):
            total = total + dot(att_ref[i], ow_ref[j, i * depth : (i + 1) * depth, :])
        hidden_ref[:, cols] = total
    hidden = hidden_ref[...]
    normed = (hidden * inverse_rms(hidden) * gain_ref[...]).astype(BF16)
    normed_ref[...] = normed
    gates_ref[...] = softmax_gates(dot(normed, router_ref[...]), mask_ref[...])


def mid_back_kernel(
    place_ref, hidden_ref, nb0_ref, nb1_ref, nb2_ref, dy_ref, gates_ref, normed_ref, router_ref, gain_ref, ow_ref, att_ref,
    hg_ref, ag_ref, owg_ref, fg_ref, rg_ref, aog_s,
):
    gates = gates_ref[...]
    width_all = hidden_ref.shape[1]
    nb = sum(ref[...].astype(F32) for ref in (nb1_ref, nb2_ref)) + nb0_ref[...].astype(F32)
    mix = nb[:, width_all:]
    mix = mix + pltpu.roll(mix, LANES - MIX_LOW, 1)
    lg = gates * (mix - jnp.sum(gates * mix, axis=-1, keepdims=True))
    high, low = split_hi_lo(lg)
    normed = normed_ref[...]
    rg_ref[...] = dot_tn(high, normed) + dot_tn(low, normed)
    router = router_ref[...]
    ng = nb[:, :width_all] + dot_nt(high, router) + dot_nt(low, router)
    hidden = hidden_ref[...]
    inv = inverse_rms(hidden)
    scaled = hidden * inv
    fg_ref[...] = jnp.sum(ng * scaled, axis=0, keepdims=True)
    w = ng * gain_ref[...]
    hg = dy_ref[...].astype(F32) + inv * (w - scaled * jnp.mean(w * scaled, axis=-1, keepdims=True))
    hg_ref[...] = hg
    aog_s[...] = hg.astype(BF16)
    parts, width = ow_ref.shape[0], ow_ref.shape[2]
    groups, _, depth = att_ref.shape
    for i in range(groups):
        rows = slice(i * depth, (i + 1) * depth)
        total = None
        for j in range(parts):
            chunk = ring_chunk(place_ref[0], j, parts)
            part = dot_nt(aog_s[:, chunk_of(chunk, width)], ow_ref[j, rows, :])
            total = part if total is None else total + part
        ag_ref[i] = total.astype(BF16)
        for j in range(parts):
            owg_ref[j, rows, :] = dot_tn(att_ref[i], aog_s[:, j * width : (j + 1) * width]).astype(BF16)


def expert_kernel(parts, e, place_ref, n2_ref, dyx_ref, router_ref, w_ref, *refs):
    previous = refs[:2] if e else ()
    moe_ref, nb_ref, g_ref, inner_ref, gg_ref, ug_ref, wg_s, wu_s, wd_s, sems = refs[len(previous) :]
    width, ff = wg_s.shape
    slab, ff_slab = width // parts, ff // parts

    @pl.when(pl.program_id(0) == 0)
    def load():
        copies = []

        def move(start, count, target):
            copies.append(pltpu.make_async_copy(w_ref.at[start : start + count, :], target, sems.at[len(copies)]))

        for k in range(parts):
            start = k * 3 * slab
            move(start, slab, wg_s.at[k * slab : (k + 1) * slab, :])
            move(start + slab, slab, wu_s.at[k * slab : (k + 1) * slab, :])
            for c in range(width // ff):
                at = start + 2 * slab + c * ff_slab
                move(at, ff_slab, wd_s.at[k * ff_slab : (k + 1) * ff_slab, c * ff : (c + 1) * ff])
        for copy in copies:
            copy.start()
        for copy in copies:
            copy.wait()

    x = n2_ref[...]
    dy = dyx_ref[:, :width].astype(F32)
    gates = softmax_gates(dot(x, router_ref[...]), dyx_ref[:, width:].astype(F32))
    lane = lax.broadcasted_iota(jnp.int32, gates.shape, 1)
    at = place_ref[1] + e
    g = jnp.sum(jnp.where(lane == at, gates, 0.0), axis=-1, keepdims=True)
    ga = dot(x, wg_s[...])
    ua = dot(x, wu_s[...])
    sg = jax.nn.sigmoid(ga)
    act = ga * sg
    inner = (act * ua).astype(BF16)
    inner_ref[...] = inner
    eo = dot(inner, wd_s[...]).astype(BF16).astype(F32)
    moe = g * eo
    high, low = split_hi_lo(jnp.sum(dy * eo, axis=-1, keepdims=True))
    mix = jnp.where(lane == at, high.astype(F32), 0.0) + jnp.where(lane == MIX_LOW + at, low.astype(F32), 0.0)
    g_ref[...] = jnp.where(lane == 0, g, 0.0)
    ig = dot_nt((g * dy).astype(BF16), wd_s[...])
    gg = (ig * ua * sg * (1.0 + ga * (1.0 - sg))).astype(BF16)
    ug = (ig * act).astype(BF16)
    gg_ref[...] = gg
    ug_ref[...] = ug
    nb = dot_nt(gg, wg_s[...]) + dot_nt(ug, wu_s[...])
    if e:
        moe = moe + previous[0][...].astype(F32)
        nb = nb + previous[1][:, :width].astype(F32)
        mix = mix + previous[1][:, width:].astype(F32)
    moe_ref[...] = moe.astype(BF16)
    nb_ref[:, :width] = nb.astype(BF16)
    nb_ref[:, width:] = mix.astype(BF16)


def expert_grad_kernel(parts, half, *refs):
    halves = (refs[:6], refs[6:12])
    out_ref, g_s, u_s, d_s = refs[12:]
    step = pl.program_id(0)
    width, ff = g_s.shape
    slab, ff_slab = width // parts, ff // parts

    @pl.when(step == 0)
    def clear():
        g_s[...] = jnp.zeros_like(g_s)
        u_s[...] = jnp.zeros_like(u_s)
        d_s[...] = jnp.zeros_like(d_s)

    def add(n2_ref, dyx_ref, g_ref, inner_ref, gg_ref, ug_ref):
        x = n2_ref[...]
        g = jnp.sum(g_ref[...], axis=-1, keepdims=True)
        og = (g * dyx_ref[:, :width].astype(F32)).astype(BF16)
        g_s[...] += dot_tn(x, gg_ref[...])
        u_s[...] += dot_tn(x, ug_ref[...])
        d_s[...] += dot_tn(inner_ref[...], og)

    pl.when(step < half)(lambda: add(*halves[0]))
    pl.when(step >= half)(lambda: add(*halves[1]))

    @pl.when(step == pl.num_programs(0) - 1)
    def store():
        for k in range(parts):
            start = k * 3 * slab
            out_ref[start : start + slab, :] = g_s[k * slab : (k + 1) * slab, :].astype(BF16)
            out_ref[start + slab : start + 2 * slab, :] = u_s[k * slab : (k + 1) * slab, :].astype(BF16)
            for c in range(width // ff):
                at = start + 2 * slab + c * ff_slab
                out_ref[at : at + ff_slab, :] = d_s[k * ff_slab : (k + 1) * ff_slab, c * ff : (c + 1) * ff].astype(BF16)


def share_kernel(count, place_ref, *refs):
    gate_ref, up_ref, down_ref = refs[-3:]
    _, _, slab, ff = gate_ref.shape
    ff_slab, width = down_ref.shape[2:]
    for i in range(count):

        @pl.when(pl.program_id(0) == i)
        def copy(piece_ref=refs[i]):
            gate_ref[0, 0] = piece_ref[:slab, :].astype(F32)
            up_ref[0, 0] = piece_ref[slab : 2 * slab, :].astype(F32)
            for c in range(width // ff):
                at = 2 * slab + c * ff_slab
                down_ref[0, 0, :, c * ff : (c + 1) * ff] = piece_ref[at : at + ff_slab, :].astype(F32)


def sds(shape, dtype):
    return jax.ShapeDtypeStruct(shape, dtype)


def params():
    return pltpu.CompilerParams(vmem_limit_bytes=VMEM_LIMIT)


def cost(flops, traffic):
    return pl.CostEstimate(flops=int(flops), bytes_accessed=int(traffic), transcendentals=0)


def per_device(
    hi, yx, n, tokens, cotangent, segment_ids, routes, attn_gain, query_weight, key_matrix, value_weight,
    out_weight, ffn_gain, router_weight, gate_weight, up_weight, down_weight,
):
    rows, width = tokens.shape
    seq = rows * n
    experts = gate_weight.shape[0]
    ep = yx * 2
    own = experts // ep
    heads, kv_heads = QUERY_HEADS // n, KEY_VALUE_HEADS // n
    qw, kw = heads * HEAD, kv_heads * HEAD
    cols = qw + 2 * kw
    slab = width // n
    ff = gate_weight.shape[2]
    z = lax.axis_index("shard").astype(jnp.int32)
    core = lax.axis_index("cr").astype(jnp.int32)
    chip = lax.axis_index("yx").astype(jnp.int32)
    r = chip * 2 + core
    place = jnp.stack([z, r * own, chip, core])
    smem = pl.BlockSpec(memory_space=pltpu.SMEM)
    vmem = pl.BlockSpec(memory_space=pltpu.VMEM)
    hbm = pl.BlockSpec(memory_space=pl.ANY)

    def shift(value, k=1):
        return lax.ppermute(value, "shard", [(i, (i + k) % n) for i in range(n)])

    def swap(value):
        return lax.ppermute(value, "cr", [(0, 1), (1, 0)])

    def flip(value, j):
        return lax.ppermute(value, "yx", [(i, i ^ j) for i in range(yx)])

    def pick(value, index, axis):
        return lax.dynamic_index_in_dim(value, index, axis, keepdims=False)

    def absolute(parts):
        stacked = jnp.stack(parts)
        return jnp.stack([pick(stacked, lax.rem(z - j + n, n), 0) for j in range(n)])

    def plus(one, other):
        return (one.astype(F32) + other.astype(F32)).astype(BF16)

    def around(value):
        return across_too(value, flip(value, 1), flip(value, 2))

    def across_too(value, by_x, by_y):
        half = value.shape[0] // 2
        across = jnp.concatenate([flip(by_x[:half], 2), flip(by_y[half:], 1)], axis=0)
        return [value, by_x, by_y, across]

    def plane_sum(blocks):
        half = blocks[0].shape[0] // 2
        low, high = flip(blocks[3][:half], 1), flip(blocks[3][half:], 2)
        to_y = jnp.concatenate([plus(blocks[2][:half], low), blocks[2][half:]], axis=0)
        to_x = jnp.concatenate([blocks[1][:half], plus(blocks[1][half:], high)], axis=0)
        return [blocks[0], flip(to_x, 1), flip(to_y, 2)]

    chunks = [tokens, shift(tokens)]

    pack = jnp.concatenate(
        [attn_gain[None], ffn_gain[None], segment_ids.astype(BF16)[None], router_weight.T], axis=0
    )
    packs = [pack] + [shift(pack, k) for k in range(1, n)]
    part_rows = slab // ep
    by_dest = jnp.concatenate(
        [
            lax.dynamic_slice_in_dim(w, r * part_rows, part_rows, axis=0).reshape(part_rows, n, -1)
            for w in (query_weight, key_matrix, value_weight)
        ],
        axis=2,
    )
    ow_rows = out_weight.shape[0] // ep
    fold = cols // slab
    ow_mine = lax.dynamic_slice_in_dim(out_weight, r * ow_rows, ow_rows, axis=0)
    ow_mine = ow_mine.reshape(fold, ow_rows // fold, slab).transpose(1, 0, 2).reshape(ow_rows // fold, cols)

    def piece(k):
        return jnp.concatenate([pick(by_dest, lax.rem(z + k, n), 1), ow_mine], axis=0)

    dense_mine = [piece(0)] + [shift(piece(k), k) for k in range(1, n)]
    ids = jnp.arange(experts, dtype=jnp.int32)
    routed = jnp.any(routes[:, :, None] == ids[None, None, :], axis=1)
    mask_own = jnp.pad(routed.astype(F32), ((0, 0), (0, LANES - experts)))
    dyx_mine = around(jnp.concatenate([cotangent, mask_own.astype(BF16)], axis=1))
    chunks[1], packs, dense_mine = lax.optimization_barrier((chunks[1], packs, dense_mine))
    chunks.append(shift(chunks[1]))
    dense_mine = around(jnp.stack(dense_mine))
    chunks[2], dense_mine, dyx_mine = lax.optimization_barrier((chunks[2], dense_mine, dyx_mine))
    for _ in range(n - 3):
        chunks.append(shift(chunks[-1]))
    dense_mine = jnp.stack(dense_mine)
    dense_mate = swap(dense_mine)
    packs = absolute(packs)
    gain1 = packs[:, 0, :].reshape(1, width).astype(F32)
    gain2 = packs[:, 1, :].reshape(1, width).astype(F32)
    segments = packs[:, 2, :].reshape(seq).astype(F32)
    seg_col, seg_row = segments[:, None], segments[None, :]
    router = jnp.pad(packs[:, 3:, :].transpose(0, 2, 1).reshape(width, experts), ((0, 0), (0, LANES - experts)))

    dyx_mine = jnp.concatenate(dyx_mine, axis=0)
    dyx_mate = swap(dyx_mine)

    positions = jnp.arange(seq, dtype=jnp.int32).astype(F32)
    frequency = ROPE_BASE ** (-jnp.arange(HEAD // 2, dtype=F32) / (HEAD // 2))
    angles = positions[:, None] * frequency[None, :]
    cosine, sine = jnp.cos(angles), jnp.sin(angles)
    cosine = jnp.concatenate([cosine] * 4, axis=1)
    sine = jnp.concatenate([-sine, sine] * 2, axis=1)

    folds = width // ff
    packed = []
    for e in range(own):
        gate, up, down = (pick(w, r * own + e, 0) for w in (gate_weight, up_weight, down_weight))
        down = [down[:, c * ff : (c + 1) * ff] for c in range(folds)]
        packed.append(jnp.concatenate([gate, up] + down, axis=0))
    packed, chunks = lax.optimization_barrier((packed, chunks))
    weights = [lax.all_gather(w, "shard", axis=0, tiled=True) for w in packed]

    x_all, w_qkv, normed, q, k, v, att, lse = pl.pallas_call(
        functools.partial(front_kernel, rows, heads, kv_heads, n),
        in_specs=[smem] + [hbm] * n + [vmem] * 7,
        out_shape=(
            sds((seq, width), BF16),
            sds((width, cols), BF16),
            sds((seq, width), BF16),
            sds((heads, seq, HEAD), BF16),
            sds((kv_heads, seq, HEAD), BF16),
            sds((kv_heads, seq, HEAD), BF16),
            sds((seq, qw), BF16),
            sds((heads, seq, 1), F32),
        ),
        scratch_shapes=[pltpu.VMEM((heads, seq, HEAD), F32), pltpu.SemaphoreType.DMA((n,))],
        compiler_params=params(),
        cost_estimate=cost(2 * seq * width * cols, 60e6),
        name="front",
    )(place, *chunks, gain1, dense_mine, dense_mate, cosine, sine, seg_col, seg_row)

    att = lax.all_to_all(att.reshape(n, rows, qw), "shard", 0, 0)
    hidden, normed2, gates_own, ow = pl.pallas_call(
        mid_kernel,
        in_specs=[smem] + [vmem] * 7,
        out_shape=(
            sds((rows, width), F32),
            sds((rows, width), BF16),
            sds((rows, LANES), F32),
            sds((n, ep * ow_rows, slab), BF16),
        ),
        compiler_params=params(),
        cost_estimate=cost(2 * rows * width * width, 14e6),
        name="mid",
    )(place, tokens, att, dense_mine, dense_mate, gain2, router, mask_own)

    n2_mine = jnp.concatenate(around(normed2), axis=0)
    n2_mate = swap(n2_mine)

    total = yx * rows
    block = min(512, total)
    steps = total // block

    def by_block(size):
        return pl.BlockSpec((block, size), lambda i: (i, 0))

    def run_expert(e, n2, dyx, previous):
        return pl.pallas_call(
            functools.partial(expert_kernel, n, e),
            grid=(steps,),
            in_specs=[
                smem,
                by_block(width),
                by_block(width + LANES),
                pl.BlockSpec((width, LANES), lambda i: (0, 0)),
                hbm,
            ]
            + ([by_block(width), by_block(width + LANES)] if e else []),
            out_specs=(
                by_block(width),
                by_block(width + LANES),
                by_block(LANES),
                by_block(ff),
                by_block(ff),
                by_block(ff),
            ),
            out_shape=(
                sds((total, width), BF16),
                sds((total, width + LANES), BF16),
                sds((total, LANES), F32),
                sds((total, ff), BF16),
                sds((total, ff), BF16),
                sds((total, ff), BF16),
            ),
            scratch_shapes=[
                pltpu.VMEM((width, ff), BF16),
                pltpu.VMEM((width, ff), BF16),
                pltpu.VMEM((ff, width), BF16),
                pltpu.SemaphoreType.DMA(((2 + folds) * n,)),
            ],
            compiler_params=params(),
            cost_estimate=cost(12 * total * width * ff, 36e6),
            name="expert",
        )(place, n2, dyx, router, weights[e], *previous)

    def half_specs(at):
        sizes = (width, width + LANES, LANES, ff, ff, ff)
        return [pl.BlockSpec((block, size), lambda i: (at(i), 0)) for size in sizes]

    def weight_grads(mate, mine):
        return pl.pallas_call(
            functools.partial(expert_grad_kernel, n, steps),
            grid=(2 * steps,),
            in_specs=half_specs(lambda i: jnp.minimum(i, steps - 1))
            + half_specs(lambda i: jnp.maximum(i - steps, 0)),
            out_specs=pl.BlockSpec((3 * width, ff), lambda i: (0, 0)),
            out_shape=sds((3 * width, ff), BF16),
            scratch_shapes=[
                pltpu.VMEM((width, ff), F32),
                pltpu.VMEM((width, ff), F32),
                pltpu.VMEM((ff, width), F32),
            ],
            compiler_params=params(),
            cost_estimate=cost(12 * total * width * ff, 40e6),
            name="expert_grads",
        )(n2_mate, dyx_mate, *mate, n2_mine, dyx_mine, *mine)

    def spread(value):
        return [value[j * rows : (j + 1) * rows] for j in range(yx)]

    previous_mate = previous_mine = ()
    owned = []
    for e in range(own):
        *previous_mate, g_mate, in_mate, gg_mate, ug_mate = run_expert(e, n2_mate, dyx_mate, previous_mate)
        if e == own - 1:
            moe_got, nb_got = swap(previous_mate[0]), swap(previous_mate[1])
        *previous_mine, g_mine, in_mine, gg_mine, ug_mine = run_expert(e, n2_mine, dyx_mine, previous_mine)
        grads = weight_grads((g_mate, in_mate, gg_mate, ug_mate), (g_mine, in_mine, gg_mine, ug_mine))
        if e < own - 1:
            grads, weights[e + 1] = lax.optimization_barrier((grads, weights[e + 1]))
        else:
            nb_parts = plane_sum(spread(plus(previous_mine[1], nb_got)))
            moe_sum = plus(previous_mine[0], moe_got)
            nb_parts, moe_sum, grads = lax.optimization_barrier((nb_parts, moe_sum, grads))
        grads = lax.psum_scatter(grads, "shard", scatter_dimension=0, tiled=True)
        if hi > 1:
            grads = lax.psum(grads.astype(F32), "hi").astype(BF16)
        owned.append(grads)

    hidden_grad, att_grad, ow_grad, ffn_grad, router_grad = pl.pallas_call(
        mid_back_kernel,
        in_specs=[smem] + [vmem] * 11,
        out_shape=(
            sds((rows, width), F32),
            sds((n, rows, qw), BF16),
            sds((n, n * qw, slab), BF16),
            sds((1, width), F32),
            sds((LANES, width), F32),
        ),
        scratch_shapes=[pltpu.VMEM((rows, width), BF16)],
        compiler_params=params(),
        cost_estimate=cost(4 * rows * width * width, 20e6),
        name="mid_back",
    )(place, hidden, *nb_parts, cotangent, gates_own, normed2, router, gain2, ow, att)

    kvw = 2 * kw
    wide = max(slab, qw, kvw)
    small_rows = 16

    def widen(part):
        return jnp.pad(part, ((0, 0),) * 3 + ((0, wide - part.shape[3]),))

    def rows_of(small):
        small = jnp.pad(small, ((0, ep * small_rows - small.shape[0]), (0, 0)))
        return widen(small.reshape(ep, small_rows, n, slab).transpose(2, 0, 1, 3).astype(BF16))

    def dense_sum(pieces):
        dense = jnp.concatenate(pieces, axis=2)
        depth = dense.shape[2]
        dense = dense.reshape(n, yx, 2, depth, wide).transpose(2, 1, 0, 3, 4)
        dense = plus(pick(dense, core, 0), swap(pick(dense, 1 - core, 0)))
        parts = plane_sum([pick(dense, lax.bitwise_xor(chip, jnp.int32(j)), 0) for j in range(yx)])
        return sum(p.astype(F32) for p in parts).astype(BF16)

    att_grad = lax.all_to_all(att_grad, "shard", 0, 0).reshape(seq, qw)
    att_grad, owned[0] = lax.optimization_barrier((att_grad, owned[0]))
    early = around(owned[0])
    small = rows_of(jnp.concatenate([ffn_grad, router_grad[:experts]], axis=0))
    dense_early = dense_sum([widen(ow_grad.reshape(n, ep, ow_rows, slab)), small])
    raw = pl.pallas_call(
        functools.partial(back_kernel, rows, heads, kv_heads),
        out_shape=sds((seq, cols), F32),
        scratch_shapes=[
            pltpu.VMEM((heads, seq, HEAD), BF16),
            pltpu.VMEM((heads, seq, HEAD), F32),
            pltpu.VMEM((kv_heads, seq, HEAD), F32),
            pltpu.VMEM((kv_heads, seq, HEAD), F32),
        ],
        compiler_params=params(),
        cost_estimate=cost(2 * seq * width * cols, 52e6),
        name="back",
    )(q, k, v, att_grad, lse, seg_col, seg_row)
    raw, owned, early, dense_early = lax.optimization_barrier((raw, owned, early, dense_early))
    ng, qkv_grad, gain_grad = pl.pallas_call(
        functools.partial(finish_kernel, rows, qw + kw),
        in_specs=[smem] + [vmem] * 6,
        out_shape=(sds((n, rows, width), BF16), sds((width, cols), BF16), sds((1, width), F32)),
        scratch_shapes=[pltpu.VMEM((seq, cols), BF16)],
        compiler_params=params(),
        cost_estimate=cost(4 * seq * width * cols, 30e6),
        name="finish",
    )(place, raw, x_all, normed, w_qkv, cosine, sine)
    qkv_rows = qkv_grad.reshape(n, ep, part_rows, cols)
    def share(e, mine, shared):
        pieces = [p for one in mine for p in (one, swap(one))]

        def out_index(j, place_ref):
            return (peer(place_ref, j % 2, j // 2), e, 0, 0)

        return pl.pallas_call(
            functools.partial(share_kernel, ep),
            grid_spec=pltpu.PrefetchScalarGridSpec(
                num_scalar_prefetch=1,
                grid=(ep,),
                in_specs=[pl.BlockSpec((3 * slab, ff), lambda j, place_ref: (0, 0))] * ep + [hbm] * len(shared),
                out_specs=(
                    pl.BlockSpec((1, 1, slab, ff), out_index),
                    pl.BlockSpec((1, 1, slab, ff), out_index),
                    pl.BlockSpec((1, 1, ff // n, width), out_index),
                ),
            ),
            out_shape=(
                sds((ep, own, slab, ff), F32),
                sds((ep, own, slab, ff), F32),
                sds((ep, own, ff // n, width), F32),
            ),
            input_output_aliases={1 + ep + i: i for i in range(len(shared))},
            compiler_params=params(),
            cost_estimate=cost(0, 20e6),
            name="share",
        )(place, *pieces, *shared)

    dense = dense_sum([rows_of(gain_grad), widen(qkv_rows[..., :qw]), widen(qkv_rows[..., qw:])])
    dense = jnp.concatenate([dense_early, dense], axis=1)
    if hi > 1:
        dense = lax.psum(dense.astype(F32), "hi").astype(BF16)
    got = shift(ng[1])
    shared = share(0, early, ())
    last = [(value, flip(value, 1), flip(value, 2)) for value in owned[1:]]
    dense, got, shared, last = lax.optimization_barrier((dense, got, shared, last))
    for e in range(1, own):
        shared = share(e, across_too(*last[e - 1]), shared)
    for step in range(2, n):
        got = shift((got.astype(F32) + ng[step].astype(F32)).astype(BF16))
    part = got.astype(F32) + ng[0].astype(F32)
    x = tokens.astype(F32)
    inv = inverse_rms(x)
    scaled = x * inv
    w1 = part * gain1
    input_grad = hidden_grad + inv * (w1 - scaled * jnp.mean(w1 * scaled, axis=-1, keepdims=True))

    moe_parts = plane_sum(spread(moe_sum))
    output = (hidden + sum(p.astype(F32) for p in moe_parts)).astype(BF16)

    gate_grad, up_grad, down_grad = (g.reshape((experts,) + g.shape[2:]) for g in shared)

    dense = [pick(dense, z, 0)] + [shift(pick(dense, lax.rem(z + k, n), 0), k) for k in range(1, n)]
    cut = ow_rows + 2 * small_rows
    summed = sum(p[:cut].astype(F32) for p in dense).astype(BF16)
    kept = absolute([p[cut:] for p in dense]).reshape(n * 2 * part_rows, wide)
    mine = jnp.stack(around(jnp.concatenate([summed, kept], axis=0)))
    both = jnp.stack([mine, swap(mine)], axis=1).reshape((ep,) + mine.shape[1:])
    full = jnp.stack([pick(both, lax.bitwise_xor(r, jnp.int32(i)), 0) for i in range(ep)])
    ow_full = full[:, :ow_rows, :slab].reshape(-1, slab).astype(F32)
    small_full = full[:, ow_rows : ow_rows + small_rows, :slab].reshape(-1, slab).astype(F32)
    gain_full = full[0, ow_rows + small_rows, :slab].astype(F32)
    kept = full[:, cut:].reshape(ep, n, 2, part_rows, wide)

    def columns(which, start, size):
        part = kept[:, :, which, :, start : start + size]
        return part.transpose(0, 2, 1, 3).reshape(slab, n * size).astype(F32)

    return (
        output,
        input_grad,
        gain_full,
        columns(0, 0, qw),
        columns(1, 0, kw),
        columns(1, kw, kw),
        ow_full,
        small_full[0],
        small_full[1 : 1 + experts].T,
        gate_grad,
        up_grad,
        down_grad,
    )


def solution(mesh):
    rep, n = mesh.shape["rep"], mesh.shape["shard"]
    yx = math.gcd(rep // 2, 4)
    hi = rep // (2 * yx)
    split = Mesh(mesh.devices.reshape(hi, yx, 2, n), ("hi", "yx", "cr", "shard"))
    rows = ("hi", "yx", "cr", "shard")
    placed = (
        P(rows, None),
        P(rows, None),
        P(rows),
        P(rows, None),
        P("shard"),
        P("shard", None),
        P("shard", None),
        P("shard", None),
        P(None, "shard"),
        P("shard"),
        P("shard", None),
        P(None, "shard", None),
        P(None, "shard", None),
        P(None, "shard", None),
    )
    return jax.shard_map(
        functools.partial(per_device, hi, yx, n),
        mesh=split,
        in_specs=placed,
        out_specs=(
            P(rows, None),
            P(rows, None),
            P("shard"),
            P("shard", None),
            P("shard", None),
            P("shard", None),
            P(None, "shard"),
            P("shard"),
            P("shard", None),
            P(None, "shard", None),
            P(None, "shard", None),
            P(None, "shard", None),
        ),
        check_vma=False,
    )
```

```python
import functools
import math

import jax
import jax.numpy as jnp
from jax import lax
from jax.experimental import pallas as pl
from jax.experimental.pallas import tpu as pltpu
from jax.sharding import Mesh
from jax.sharding import PartitionSpec as P

QUERY_HEADS = 16
KEY_VALUE_HEADS = 8
HEAD = 64
LANES = 128
MIX_LOW = 64
SCALE = 0.02

EPS = 1e-06
ROPE_BASE = 10000.0
MASKED = -1e30
F32 = jnp.float32
BF16 = jnp.bfloat16
NT = (((1,), (1,)), ((), ()))
TN = (((0,), (0,)), ((), ()))
VMEM_LIMIT = 60 * 1024 * 1024


def dot(a, b):
    return jnp.dot(a, b, preferred_element_type=F32)


def dot_nt(a, b):
    return lax.dot_general(a, b, NT, preferred_element_type=F32)


def dot_tn(a, b):
    return lax.dot_general(a, b, TN, preferred_element_type=F32)


def split_hi_lo(value):
    high = value.astype(BF16)
    return high, (value - high.astype(F32)).astype(BF16)


def inverse_rms(value):
    return lax.rsqrt(jnp.mean(value * value, axis=-1, keepdims=True) + EPS)


def swap_halves(value):
    width = value.shape[1]
    lane = lax.broadcasted_iota(jnp.int32, value.shape, 1)
    up = pltpu.roll(value, width - HEAD // 2, 1)
    down = pltpu.roll(value, HEAD // 2, 1)
    return jnp.where(lane % HEAD < HEAD // 2, up, down)


def rotate(value, cosine, sine):
    copies = value.shape[1] // LANES
    cosine = jnp.concatenate([cosine] * copies, axis=1)
    sine = jnp.concatenate([sine] * copies, axis=1)
    return value * cosine + swap_halves(value) * sine


def allowed_pairs(seg_col, seg_row, row0, count):
    rows = seg_col.shape[0]
    row = row0 + lax.broadcasted_iota(jnp.int32, (rows, count), 0)
    col = lax.broadcasted_iota(jnp.int32, (rows, count), 1)
    return (seg_col == seg_row) & (col <= row)


def ring_chunk(z, k, parts):
    return lax.rem(z - k + parts, parts)


def chunk_of(index, size):
    return pl.ds(pl.multiple_of(index * size, size), size)


def peer(place_ref, c, j):
    return lax.bitwise_xor(place_ref[2], jnp.int32(j)) * 2 + lax.bitwise_xor(place_ref[3], jnp.int32(c))


def front_kernel(
    block, heads, kv_heads, place_ref, x_ref, gain_ref, mine_ref, mate_ref, cos_ref, sin_ref, segc_ref, segr_ref,
    w_ref, normed_ref, q_ref, k_ref, v_ref, att_ref, lse_ref, out_s,
):
    seq = x_ref.shape[0]
    blocks = seq // block
    group = heads // kv_heads
    qw, kw = heads * HEAD, kv_heads * HEAD
    z = place_ref[0]
    slab = w_ref.shape[0] // blocks
    part = slab // (2 * mine_ref.shape[0])
    for c, piece_ref in enumerate((mine_ref, mate_ref)):
        for j in range(piece_ref.shape[0]):
            at = peer(place_ref, c, j) * part
            for i in range(blocks):
                start = pl.multiple_of(ring_chunk(z, i, blocks) * slab + at, part)
                w_ref[pl.ds(start, part), :] = piece_ref[j, i, :part, :]

    def project(i, carry):
        rows = pl.ds(pl.multiple_of(i * block, block), block)
        x = x_ref[rows, :].astype(F32)
        normed = (x * inverse_rms(x) * gain_ref[...]).astype(BF16)
        normed_ref[rows, :] = normed
        qkv = dot(normed, w_ref[...])
        turned = rotate(qkv[:, : qw + kw], cos_ref[rows, :], sin_ref[rows, :])
        for h in range(heads):
            q_ref[h, rows, :] = turned[:, h * HEAD : (h + 1) * HEAD].astype(BF16)
        for h in range(kv_heads):
            k_ref[h, rows, :] = turned[:, qw + h * HEAD : qw + (h + 1) * HEAD].astype(BF16)
            v_ref[h, rows, :] = qkv[:, qw + kw + h * HEAD : qw + kw + (h + 1) * HEAD].astype(BF16)
        return carry

    lax.fori_loop(0, blocks, project, 0)

    def one_head(h, carry):
        kv = h // group
        for i in range(blocks):
            count = (i + 1) * block
            rows = slice(i * block, (i + 1) * block)
            q = q_ref[h, rows, :] * jnp.asarray(0.125, BF16)
            k = k_ref[kv, :count, :]
            v = v_ref[kv, :count, :]
            allowed = allowed_pairs(segc_ref[rows, :], segr_ref[:, :count], i * block, count)
            s = jnp.where(allowed, dot_nt(q, k), MASKED)
            top = jnp.max(s, axis=-1, keepdims=True)
            e = jnp.exp(s - top)
            total = jnp.sum(e, axis=-1, keepdims=True)
            lse_ref[h, rows, :] = top + jnp.log(total)
            p = (e * (1.0 / total)).astype(BF16)
            out_s[h, rows, :] = dot(p, v)
        return carry

    lax.fori_loop(0, heads, one_head, 0)
    for i in range(blocks):
        k = lax.rem(i - z + blocks, blocks)
        for h in range(heads):
            att_ref[k, :, h * HEAD : (h + 1) * HEAD] = out_s[h, i * block : (i + 1) * block, :].astype(BF16)


def back_kernel(
    block, heads, kv_heads, place_ref, q_ref, k_ref, v_ref, lse_ref, segc_ref, segr_ref, *refs
):
    seq = q_ref.shape[1]
    blocks = seq // block
    raw_ref, do_s, dq_s, dk_s, dv_s = refs[blocks:]
    group = heads // kv_heads
    qw, kw = heads * HEAD, kv_heads * HEAD
    for k in range(blocks):
        at = chunk_of(lax.rem(place_ref[0] + k, blocks), block)
        for h in range(heads):
            do_s[h, at, :] = refs[k][:, h * HEAD : (h + 1) * HEAD]
    dk_s[...] = jnp.zeros_like(dk_s)
    dv_s[...] = jnp.zeros_like(dv_s)

    def one_head(h, carry):
        kv = h // group
        for i in range(blocks):
            count = (i + 1) * block
            rows = slice(i * block, (i + 1) * block)
            q = q_ref[h, rows, :] * jnp.asarray(0.125, BF16)
            k = k_ref[kv, :count, :]
            v = v_ref[kv, :count, :]
            do = do_s[h, rows, :]
            allowed = allowed_pairs(segc_ref[rows, :], segr_ref[:, :count], i * block, count)
            s = jnp.where(allowed, dot_nt(q, k), MASKED)
            prob = jnp.exp(s - lse_ref[h, rows, :])
            grad = dot_nt(do, v)
            inner = jnp.sum(prob * grad, axis=-1, keepdims=True)
            ds = (prob * (grad - inner)).astype(BF16)
            dq_s[h, rows, :] = dot(ds, k) * 0.125
            dk_s[kv, :count, :] += dot_tn(ds, q)
            dv_s[kv, :count, :] += dot_tn(prob.astype(BF16), do)
        return carry

    lax.fori_loop(0, heads, one_head, 0)
    for h in range(heads):
        raw_ref[:, h * HEAD : (h + 1) * HEAD] = dq_s[h]
    for h in range(kv_heads):
        raw_ref[:, qw + h * HEAD : qw + (h + 1) * HEAD] = dk_s[h]
        raw_ref[:, qw + kw + h * HEAD : qw + kw + (h + 1) * HEAD] = dv_s[h]


def finish_kernel(
    block, turned, raw_ref, x_ref, normed_ref, w_ref, cos_ref, sin_ref, ng_ref, dw_ref, gain_ref, g_s,
):
    seq = x_ref.shape[0]
    blocks = seq // block
    gain_ref[...] = jnp.zeros_like(gain_ref)

    def finish(i, carry):
        rows = pl.ds(pl.multiple_of(i * block, block), block)
        g_s[rows, :turned] = rotate(raw_ref[rows, :turned], cos_ref[rows, :], -sin_ref[rows, :]).astype(BF16)
        g_s[rows, turned:] = raw_ref[rows, turned:].astype(BF16)
        ng = dot_nt(g_s[rows, :], w_ref[...])
        x = x_ref[rows, :].astype(F32)
        gain_ref[...] += jnp.sum(ng * (x * inverse_rms(x)), axis=0, keepdims=True)
        ng_ref[rows, :] = ng.astype(BF16)
        return carry

    lax.fori_loop(0, blocks, finish, 0)
    width = normed_ref.shape[1]
    for c in range(0, width, 256):
        dw_ref[c : c + 256, :] = dot_tn(normed_ref[:, c : c + 256], g_s[...]).astype(BF16)


def softmax_gates(logits, mask):
    shown = jnp.where(mask > 0.0, logits, MASKED)
    e = jnp.where(mask > 0.0, jnp.exp(shown - jnp.max(shown, axis=-1, keepdims=True)), 0.0)
    return e * (1.0 / jnp.sum(e, axis=-1, keepdims=True))


def mid_kernel(
    place_ref, x_ref, mine_ref, mate_ref, gain_ref, router_ref, mask_ref, *refs
):
    hidden_ref, normed_ref, gates_ref, ow_ref = refs[-4:]
    att_refs = refs[:-4]
    parts, width = ow_ref.shape[0], ow_ref.shape[2]
    share = ow_ref.shape[1] // (2 * mine_ref.shape[0])
    fold = mine_ref.shape[3] // width
    lines = share // fold
    skip = ow_ref.shape[0] * width // (2 * parts * mine_ref.shape[0])
    for c, piece_ref in enumerate((mine_ref, mate_ref)):
        for j in range(piece_ref.shape[0]):
            at = peer(place_ref, c, j) * share
            for k in range(parts):
                for f in range(fold):
                    start = pl.multiple_of(at + f * lines, lines)
                    ow_ref[k, pl.ds(start, lines), :] = piece_ref[j, k, skip : skip + lines, f * width : (f + 1) * width]
    depth = att_refs[0].shape[1]
    for j in range(parts):
        cols = chunk_of(ring_chunk(place_ref[0], j, parts), width)
        total = x_ref[:, cols].astype(F32)
        for i in range(parts):
            at = chunk_of(ring_chunk(place_ref[0], i, parts), depth)
            total = total + dot(att_refs[i][...], ow_ref[j, at, :])
        hidden_ref[:, cols] = total
    hidden = hidden_ref[...]
    normed = (hidden * inverse_rms(hidden) * gain_ref[...]).astype(BF16)
    normed_ref[...] = normed
    gates_ref[...] = softmax_gates(dot(normed, router_ref[...]), mask_ref[...])


def mid_back_kernel(
    place_ref, hidden_ref, dy_ref, gates_ref, normed_ref, router_ref, gain_ref, ow_ref, *refs
):
    hg_ref, ag_ref, owg_ref, fg_ref, rg_ref, aog_s = refs[-6:]
    att_refs = refs[: ow_ref.shape[0]]
    nb_refs = refs[ow_ref.shape[0] : -6]
    gates = gates_ref[...]
    width_all = hidden_ref.shape[1]
    nb = sum(ref[...].astype(F32) for ref in nb_refs)
    mix = nb[:, width_all:]
    mix = mix + pltpu.roll(mix, LANES - MIX_LOW, 1)
    lg = gates * (mix - jnp.sum(gates * mix, axis=-1, keepdims=True))
    high, low = split_hi_lo(lg)
    normed = normed_ref[...]
    rg_ref[...] = dot_tn(high, normed) + dot_tn(low, normed)
    router = router_ref[...]
    ng = nb[:, :width_all] + dot_nt(high, router) + dot_nt(low, router)
    hidden = hidden_ref[...]
    inv = inverse_rms(hidden)
    scaled = hidden * inv
    fg_ref[...] = jnp.sum(ng * scaled, axis=0, keepdims=True)
    w = ng * gain_ref[...]
    hg = dy_ref[...].astype(F32) + inv * (w - scaled * jnp.mean(w * scaled, axis=-1, keepdims=True))
    hg_ref[...] = hg
    aog_s[...] = hg.astype(BF16)
    parts, width = ow_ref.shape[0], ow_ref.shape[2]
    depth = att_refs[0].shape[1]
    for i in range(parts):
        rows = chunk_of(ring_chunk(place_ref[0], i, parts), depth)
        total = None
        for j in range(parts):
            chunk = ring_chunk(place_ref[0], j, parts)
            part = dot_nt(aog_s[:, chunk_of(chunk, width)], ow_ref[j, rows, :])
            total = part if total is None else total + part
        ag_ref[i] = total.astype(BF16)
        for j in range(parts):
            owg_ref[j, rows, :] = dot_tn(att_refs[i][...], aog_s[:, j * width : (j + 1) * width]).astype(BF16)


def expert_kernel(parts, e, place_ref, n2_ref, dyx_ref, router_ref, w_ref, *refs):
    previous = refs[:2] if e else ()
    moe_ref, nb_ref, g_ref, inner_ref, gg_ref, ug_ref, wg_s, wu_s, wd_s, sems = refs[len(previous) :]
    width, ff = wg_s.shape
    slab, ff_slab = width // parts, ff // parts

    @pl.when(pl.program_id(0) == 0)
    def load():
        copies = []

        def move(start, count, target):
            copies.append(pltpu.make_async_copy(w_ref.at[start : start + count, :], target, sems.at[len(copies)]))

        for k in range(parts):
            start = k * 3 * slab
            move(start, slab, wg_s.at[k * slab : (k + 1) * slab, :])
            move(start + slab, slab, wu_s.at[k * slab : (k + 1) * slab, :])
            for c in range(width // ff):
                at = start + 2 * slab + c * ff_slab
                move(at, ff_slab, wd_s.at[k * ff_slab : (k + 1) * ff_slab, c * ff : (c + 1) * ff])
        for copy in copies:
            copy.start()
        for copy in copies:
            copy.wait()

    x = n2_ref[...]
    dy = dyx_ref[:, :width].astype(F32)
    gates = softmax_gates(dot(x, router_ref[...]), dyx_ref[:, width:].astype(F32))
    lane = lax.broadcasted_iota(jnp.int32, gates.shape, 1)
    at = place_ref[1] + e
    g = jnp.sum(jnp.where(lane == at, gates, 0.0), axis=-1, keepdims=True)
    ga = dot(x, wg_s[...])
    ua = dot(x, wu_s[...])
    sg = jax.nn.sigmoid(ga)
    act = ga * sg
    inner = (act * ua).astype(BF16)
    inner_ref[...] = inner
    eo = dot(inner, wd_s[...]).astype(BF16).astype(F32)
    moe = g * eo
    high, low = split_hi_lo(jnp.sum(dy * eo, axis=-1, keepdims=True))
    mix = jnp.where(lane == at, high.astype(F32), 0.0) + jnp.where(lane == MIX_LOW + at, low.astype(F32), 0.0)
    g_ref[...] = jnp.where(lane == 0, g, 0.0)
    ig = dot_nt((g * dy).astype(BF16), wd_s[...])
    gg = (ig * ua * sg * (1.0 + ga * (1.0 - sg))).astype(BF16)
    ug = (ig * act).astype(BF16)
    gg_ref[...] = gg
    ug_ref[...] = ug
    nb = dot_nt(gg, wg_s[...]) + dot_nt(ug, wu_s[...])
    if e:
        moe = moe + previous[0][...].astype(F32)
        nb = nb + previous[1][:, :width].astype(F32)
        mix = mix + previous[1][:, width:].astype(F32)
    moe_ref[...] = moe.astype(BF16)
    nb_ref[:, :width] = nb.astype(BF16)
    nb_ref[:, width:] = mix.astype(BF16)


def expert_grad_kernel(parts, half, *refs):
    halves = (refs[:6], refs[6:12])
    out_ref, g_s, u_s, d_s = refs[12:]
    step = pl.program_id(0)
    width, ff = g_s.shape
    slab, ff_slab = width // parts, ff // parts

    @pl.when(step == 0)
    def clear():
        g_s[...] = jnp.zeros_like(g_s)
        u_s[...] = jnp.zeros_like(u_s)
        d_s[...] = jnp.zeros_like(d_s)

    def add(n2_ref, dyx_ref, g_ref, inner_ref, gg_ref, ug_ref):
        x = n2_ref[...]
        g = jnp.sum(g_ref[...], axis=-1, keepdims=True)
        og = (g * dyx_ref[:, :width].astype(F32)).astype(BF16)
        g_s[...] += dot_tn(x, gg_ref[...])
        u_s[...] += dot_tn(x, ug_ref[...])
        d_s[...] += dot_tn(inner_ref[...], og)

    pl.when(step < half)(lambda: add(*halves[0]))
    pl.when(step >= half)(lambda: add(*halves[1]))

    @pl.when(step == pl.num_programs(0) - 1)
    def store():
        for k in range(parts):
            start = k * 3 * slab
            out_ref[start : start + slab, :] = g_s[k * slab : (k + 1) * slab, :].astype(BF16)
            out_ref[start + slab : start + 2 * slab, :] = u_s[k * slab : (k + 1) * slab, :].astype(BF16)
            for c in range(width // ff):
                at = start + 2 * slab + c * ff_slab
                out_ref[at : at + ff_slab, :] = d_s[k * ff_slab : (k + 1) * ff_slab, c * ff : (c + 1) * ff].astype(BF16)


def share_kernel(count, place_ref, *refs):
    gate_ref, up_ref, down_ref = refs[-3:]
    _, _, slab, ff = gate_ref.shape
    ff_slab, width = down_ref.shape[2:]
    for i in range(count):

        @pl.when(pl.program_id(0) == i)
        def copy(piece_ref=refs[i]):
            gate_ref[0, 0] = piece_ref[:slab, :].astype(F32)
            up_ref[0, 0] = piece_ref[slab : 2 * slab, :].astype(F32)
            for c in range(width // ff):
                at = 2 * slab + c * ff_slab
                down_ref[0, 0, :, c * ff : (c + 1) * ff] = piece_ref[at : at + ff_slab, :].astype(F32)


def sds(shape, dtype):
    return jax.ShapeDtypeStruct(shape, dtype)


def params():
    return pltpu.CompilerParams(vmem_limit_bytes=VMEM_LIMIT)


def cost(flops, traffic):
    return pl.CostEstimate(flops=int(flops * SCALE), bytes_accessed=int(traffic * SCALE), transcendentals=0)


def per_device(
    hi, yx, n, tokens, cotangent, segment_ids, routes, attn_gain, query_weight, key_matrix, value_weight,
    out_weight, ffn_gain, router_weight, gate_weight, up_weight, down_weight,
):
    rows, width = tokens.shape
    seq = rows * n
    experts = gate_weight.shape[0]
    ep = yx * 2
    own = experts // ep
    heads, kv_heads = QUERY_HEADS // n, KEY_VALUE_HEADS // n
    qw, kw = heads * HEAD, kv_heads * HEAD
    cols = qw + 2 * kw
    slab = width // n
    ff = gate_weight.shape[2]
    z = lax.axis_index("shard").astype(jnp.int32)
    core = lax.axis_index("cr").astype(jnp.int32)
    chip = lax.axis_index("yx").astype(jnp.int32)
    r = chip * 2 + core
    place = jnp.stack([z, r * own, chip, core])
    smem = pl.BlockSpec(memory_space=pltpu.SMEM)
    vmem = pl.BlockSpec(memory_space=pltpu.VMEM)
    hbm = pl.BlockSpec(memory_space=pl.ANY)

    def shift(value, k=1):
        return lax.ppermute(value, "shard", [(i, (i + k) % n) for i in range(n)])

    def swap(value):
        return lax.ppermute(value, "cr", [(0, 1), (1, 0)])

    def flip(value, j):
        return lax.ppermute(value, "yx", [(i, i ^ j) for i in range(yx)])

    def pick(value, index, axis):
        return lax.dynamic_index_in_dim(value, index, axis, keepdims=False)

    def absolute(parts):
        stacked = jnp.stack(parts)
        return jnp.stack([pick(stacked, lax.rem(z - j + n, n), 0) for j in range(n)])

    def plus(one, other):
        return (one.astype(F32) + other.astype(F32)).astype(BF16)

    def around(value):
        return across_too(value, flip(value, 1), flip(value, 2))

    def across_too(value, by_x, by_y):
        half = value.shape[0] // 2
        across = jnp.concatenate([flip(by_x[:half], 2), flip(by_y[half:], 1)], axis=0)
        return [value, by_x, by_y, across]

    def plane_sum(blocks):
        half = blocks[0].shape[0] // 2
        low, high = flip(blocks[3][:half], 1), flip(blocks[3][half:], 2)
        to_y = jnp.concatenate([plus(blocks[2][:half], low), blocks[2][half:]], axis=0)
        to_x = jnp.concatenate([blocks[1][:half], plus(blocks[1][half:], high)], axis=0)
        return [blocks[0], flip(to_x, 1), flip(to_y, 2)]

    x_all = lax.all_gather(tokens, "shard", axis=0, tiled=True)

    pack = jnp.concatenate(
        [attn_gain[None], ffn_gain[None], segment_ids.astype(BF16)[None], router_weight.T], axis=0
    )
    pack_rows = 16
    pack = jnp.pad(pack, ((0, 2 * pack_rows - pack.shape[0]), (0, 0)))
    pack = jnp.concatenate([pack[:pack_rows], pack[pack_rows:]], axis=1)
    part_rows = slab // ep
    by_dest = jnp.concatenate(
        [
            lax.dynamic_slice_in_dim(w, r * part_rows, part_rows, axis=0).reshape(part_rows, n, -1)
            for w in (query_weight, key_matrix, value_weight)
        ],
        axis=2,
    )
    ow_rows = out_weight.shape[0] // ep
    fold = cols // slab
    ow_mine = lax.dynamic_slice_in_dim(out_weight, r * ow_rows, ow_rows, axis=0)
    ow_mine = ow_mine.reshape(fold, ow_rows // fold, slab).transpose(1, 0, 2).reshape(ow_rows // fold, cols)

    def piece(k):
        return jnp.concatenate([pick(by_dest, lax.rem(z + k, n), 1), ow_mine, pack], axis=0)

    dense_mine = [piece(0)] + [shift(piece(k), k) for k in range(1, n)]
    ids = jnp.arange(experts, dtype=jnp.int32)
    routed = jnp.any(routes[:, :, None] == ids[None, None, :], axis=1)
    mask_own = jnp.pad(routed.astype(F32), ((0, 0), (0, LANES - experts)))
    dyx_mine = around(jnp.concatenate([cotangent, mask_own.astype(BF16)], axis=1))

    folds = width // ff
    packed = []
    for e in range(own):
        gate, up, down = (pick(w, r * own + e, 0) for w in (gate_weight, up_weight, down_weight))
        down = [down[:, c * ff : (c + 1) * ff] for c in range(folds)]
        packed.append(jnp.concatenate([gate, up] + down, axis=0))
    packed, dense_mine = lax.optimization_barrier((packed, dense_mine))
    weights = [lax.all_gather(w, "shard", axis=0, tiled=True) for w in packed]

    packs = absolute([p[-pack_rows:] for p in dense_mine])
    packs = jnp.concatenate([packs[:, :, :slab], packs[:, :, slab : 2 * slab]], axis=1)
    dense_mine = jnp.stack(around(jnp.stack([p[:-pack_rows] for p in dense_mine])))
    dense_mate = swap(dense_mine)
    gain1 = packs[:, 0, :].reshape(1, width).astype(F32)
    gain2 = packs[:, 1, :].reshape(1, width).astype(F32)
    segments = packs[:, 2, :].reshape(seq).astype(F32)
    seg_col, seg_row = segments[:, None], segments[None, :]
    router = jnp.pad(packs[:, 3 : 3 + experts, :].transpose(0, 2, 1).reshape(width, experts), ((0, 0), (0, LANES - experts)))


    positions = jnp.arange(seq, dtype=jnp.int32).astype(F32)
    frequency = ROPE_BASE ** (-jnp.arange(HEAD // 2, dtype=F32) / (HEAD // 2))
    angles = positions[:, None] * frequency[None, :]
    cosine, sine = jnp.cos(angles), jnp.sin(angles)
    cosine = jnp.concatenate([cosine] * 4, axis=1)
    sine = jnp.concatenate([-sine, sine] * 2, axis=1)

    x_all, dyx_mine = lax.optimization_barrier((x_all, dyx_mine))
    dyx_mine = jnp.concatenate(dyx_mine, axis=0)
    dyx_mate = swap(dyx_mine)
    w_qkv, normed, q, k, v, att, lse = pl.pallas_call(
        functools.partial(front_kernel, rows, heads, kv_heads),
        in_specs=[smem] + [vmem] * 8,
        out_shape=(
            sds((width, cols), BF16),
            sds((seq, width), BF16),
            sds((heads, seq, HEAD), BF16),
            sds((kv_heads, seq, HEAD), BF16),
            sds((kv_heads, seq, HEAD), BF16),
            sds((n, rows, qw), BF16),
            sds((heads, seq, 1), F32),
        ),
        scratch_shapes=[pltpu.VMEM((heads, seq, HEAD), F32)],
        compiler_params=params(),
        cost_estimate=cost(2 * seq * width * cols, 60e6),
        name="front",
    )(place, x_all, gain1, dense_mine, dense_mate, cosine, sine, seg_col, seg_row)

    att = [att[0]] + [shift(att[k], k) for k in range(1, n)]
    hidden, normed2, gates_own, ow = pl.pallas_call(
        mid_kernel,
        in_specs=[smem] + [vmem] * (6 + n),
        out_shape=(
            sds((rows, width), F32),
            sds((rows, width), BF16),
            sds((rows, LANES), F32),
            sds((n, ep * ow_rows, slab), BF16),
        ),
        compiler_params=params(),
        cost_estimate=cost(2 * rows * width * width, 14e6),
        name="mid",
    )(place, tokens, dense_mine, dense_mate, gain2, router, mask_own, *att)

    n2_mine = jnp.concatenate(around(normed2), axis=0)
    n2_mate = swap(n2_mine)

    total = yx * rows
    block = min(512, total)
    steps = total // block

    def by_block(size):
        return pl.BlockSpec((block, size), lambda i: (i, 0))

    def run_expert(e, n2, dyx, previous):
        return pl.pallas_call(
            functools.partial(expert_kernel, n, e),
            grid=(steps,),
            in_specs=[
                smem,
                by_block(width),
                by_block(width + LANES),
                pl.BlockSpec((width, LANES), lambda i: (0, 0)),
                hbm,
            ]
            + ([by_block(width), by_block(width + LANES)] if e else []),
            out_specs=(
                by_block(width),
                by_block(width + LANES),
                by_block(LANES),
                by_block(ff),
                by_block(ff),
                by_block(ff),
            ),
            out_shape=(
                sds((total, width), BF16),
                sds((total, width + LANES), BF16),
                sds((total, LANES), F32),
                sds((total, ff), BF16),
                sds((total, ff), BF16),
                sds((total, ff), BF16),
            ),
            scratch_shapes=[
                pltpu.VMEM((width, ff), BF16),
                pltpu.VMEM((width, ff), BF16),
                pltpu.VMEM((ff, width), BF16),
                pltpu.SemaphoreType.DMA(((2 + folds) * n,)),
            ],
            compiler_params=params(),
            cost_estimate=cost(12 * total * width * ff, 36e6),
            name="expert",
        )(place, n2, dyx, router, weights[e], *previous)

    def half_specs(at):
        sizes = (width, width + LANES, LANES, ff, ff, ff)
        return [pl.BlockSpec((block, size), lambda i: (at(i), 0)) for size in sizes]

    def weight_grads(mate, mine):
        return pl.pallas_call(
            functools.partial(expert_grad_kernel, n, steps),
            grid=(2 * steps,),
            in_specs=half_specs(lambda i: jnp.minimum(i, steps - 1))
            + half_specs(lambda i: jnp.maximum(i - steps, 0)),
            out_specs=pl.BlockSpec((3 * width, ff), lambda i: (0, 0)),
            out_shape=sds((3 * width, ff), BF16),
            scratch_shapes=[
                pltpu.VMEM((width, ff), F32),
                pltpu.VMEM((width, ff), F32),
                pltpu.VMEM((ff, width), F32),
            ],
            compiler_params=params(),
            cost_estimate=cost(12 * total * width * ff, 40e6),
            name="expert_grads",
        )(n2_mate, dyx_mate, *mate, n2_mine, dyx_mine, *mine)

    def spread(value):
        return [value[j * rows : (j + 1) * rows] for j in range(yx)]

    previous_mate = previous_mine = ()
    owned = []
    for e in range(own):
        *previous_mate, g_mate, in_mate, gg_mate, ug_mate = run_expert(e, n2_mate, dyx_mate, previous_mate)
        if e == own - 1:
            moe_got, nb_got = swap(previous_mate[0]), swap(previous_mate[1])
        *previous_mine, g_mine, in_mine, gg_mine, ug_mine = run_expert(e, n2_mine, dyx_mine, previous_mine)
        grads = weight_grads((g_mate, in_mate, gg_mate, ug_mate), (g_mine, in_mine, gg_mine, ug_mine))
        if e < own - 1:
            grads, weights[e + 1] = lax.optimization_barrier((grads, weights[e + 1]))
        else:
            nb_parts = spread(plus(previous_mine[1], nb_got))
            nb_parts = [nb_parts[0]] + [flip(nb_parts[j], j) for j in range(1, yx)]
            moe_sum = plus(previous_mine[0], moe_got)
            nb_parts, moe_sum, grads, owned = lax.optimization_barrier((nb_parts, moe_sum, grads, owned))
        grads = lax.psum_scatter(grads, "shard", scatter_dimension=0, tiled=True)
        if hi > 1:
            grads = lax.psum(grads.astype(F32), "hi").astype(BF16)
        owned.append(grads)

    hidden_grad, att_grad, ow_grad, ffn_grad, router_grad = pl.pallas_call(
        mid_back_kernel,
        in_specs=[smem] + [vmem] * (7 + n + yx),
        out_shape=(
            sds((rows, width), F32),
            sds((n, rows, qw), BF16),
            sds((n, n * qw, slab), BF16),
            sds((1, width), F32),
            sds((LANES, width), F32),
        ),
        scratch_shapes=[pltpu.VMEM((rows, width), BF16)],
        compiler_params=params(),
        cost_estimate=cost(4 * rows * width * width, 20e6),
        name="mid_back",
    )(place, hidden, cotangent, gates_own, normed2, router, gain2, ow, *att, *nb_parts)

    kvw = 2 * kw
    wide = max(slab, qw, kvw)
    small_rows = 16

    def widen(part):
        return jnp.pad(part, ((0, 0),) * 3 + ((0, wide - part.shape[3]),))

    def rows_of(small):
        small = jnp.pad(small, ((0, ep * small_rows - small.shape[0]), (0, 0)))
        return widen(small.reshape(ep, small_rows, n, slab).transpose(2, 0, 1, 3).astype(BF16))

    def dense_sum(pieces):
        dense = jnp.concatenate(pieces, axis=2)
        depth = dense.shape[2]
        dense = dense.reshape(n, yx, 2, depth, wide).transpose(2, 1, 0, 3, 4)
        dense = plus(pick(dense, core, 0), swap(pick(dense, 1 - core, 0)))
        parts = plane_sum([pick(dense, lax.bitwise_xor(chip, jnp.int32(j)), 0) for j in range(yx)])
        return sum(p.astype(F32) for p in parts).astype(BF16)

    att_grad = [att_grad[0]] + [shift(att_grad[k], n - k) for k in range(1, n)]
    early = (owned[0], flip(owned[0], 1), flip(owned[0], 2))
    att_grad, early = lax.optimization_barrier((att_grad, early))
    early = across_too(*early)
    small = rows_of(jnp.concatenate([ffn_grad, router_grad[:experts]], axis=0))
    dense_early = dense_sum([widen(ow_grad.reshape(n, ep, ow_rows, slab)), small])
    def share(e, mine, shared):
        pieces = [p for one in mine for p in (one, swap(one))]

        def out_index(j, place_ref):
            return (peer(place_ref, j % 2, j // 2), e, 0, 0)

        return pl.pallas_call(
            functools.partial(share_kernel, ep),
            grid_spec=pltpu.PrefetchScalarGridSpec(
                num_scalar_prefetch=1,
                grid=(ep,),
                in_specs=[pl.BlockSpec((3 * slab, ff), lambda j, place_ref: (0, 0))] * ep + [hbm] * len(shared),
                out_specs=(
                    pl.BlockSpec((1, 1, slab, ff), out_index),
                    pl.BlockSpec((1, 1, slab, ff), out_index),
                    pl.BlockSpec((1, 1, ff // n, width), out_index),
                ),
            ),
            out_shape=(
                sds((ep, own, slab, ff), F32),
                sds((ep, own, slab, ff), F32),
                sds((ep, own, ff // n, width), F32),
            ),
            input_output_aliases={1 + ep + i: i for i in range(len(shared))},
            compiler_params=params(),
            cost_estimate=cost(0, 20e6),
            name="share",
        )(place, *pieces, *shared)

    raw = pl.pallas_call(
        functools.partial(back_kernel, rows, heads, kv_heads),
        in_specs=[smem] + [vmem] * (6 + n),
        out_shape=sds((seq, cols), F32),
        scratch_shapes=[
            pltpu.VMEM((heads, seq, HEAD), BF16),
            pltpu.VMEM((heads, seq, HEAD), F32),
            pltpu.VMEM((kv_heads, seq, HEAD), F32),
            pltpu.VMEM((kv_heads, seq, HEAD), F32),
        ],
        compiler_params=params(),
        cost_estimate=cost(2 * seq * width * cols, 52e6),
        name="back",
    )(place, q, k, v, lse, seg_col, seg_row, *att_grad)
    raw, early, dense_early, owned = lax.optimization_barrier((raw, early, dense_early, owned))
    moe_parts = plane_sum(spread(moe_sum))
    shared = share(0, early, ())
    ng, qkv_grad, gain_grad = pl.pallas_call(
        functools.partial(finish_kernel, rows, qw + kw),
        out_shape=(sds((seq, width), BF16), sds((width, cols), BF16), sds((1, width), F32)),
        scratch_shapes=[pltpu.VMEM((seq, cols), BF16)],
        compiler_params=params(),
        cost_estimate=cost(4 * seq * width * cols, 30e6),
        name="finish",
    )(raw, x_all, normed, w_qkv, cosine, sine)
    qkv_rows = qkv_grad.reshape(n, ep, part_rows, cols)
    part = lax.psum_scatter(ng, "shard", scatter_dimension=0, tiled=True).astype(F32)
    last = [(value, flip(value, 1), flip(value, 2)) for value in owned[1:]]
    dense = dense_sum([rows_of(gain_grad), widen(qkv_rows[..., :qw]), widen(qkv_rows[..., qw:])])
    dense = jnp.concatenate([dense_early, dense], axis=1)
    if hi > 1:
        dense = lax.psum(dense.astype(F32), "hi").astype(BF16)
    dense, last, shared, moe_parts = lax.optimization_barrier((dense, last, shared, moe_parts))
    for e in range(1, own):
        shared = share(e, across_too(*last[e - 1]), shared)
    output = (hidden + sum(p.astype(F32) for p in moe_parts)).astype(BF16)


    dense = [pick(dense, z, 0)] + [shift(pick(dense, lax.rem(z + k, n), 0), k) for k in range(1, n)]
    part, dense, shared = lax.optimization_barrier((part, dense, shared))
    x = tokens.astype(F32)
    inv = inverse_rms(x)
    scaled = x * inv
    w1 = part * gain1
    input_grad = hidden_grad + inv * (w1 - scaled * jnp.mean(w1 * scaled, axis=-1, keepdims=True))

    cut = ow_rows + 2 * small_rows
    summed = sum(p[:cut].astype(F32) for p in dense).astype(BF16)
    kept = absolute([p[cut:] for p in dense]).reshape(n * 2 * part_rows, wide)
    mine = jnp.stack(around(jnp.concatenate([summed, kept], axis=0)))
    both = jnp.stack([mine, swap(mine)], axis=1).reshape((ep,) + mine.shape[1:])
    full = jnp.stack([pick(both, lax.bitwise_xor(r, jnp.int32(i)), 0) for i in range(ep)])
    ow_full = full[:, :ow_rows, :slab].reshape(-1, slab).astype(F32)
    small_full = full[:, ow_rows : ow_rows + small_rows, :slab].reshape(-1, slab).astype(F32)
    gain_full = full[0, ow_rows + small_rows, :slab].astype(F32)
    kept = full[:, cut:].reshape(ep, n, 2, part_rows, wide)

    gate_grad, up_grad, down_grad = (g.reshape((experts,) + g.shape[2:]) for g in shared)

    def columns(which, start, size):
        part = kept[:, :, which, :, start : start + size]
        return part.transpose(0, 2, 1, 3).reshape(slab, n * size).astype(F32)

    return (
        output,
        input_grad,
        gain_full,
        columns(0, 0, qw),
        columns(1, 0, kw),
        columns(1, kw, kw),
        ow_full,
        small_full[0],
        small_full[1 : 1 + experts].T,
        gate_grad,
        up_grad,
        down_grad,
    )


def solution(mesh):
    rep, n = mesh.shape["rep"], mesh.shape["shard"]
    yx = math.gcd(rep // 2, 4)
    hi = rep // (2 * yx)
    split = Mesh(mesh.devices.reshape(hi, yx, 2, n), ("hi", "yx", "cr", "shard"))
    rows = ("hi", "yx", "cr", "shard")
    placed = (
        P(rows, None),
        P(rows, None),
        P(rows),
        P(rows, None),
        P("shard"),
        P("shard", None),
        P("shard", None),
        P("shard", None),
        P(None, "shard"),
        P("shard"),
        P("shard", None),
        P(None, "shard", None),
        P(None, "shard", None),
        P(None, "shard", None),
    )
    return jax.shard_map(
        functools.partial(per_device, hi, yx, n),
        mesh=split,
        in_specs=placed,
        out_specs=(
            P(rows, None),
            P(rows, None),
            P("shard"),
            P("shard", None),
            P("shard", None),
            P("shard", None),
            P(None, "shard"),
            P("shard"),
            P("shard", None),
            P(None, "shard", None),
            P(None, "shard", None),
            P(None, "shard", None),
        ),
        check_vma=False,
    )
```

```python
import functools
import math

import jax
import jax.numpy as jnp
from jax import lax
from jax.experimental import pallas as pl
from jax.experimental.pallas import tpu as pltpu
from jax.sharding import Mesh
from jax.sharding import PartitionSpec as P

QUERY_HEADS = 16
KEY_VALUE_HEADS = 8
HEAD = 64
LANES = 128
MIX_LOW = 64
SCALE = 0.02

EPS = 1e-06
ROPE_BASE = 10000.0
MASKED = -1e30
F32 = jnp.float32
BF16 = jnp.bfloat16
NT = (((1,), (1,)), ((), ()))
TN = (((0,), (0,)), ((), ()))
VMEM_LIMIT = 60 * 1024 * 1024


def dot(a, b):
    return jnp.dot(a, b, preferred_element_type=F32)


def dot_nt(a, b):
    return lax.dot_general(a, b, NT, preferred_element_type=F32)


def dot_tn(a, b):
    return lax.dot_general(a, b, TN, preferred_element_type=F32)


def split_hi_lo(value):
    high = value.astype(BF16)
    return high, (value - high.astype(F32)).astype(BF16)


def inverse_rms(value):
    return lax.rsqrt(jnp.mean(value * value, axis=-1, keepdims=True) + EPS)


def swap_halves(value):
    width = value.shape[1]
    lane = lax.broadcasted_iota(jnp.int32, value.shape, 1)
    up = pltpu.roll(value, width - HEAD // 2, 1)
    down = pltpu.roll(value, HEAD // 2, 1)
    return jnp.where(lane % HEAD < HEAD // 2, up, down)


def rotate(value, cosine, sine):
    copies = value.shape[1] // LANES
    cosine = jnp.concatenate([cosine] * copies, axis=1)
    sine = jnp.concatenate([sine] * copies, axis=1)
    return value * cosine + swap_halves(value) * sine


def allowed_pairs(seg_col, seg_row, row0, count):
    rows = seg_col.shape[0]
    row = row0 + lax.broadcasted_iota(jnp.int32, (rows, count), 0)
    col = lax.broadcasted_iota(jnp.int32, (rows, count), 1)
    return (seg_col == seg_row) & (col <= row)


def ring_chunk(z, k, parts):
    return lax.rem(z - k + parts, parts)


def chunk_of(index, size):
    return pl.ds(pl.multiple_of(index * size, size), size)


def peer(place_ref, c, j):
    return lax.bitwise_xor(place_ref[2], jnp.int32(j)) * 2 + lax.bitwise_xor(place_ref[3], jnp.int32(c))


def front_kernel(
    block, heads, kv_heads, place_ref, x_ref, gain_ref, mine_ref, mate_ref, cos_ref, sin_ref, segc_ref, segr_ref,
    w_ref, normed_ref, q_ref, k_ref, v_ref, att_ref, lse_ref, out_s,
):
    seq = x_ref.shape[0]
    blocks = seq // block
    group = heads // kv_heads
    qw, kw = heads * HEAD, kv_heads * HEAD
    z = place_ref[0]
    slab = w_ref.shape[0] // blocks
    part = slab // (2 * mine_ref.shape[0])
    for c, piece_ref in enumerate((mine_ref, mate_ref)):
        for j in range(piece_ref.shape[0]):
            at = peer(place_ref, c, j) * part
            for i in range(blocks):
                start = pl.multiple_of(ring_chunk(z, i, blocks) * slab + at, part)
                w_ref[pl.ds(start, part), :] = piece_ref[j, i, :part, :]

    def project(i, carry):
        rows = pl.ds(pl.multiple_of(i * block, block), block)
        x = x_ref[rows, :].astype(F32)
        normed = (x * inverse_rms(x) * gain_ref[...]).astype(BF16)
        normed_ref[rows, :] = normed
        qkv = dot(normed, w_ref[...])
        turned = rotate(qkv[:, : qw + kw], cos_ref[rows, :], sin_ref[rows, :])
        for h in range(heads):
            q_ref[h, rows, :] = turned[:, h * HEAD : (h + 1) * HEAD].astype(BF16)
        for h in range(kv_heads):
            k_ref[h, rows, :] = turned[:, qw + h * HEAD : qw + (h + 1) * HEAD].astype(BF16)
            v_ref[h, rows, :] = qkv[:, qw + kw + h * HEAD : qw + kw + (h + 1) * HEAD].astype(BF16)
        return carry

    lax.fori_loop(0, blocks, project, 0)

    def one_head(h, carry):
        kv = h // group
        for i in range(blocks):
            count = (i + 1) * block
            rows = slice(i * block, (i + 1) * block)
            q = q_ref[h, rows, :] * jnp.asarray(0.125, BF16)
            k = k_ref[kv, :count, :]
            v = v_ref[kv, :count, :]
            allowed = allowed_pairs(segc_ref[rows, :], segr_ref[:, :count], i * block, count)
            s = jnp.where(allowed, dot_nt(q, k), MASKED)
            top = jnp.max(s, axis=-1, keepdims=True)
            e = jnp.exp(s - top)
            total = jnp.sum(e, axis=-1, keepdims=True)
            lse_ref[h, rows, :] = top + jnp.log(total)
            p = (e * (1.0 / total)).astype(BF16)
            out_s[h, rows, :] = dot(p, v)
        return carry

    lax.fori_loop(0, heads, one_head, 0)
    for i in range(blocks):
        k = lax.rem(i - z + blocks, blocks)
        for h in range(heads):
            att_ref[k, :, h * HEAD : (h + 1) * HEAD] = out_s[h, i * block : (i + 1) * block, :].astype(BF16)


def back_kernel(
    block, heads, kv_heads, q_ref, k_ref, v_ref, lse_ref, segc_ref, segr_ref, do_ref,
    raw_ref, do_s, dq_s, dk_s, dv_s,
):
    seq = q_ref.shape[1]
    blocks = seq // block
    group = heads // kv_heads
    qw, kw = heads * HEAD, kv_heads * HEAD
    for k in range(blocks):
        at = slice(k * block, (k + 1) * block)
        for h in range(heads):
            do_s[h, at, :] = do_ref[k, :, h * HEAD : (h + 1) * HEAD]
    dk_s[...] = jnp.zeros_like(dk_s)
    dv_s[...] = jnp.zeros_like(dv_s)

    def one_head(h, carry):
        kv = h // group
        for i in range(blocks):
            count = (i + 1) * block
            rows = slice(i * block, (i + 1) * block)
            q = q_ref[h, rows, :] * jnp.asarray(0.125, BF16)
            k = k_ref[kv, :count, :]
            v = v_ref[kv, :count, :]
            do = do_s[h, rows, :]
            allowed = allowed_pairs(segc_ref[rows, :], segr_ref[:, :count], i * block, count)
            s = jnp.where(allowed, dot_nt(q, k), MASKED)
            prob = jnp.exp(s - lse_ref[h, rows, :])
            grad = dot_nt(do, v)
            inner = jnp.sum(prob * grad, axis=-1, keepdims=True)
            ds = (prob * (grad - inner)).astype(BF16)
            dq_s[h, rows, :] = dot(ds, k) * 0.125
            dk_s[kv, :count, :] += dot_tn(ds, q)
            dv_s[kv, :count, :] += dot_tn(prob.astype(BF16), do)
        return carry

    lax.fori_loop(0, heads, one_head, 0)
    for h in range(heads):
        raw_ref[:, h * HEAD : (h + 1) * HEAD] = dq_s[h]
    for h in range(kv_heads):
        raw_ref[:, qw + h * HEAD : qw + (h + 1) * HEAD] = dk_s[h]
        raw_ref[:, qw + kw + h * HEAD : qw + kw + (h + 1) * HEAD] = dv_s[h]


def finish_kernel(
    block, turned, raw_ref, x_ref, normed_ref, w_ref, cos_ref, sin_ref, ng_ref, dw_ref, gain_ref, g_s,
):
    seq = x_ref.shape[0]
    blocks = seq // block
    gain_ref[...] = jnp.zeros_like(gain_ref)

    def finish(i, carry):
        rows = pl.ds(pl.multiple_of(i * block, block), block)
        g_s[rows, :turned] = rotate(raw_ref[rows, :turned], cos_ref[rows, :], -sin_ref[rows, :]).astype(BF16)
        g_s[rows, turned:] = raw_ref[rows, turned:].astype(BF16)
        ng = dot_nt(g_s[rows, :], w_ref[...])
        x = x_ref[rows, :].astype(F32)
        gain_ref[...] += jnp.sum(ng * (x * inverse_rms(x)), axis=0, keepdims=True)
        ng_ref[rows, :] = ng.astype(BF16)
        return carry

    lax.fori_loop(0, blocks, finish, 0)
    width = normed_ref.shape[1]
    for c in range(0, width, 256):
        dw_ref[c : c + 256, :] = dot_tn(normed_ref[:, c : c + 256], g_s[...]).astype(BF16)


def softmax_gates(logits, mask):
    shown = jnp.where(mask > 0.0, logits, MASKED)
    e = jnp.where(mask > 0.0, jnp.exp(shown - jnp.max(shown, axis=-1, keepdims=True)), 0.0)
    return e * (1.0 / jnp.sum(e, axis=-1, keepdims=True))


def mid_kernel(
    place_ref, x_ref, mine_ref, mate_ref, gain_ref, router_ref, mask_ref, *refs
):
    hidden_ref, normed_ref, gates_ref, ow_ref = refs[-4:]
    att_refs = refs[:-4]
    parts, width = ow_ref.shape[0], ow_ref.shape[2]
    share = ow_ref.shape[1] // (2 * mine_ref.shape[0])
    fold = mine_ref.shape[3] // width
    lines = share // fold
    skip = ow_ref.shape[0] * width // (2 * parts * mine_ref.shape[0])
    for c, piece_ref in enumerate((mine_ref, mate_ref)):
        for j in range(piece_ref.shape[0]):
            at = peer(place_ref, c, j) * share
            for k in range(parts):
                for f in range(fold):
                    start = pl.multiple_of(at + f * lines, lines)
                    ow_ref[k, pl.ds(start, lines), :] = piece_ref[j, k, skip : skip + lines, f * width : (f + 1) * width]
    depth = att_refs[0].shape[1]
    for j in range(parts):
        cols = chunk_of(ring_chunk(place_ref[0], j, parts), width)
        total = x_ref[:, cols].astype(F32)
        for i in range(parts):
            at = chunk_of(ring_chunk(place_ref[0], i, parts), depth)
            total = total + dot(att_refs[i][...], ow_ref[j, at, :])
        hidden_ref[:, cols] = total
    hidden = hidden_ref[...]
    normed = (hidden * inverse_rms(hidden) * gain_ref[...]).astype(BF16)
    normed_ref[...] = normed
    gates_ref[...] = softmax_gates(dot(normed, router_ref[...]), mask_ref[...])


def mid_back_kernel(
    place_ref, hidden_ref, dy_ref, gates_ref, normed_ref, router_ref, gain_ref, ow_ref, *refs
):
    hg_ref, ag_ref, owg_ref, fg_ref, rg_ref, aog_s = refs[-6:]
    att_refs = refs[: ow_ref.shape[0]]
    nb_refs = refs[ow_ref.shape[0] : -6]
    gates = gates_ref[...]
    width_all = hidden_ref.shape[1]
    nb = sum(ref[...].astype(F32) for ref in nb_refs)
    mix = nb[:, width_all:]
    mix = mix + pltpu.roll(mix, LANES - MIX_LOW, 1)
    lg = gates * (mix - jnp.sum(gates * mix, axis=-1, keepdims=True))
    high, low = split_hi_lo(lg)
    normed = normed_ref[...]
    rg_ref[...] = dot_tn(high, normed) + dot_tn(low, normed)
    router = router_ref[...]
    ng = nb[:, :width_all] + dot_nt(high, router) + dot_nt(low, router)
    hidden = hidden_ref[...]
    inv = inverse_rms(hidden)
    scaled = hidden * inv
    fg_ref[...] = jnp.sum(ng * scaled, axis=0, keepdims=True)
    w = ng * gain_ref[...]
    hg = dy_ref[...].astype(F32) + inv * (w - scaled * jnp.mean(w * scaled, axis=-1, keepdims=True))
    hg_ref[...] = hg
    aog_s[...] = hg.astype(BF16)
    parts, width = ow_ref.shape[0], ow_ref.shape[2]
    depth = att_refs[0].shape[1]
    for i in range(parts):
        group = ring_chunk(place_ref[0], i, parts)
        rows = chunk_of(group, depth)
        total = None
        for j in range(parts):
            chunk = ring_chunk(place_ref[0], j, parts)
            part = dot_nt(aog_s[:, chunk_of(chunk, width)], ow_ref[j, rows, :])
            total = part if total is None else total + part
        ag_ref[group] = total.astype(BF16)
        for j in range(parts):
            owg_ref[j, rows, :] = dot_tn(att_refs[i][...], aog_s[:, j * width : (j + 1) * width]).astype(BF16)


def expert_kernel(parts, e, place_ref, n2_ref, dyx_ref, router_ref, w_ref, *refs):
    previous = refs[:2] if e else ()
    moe_ref, nb_ref, g_ref, inner_ref, gg_ref, ug_ref, wg_s, wu_s, wd_s, sems = refs[len(previous) :]
    width, ff = wg_s.shape
    slab, ff_slab = width // parts, ff // parts

    first_step = pl.program_id(0) == 0

    def move(start, count, target, sem):
        return pltpu.make_async_copy(w_ref.at[start : start + count, :], target, sems.at[sem])

    gate_copies, up_copies, down_copies = [], [], []
    for k in range(parts):
        start = k * 3 * slab
        rows = slice(k * slab, (k + 1) * slab)
        gate_copies.append(move(start, slab, wg_s.at[rows, :], k))
        up_copies.append(move(start + slab, slab, wu_s.at[rows, :], parts + k))
        for c in range(width // ff):
            at = start + 2 * slab + c * ff_slab
            target = wd_s.at[k * ff_slab : (k + 1) * ff_slab, c * ff : (c + 1) * ff]
            down_copies.append(move(at, ff_slab, target, (2 + c) * parts + k))

    @pl.when(first_step)
    def load():
        for copy in gate_copies + up_copies + down_copies:
            copy.start()

    def ready(copies):
        @pl.when(first_step)
        def wait():
            for copy in copies:
                copy.wait()

    x = n2_ref[...]
    dy = dyx_ref[:, :width].astype(F32)
    gates = softmax_gates(dot(x, router_ref[...]), dyx_ref[:, width:].astype(F32))
    lane = lax.broadcasted_iota(jnp.int32, gates.shape, 1)
    at = place_ref[1] + e
    g = jnp.sum(jnp.where(lane == at, gates, 0.0), axis=-1, keepdims=True)
    ready(gate_copies)
    ga = dot(x, wg_s[...])
    ready(up_copies)
    ua = dot(x, wu_s[...])
    sg = jax.nn.sigmoid(ga)
    act = ga * sg
    inner = (act * ua).astype(BF16)
    inner_ref[...] = inner
    ready(down_copies)
    eo = dot(inner, wd_s[...]).astype(BF16).astype(F32)
    moe = g * eo
    high, low = split_hi_lo(jnp.sum(dy * eo, axis=-1, keepdims=True))
    mix = jnp.where(lane == at, high.astype(F32), 0.0) + jnp.where(lane == MIX_LOW + at, low.astype(F32), 0.0)
    g_ref[...] = jnp.where(lane == 0, g, 0.0)
    ig = dot_nt((g * dy).astype(BF16), wd_s[...])
    gg = (ig * ua * sg * (1.0 + ga * (1.0 - sg))).astype(BF16)
    ug = (ig * act).astype(BF16)
    gg_ref[...] = gg
    ug_ref[...] = ug
    nb = dot_nt(gg, wg_s[...]) + dot_nt(ug, wu_s[...])
    if e:
        moe = moe + previous[0][...].astype(F32)
        nb = nb + previous[1][:, :width].astype(F32)
        mix = mix + previous[1][:, width:].astype(F32)
    moe_ref[...] = moe.astype(BF16)
    nb_ref[:, :width] = nb.astype(BF16)
    nb_ref[:, width:] = mix.astype(BF16)


def expert_grad_kernel(parts, half, *refs):
    halves = (refs[:6], refs[6:12])
    out_ref, g_s, u_s, d_s = refs[12:]
    step = pl.program_id(0)
    width, ff = g_s.shape
    slab, ff_slab = width // parts, ff // parts

    @pl.when(step == 0)
    def clear():
        g_s[...] = jnp.zeros_like(g_s)
        u_s[...] = jnp.zeros_like(u_s)
        d_s[...] = jnp.zeros_like(d_s)

    def add(n2_ref, dyx_ref, g_ref, inner_ref, gg_ref, ug_ref):
        x = n2_ref[...]
        g = jnp.sum(g_ref[...], axis=-1, keepdims=True)
        og = (g * dyx_ref[:, :width].astype(F32)).astype(BF16)
        g_s[...] += dot_tn(x, gg_ref[...])
        u_s[...] += dot_tn(x, ug_ref[...])
        d_s[...] += dot_tn(inner_ref[...], og)

    pl.when(step < half)(lambda: add(*halves[0]))
    pl.when(step >= half)(lambda: add(*halves[1]))

    @pl.when(step == pl.num_programs(0) - 1)
    def store():
        for k in range(parts):
            start = k * 3 * slab
            out_ref[start : start + slab, :] = g_s[k * slab : (k + 1) * slab, :].astype(BF16)
            out_ref[start + slab : start + 2 * slab, :] = u_s[k * slab : (k + 1) * slab, :].astype(BF16)
            for c in range(width // ff):
                at = start + 2 * slab + c * ff_slab
                out_ref[at : at + ff_slab, :] = d_s[k * ff_slab : (k + 1) * ff_slab, c * ff : (c + 1) * ff].astype(BF16)


def share_kernel(count, place_ref, *refs):
    gate_ref, up_ref, down_ref = refs[-3:]
    _, _, slab, ff = gate_ref.shape
    ff_slab, width = down_ref.shape[2:]
    for i in range(count):

        @pl.when(pl.program_id(0) == i)
        def copy(piece_ref=refs[i]):
            gate_ref[0, 0] = piece_ref[:slab, :].astype(F32)
            up_ref[0, 0] = piece_ref[slab : 2 * slab, :].astype(F32)
            for c in range(width // ff):
                at = 2 * slab + c * ff_slab
                down_ref[0, 0, :, c * ff : (c + 1) * ff] = piece_ref[at : at + ff_slab, :].astype(F32)


def sds(shape, dtype):
    return jax.ShapeDtypeStruct(shape, dtype)


def params():
    return pltpu.CompilerParams(vmem_limit_bytes=VMEM_LIMIT)


def cost(flops, traffic):
    return pl.CostEstimate(flops=int(flops * SCALE), bytes_accessed=int(traffic * SCALE), transcendentals=0)


def per_device(
    hi, yx, n, tokens, cotangent, segment_ids, routes, attn_gain, query_weight, key_matrix, value_weight,
    out_weight, ffn_gain, router_weight, gate_weight, up_weight, down_weight,
):
    rows, width = tokens.shape
    seq = rows * n
    experts = gate_weight.shape[0]
    ep = yx * 2
    own = experts // ep
    heads, kv_heads = QUERY_HEADS // n, KEY_VALUE_HEADS // n
    qw, kw = heads * HEAD, kv_heads * HEAD
    cols = qw + 2 * kw
    slab = width // n
    ff = gate_weight.shape[2]
    z = lax.axis_index("shard").astype(jnp.int32)
    core = lax.axis_index("cr").astype(jnp.int32)
    chip = lax.axis_index("yx").astype(jnp.int32)
    r = chip * 2 + core
    place = jnp.stack([z, r * own, chip, core])
    smem = pl.BlockSpec(memory_space=pltpu.SMEM)
    vmem = pl.BlockSpec(memory_space=pltpu.VMEM)
    hbm = pl.BlockSpec(memory_space=pl.ANY)

    def shift(value, k=1):
        return lax.ppermute(value, "shard", [(i, (i + k) % n) for i in range(n)])

    def swap(value):
        return lax.ppermute(value, "cr", [(0, 1), (1, 0)])

    def flip(value, j):
        return lax.ppermute(value, "yx", [(i, i ^ j) for i in range(yx)])

    def pick(value, index, axis):
        return lax.dynamic_index_in_dim(value, index, axis, keepdims=False)

    def absolute(parts):
        stacked = jnp.stack(parts)
        return jnp.stack([pick(stacked, lax.rem(z - j + n, n), 0) for j in range(n)])

    def plus(one, other):
        return (one.astype(F32) + other.astype(F32)).astype(BF16)

    def around(value):
        return across_too(value, flip(value, 1), flip(value, 2))

    def across_too(value, by_x, by_y):
        half = value.shape[0] // 2
        across = jnp.concatenate([flip(by_x[:half], 2), flip(by_y[half:], 1)], axis=0)
        return [value, by_x, by_y, across]

    def to_owners(blocks):
        return [blocks[0]] + [flip(blocks[j], j) for j in range(1, yx)]

    x_all = lax.all_gather(tokens, "shard", axis=0, tiled=True)

    pack = jnp.concatenate(
        [attn_gain[None], ffn_gain[None], segment_ids.astype(BF16)[None], router_weight.T], axis=0
    )
    pack_rows = 16
    pack = jnp.pad(pack, ((0, 2 * pack_rows - pack.shape[0]), (0, 0)))
    pack = jnp.concatenate([pack[:pack_rows], pack[pack_rows:]], axis=1)
    part_rows = slab // ep
    by_dest = jnp.concatenate(
        [
            lax.dynamic_slice_in_dim(w, r * part_rows, part_rows, axis=0).reshape(part_rows, n, -1)
            for w in (query_weight, key_matrix, value_weight)
        ],
        axis=2,
    )
    ow_rows = out_weight.shape[0] // ep
    fold = cols // slab
    ow_mine = lax.dynamic_slice_in_dim(out_weight, r * ow_rows, ow_rows, axis=0)
    ow_mine = ow_mine.reshape(fold, ow_rows // fold, slab).transpose(1, 0, 2).reshape(ow_rows // fold, cols)

    def piece(k):
        return jnp.concatenate([pick(by_dest, lax.rem(z + k, n), 1), ow_mine, pack], axis=0)

    dense_mine = [piece(0)] + [shift(piece(k), k) for k in range(1, n)]
    ids = jnp.arange(experts, dtype=jnp.int32)
    routed = jnp.any(routes[:, :, None] == ids[None, None, :], axis=1)
    mask_own = jnp.pad(routed.astype(F32), ((0, 0), (0, LANES - experts)))
    dyx_mine = around(jnp.concatenate([cotangent, mask_own.astype(BF16)], axis=1))

    folds = width // ff
    packed = []
    for e in range(own):
        gate, up, down = (pick(w, r * own + e, 0) for w in (gate_weight, up_weight, down_weight))
        down = [down[:, c * ff : (c + 1) * ff] for c in range(folds)]
        packed.append(jnp.concatenate([gate, up] + down, axis=0))
    packed, dense_mine = lax.optimization_barrier((packed, dense_mine))
    weights = [lax.all_gather(w, "shard", axis=0, tiled=True) for w in packed]

    packs = absolute([p[-pack_rows:] for p in dense_mine])
    packs = jnp.concatenate([packs[:, :, :slab], packs[:, :, slab : 2 * slab]], axis=1)
    dense_mine = jnp.stack(around(jnp.stack([p[:-pack_rows] for p in dense_mine])))
    dense_mate = swap(dense_mine)
    gain1 = packs[:, 0, :].reshape(1, width).astype(F32)
    gain2 = packs[:, 1, :].reshape(1, width).astype(F32)
    segments = packs[:, 2, :].reshape(seq).astype(F32)
    seg_col, seg_row = segments[:, None], segments[None, :]
    router = jnp.pad(packs[:, 3 : 3 + experts, :].transpose(0, 2, 1).reshape(width, experts), ((0, 0), (0, LANES - experts)))


    positions = jnp.arange(seq, dtype=jnp.int32).astype(F32)
    frequency = ROPE_BASE ** (-jnp.arange(HEAD // 2, dtype=F32) / (HEAD // 2))
    angles = positions[:, None] * frequency[None, :]
    cosine, sine = jnp.cos(angles), jnp.sin(angles)
    cosine = jnp.concatenate([cosine] * 4, axis=1)
    sine = jnp.concatenate([-sine, sine] * 2, axis=1)

    x_all, dyx_mine = lax.optimization_barrier((x_all, dyx_mine))
    dyx_mine = jnp.concatenate(dyx_mine, axis=0)
    dyx_mate = swap(dyx_mine)
    w_qkv, normed, q, k, v, att, lse = pl.pallas_call(
        functools.partial(front_kernel, rows, heads, kv_heads),
        in_specs=[smem] + [vmem] * 8,
        out_shape=(
            sds((width, cols), BF16),
            sds((seq, width), BF16),
            sds((heads, seq, HEAD), BF16),
            sds((kv_heads, seq, HEAD), BF16),
            sds((kv_heads, seq, HEAD), BF16),
            sds((n, rows, qw), BF16),
            sds((heads, seq, 1), F32),
        ),
        scratch_shapes=[pltpu.VMEM((heads, seq, HEAD), F32)],
        compiler_params=params(),
        cost_estimate=cost(2 * seq * width * cols, 60e6),
        name="front",
    )(place, x_all, gain1, dense_mine, dense_mate, cosine, sine, seg_col, seg_row)

    att = [att[0]] + [shift(att[k], k) for k in range(1, n)]
    hidden, normed2, gates_own, ow = pl.pallas_call(
        mid_kernel,
        in_specs=[smem] + [vmem] * (6 + n),
        out_shape=(
            sds((rows, width), F32),
            sds((rows, width), BF16),
            sds((rows, LANES), F32),
            sds((n, ep * ow_rows, slab), BF16),
        ),
        compiler_params=params(),
        cost_estimate=cost(2 * rows * width * width, 14e6),
        name="mid",
    )(place, tokens, dense_mine, dense_mate, gain2, router, mask_own, *att)

    n2_mine = jnp.concatenate(around(normed2), axis=0)
    n2_mate = swap(n2_mine)

    total = yx * rows
    block = min(512, total)
    steps = total // block

    def by_block(size):
        return pl.BlockSpec((block, size), lambda i: (i, 0))

    def run_expert(e, n2, dyx, previous):
        return pl.pallas_call(
            functools.partial(expert_kernel, n, e),
            grid=(steps,),
            in_specs=[
                smem,
                by_block(width),
                by_block(width + LANES),
                pl.BlockSpec((width, LANES), lambda i: (0, 0)),
                hbm,
            ]
            + ([by_block(width), by_block(width + LANES)] if e else []),
            out_specs=(
                by_block(width),
                by_block(width + LANES),
                by_block(LANES),
                by_block(ff),
                by_block(ff),
                by_block(ff),
            ),
            out_shape=(
                sds((total, width), BF16),
                sds((total, width + LANES), BF16),
                sds((total, LANES), F32),
                sds((total, ff), BF16),
                sds((total, ff), BF16),
                sds((total, ff), BF16),
            ),
            scratch_shapes=[
                pltpu.VMEM((width, ff), BF16),
                pltpu.VMEM((width, ff), BF16),
                pltpu.VMEM((ff, width), BF16),
                pltpu.SemaphoreType.DMA(((2 + folds) * n,)),
            ],
            compiler_params=params(),
            cost_estimate=cost(12 * total * width * ff, 36e6),
            name="expert",
        )(place, n2, dyx, router, weights[e], *previous)

    def half_specs(at):
        sizes = (width, width + LANES, LANES, ff, ff, ff)
        return [pl.BlockSpec((block, size), lambda i: (at(i), 0)) for size in sizes]

    def weight_grads(mate, mine):
        return pl.pallas_call(
            functools.partial(expert_grad_kernel, n, steps),
            grid=(2 * steps,),
            in_specs=half_specs(lambda i: jnp.minimum(i, steps - 1))
            + half_specs(lambda i: jnp.maximum(i - steps, 0)),
            out_specs=pl.BlockSpec((3 * width, ff), lambda i: (0, 0)),
            out_shape=sds((3 * width, ff), BF16),
            scratch_shapes=[
                pltpu.VMEM((width, ff), F32),
                pltpu.VMEM((width, ff), F32),
                pltpu.VMEM((ff, width), F32),
            ],
            compiler_params=params(),
            cost_estimate=cost(12 * total * width * ff, 40e6),
            name="expert_grads",
        )(n2_mate, dyx_mate, *mate, n2_mine, dyx_mine, *mine)

    def spread(value):
        return [value[j * rows : (j + 1) * rows] for j in range(yx)]

    previous_mate = previous_mine = ()
    owned = []
    for e in range(own):
        *previous_mate, g_mate, in_mate, gg_mate, ug_mate = run_expert(e, n2_mate, dyx_mate, previous_mate)
        if e == own - 1:
            moe_got, nb_got = swap(previous_mate[0]), swap(previous_mate[1])
        *previous_mine, g_mine, in_mine, gg_mine, ug_mine = run_expert(e, n2_mine, dyx_mine, previous_mine)
        grads = weight_grads((g_mate, in_mate, gg_mate, ug_mate), (g_mine, in_mine, gg_mine, ug_mine))
        if e < own - 1:
            grads, weights[e + 1] = lax.optimization_barrier((grads, weights[e + 1]))
        else:
            nb_parts = to_owners(spread(plus(previous_mine[1], nb_got)))
            moe_sum = plus(previous_mine[0], moe_got)
            nb_parts, moe_sum, grads, owned = lax.optimization_barrier((nb_parts, moe_sum, grads, owned))
        grads = lax.psum_scatter(grads, "shard", scatter_dimension=0, tiled=True)
        if hi > 1:
            grads = lax.psum(grads.astype(F32), "hi").astype(BF16)
        owned.append(grads)

    hidden_grad, att_grad, ow_grad, ffn_grad, router_grad = pl.pallas_call(
        mid_back_kernel,
        in_specs=[smem] + [vmem] * (7 + n + yx),
        out_shape=(
            sds((rows, width), F32),
            sds((n, rows, qw), BF16),
            sds((n, n * qw, slab), BF16),
            sds((1, width), F32),
            sds((LANES, width), F32),
        ),
        scratch_shapes=[pltpu.VMEM((rows, width), BF16)],
        compiler_params=params(),
        cost_estimate=cost(4 * rows * width * width, 20e6),
        name="mid_back",
    )(place, hidden, cotangent, gates_own, normed2, router, gain2, ow, *att, *nb_parts)

    kvw = 2 * kw
    wide = max(slab, qw, kvw)
    small_rows = 16

    def widen(part):
        return jnp.pad(part, ((0, 0),) * 3 + ((0, wide - part.shape[3]),))

    def rows_of(small):
        small = jnp.pad(small, ((0, ep * small_rows - small.shape[0]), (0, 0)))
        return widen(small.reshape(ep, small_rows, n, slab).transpose(2, 0, 1, 3).astype(BF16))

    def dense_sum(pieces):
        dense = jnp.concatenate(pieces, axis=2)
        depth = dense.shape[2]
        dense = dense.reshape(n, yx, 2, depth, wide).transpose(2, 1, 0, 3, 4)
        dense = plus(pick(dense, core, 0), swap(pick(dense, 1 - core, 0)))
        parts = to_owners([pick(dense, lax.bitwise_xor(chip, jnp.int32(j)), 0) for j in range(yx)])
        return sum(p.astype(F32) for p in parts).astype(BF16)

    att_grad = lax.all_to_all(att_grad, "shard", 0, 0)
    early = (owned[0], flip(owned[0], 1), flip(owned[0], 2))
    moe_parts = to_owners(spread(moe_sum))
    att_grad, early, moe_parts = lax.optimization_barrier((att_grad, early, moe_parts))
    early = across_too(*early)
    small = rows_of(jnp.concatenate([ffn_grad, router_grad[:experts]], axis=0))
    dense_early = dense_sum([widen(ow_grad.reshape(n, ep, ow_rows, slab)), small])
    def share(e, mine, shared):
        pieces = [p for one in mine for p in (one, swap(one))]

        def out_index(j, place_ref):
            return (peer(place_ref, j % 2, j // 2), e, 0, 0)

        return pl.pallas_call(
            functools.partial(share_kernel, ep),
            grid_spec=pltpu.PrefetchScalarGridSpec(
                num_scalar_prefetch=1,
                grid=(ep,),
                in_specs=[pl.BlockSpec((3 * slab, ff), lambda j, place_ref: (0, 0))] * ep + [hbm] * len(shared),
                out_specs=(
                    pl.BlockSpec((1, 1, slab, ff), out_index),
                    pl.BlockSpec((1, 1, slab, ff), out_index),
                    pl.BlockSpec((1, 1, ff // n, width), out_index),
                ),
            ),
            out_shape=(
                sds((ep, own, slab, ff), F32),
                sds((ep, own, slab, ff), F32),
                sds((ep, own, ff // n, width), F32),
            ),
            input_output_aliases={1 + ep + i: i for i in range(len(shared))},
            compiler_params=params(),
            cost_estimate=cost(0, 20e6),
            name="share",
        )(place, *pieces, *shared)

    raw = pl.pallas_call(
        functools.partial(back_kernel, rows, heads, kv_heads),
        out_shape=sds((seq, cols), F32),
        scratch_shapes=[
            pltpu.VMEM((heads, seq, HEAD), BF16),
            pltpu.VMEM((heads, seq, HEAD), F32),
            pltpu.VMEM((kv_heads, seq, HEAD), F32),
            pltpu.VMEM((kv_heads, seq, HEAD), F32),
        ],
        compiler_params=params(),
        cost_estimate=cost(2 * seq * width * cols, 52e6),
        name="back",
    )(q, k, v, lse, seg_col, seg_row, att_grad)
    ng, qkv_grad, gain_grad = pl.pallas_call(
        functools.partial(finish_kernel, rows, qw + kw),
        out_shape=(sds((seq, width), BF16), sds((width, cols), BF16), sds((1, width), F32)),
        scratch_shapes=[pltpu.VMEM((seq, cols), BF16)],
        compiler_params=params(),
        cost_estimate=cost(4 * seq * width * cols, 30e6),
        name="finish",
    )(raw, x_all, normed, w_qkv, cosine, sine)
    qkv_rows = qkv_grad.reshape(n, ep, part_rows, cols)
    qkv_rows, gain_grad, owned, early, dense_early = lax.optimization_barrier(
        (qkv_rows, gain_grad, owned, early, dense_early)
    )
    shared = share(0, early, ())
    part = lax.psum_scatter(ng, "shard", scatter_dimension=0, tiled=True).astype(F32)
    last = [(value, flip(value, 1), flip(value, 2)) for value in owned[1:]]
    dense = dense_sum([rows_of(gain_grad), widen(qkv_rows[..., :qw]), widen(qkv_rows[..., qw:])])
    dense = jnp.concatenate([dense_early, dense], axis=1)
    if hi > 1:
        dense = lax.psum(dense.astype(F32), "hi").astype(BF16)
    dense, last, shared = lax.optimization_barrier((dense, last, shared))
    for e in range(1, own):
        shared = share(e, across_too(*last[e - 1]), shared)
    output = (hidden + sum(p.astype(F32) for p in moe_parts)).astype(BF16)


    dense = [pick(dense, z, 0)] + [shift(pick(dense, lax.rem(z + k, n), 0), k) for k in range(1, n)]
    part, dense, shared = lax.optimization_barrier((part, dense, shared))
    cut = ow_rows + 2 * small_rows
    summed = sum(p[:cut].astype(F32) for p in dense).astype(BF16)
    kept = absolute([p[cut:] for p in dense]).reshape(n * 2 * part_rows, wide)
    mine = jnp.concatenate([summed, kept], axis=0)
    mine = [mine] + [flip(mine, j) for j in range(1, yx)]
    mine = jnp.stack(mine)
    x = tokens.astype(F32)
    inv = inverse_rms(x)
    scaled = x * inv
    w1 = part * gain1
    input_grad = hidden_grad + inv * (w1 - scaled * jnp.mean(w1 * scaled, axis=-1, keepdims=True))

    both = jnp.stack([mine, swap(mine)], axis=1).reshape((ep,) + mine.shape[1:])
    full = jnp.stack([pick(both, lax.bitwise_xor(r, jnp.int32(i)), 0) for i in range(ep)])
    ow_full = full[:, :ow_rows, :slab].reshape(-1, slab).astype(F32)
    small_full = full[:, ow_rows : ow_rows + small_rows, :slab].reshape(-1, slab).astype(F32)
    gain_full = full[0, ow_rows + small_rows, :slab].astype(F32)
    kept = full[:, cut:].reshape(ep, n, 2, part_rows, wide)

    gate_grad, up_grad, down_grad = (g.reshape((experts,) + g.shape[2:]) for g in shared)

    def columns(which, start, size):
        part = kept[:, :, which, :, start : start + size]
        return part.transpose(0, 2, 1, 3).reshape(slab, n * size).astype(F32)

    return (
        output,
        input_grad,
        gain_full,
        columns(0, 0, qw),
        columns(1, 0, kw),
        columns(1, kw, kw),
        ow_full,
        small_full[0],
        small_full[1 : 1 + experts].T,
        gate_grad,
        up_grad,
        down_grad,
    )


def solution(mesh):
    rep, n = mesh.shape["rep"], mesh.shape["shard"]
    yx = math.gcd(rep // 2, 4)
    hi = rep // (2 * yx)
    split = Mesh(mesh.devices.reshape(hi, yx, 2, n), ("hi", "yx", "cr", "shard"))
    rows = ("hi", "yx", "cr", "shard")
    placed = (
        P(rows, None),
        P(rows, None),
        P(rows),
        P(rows, None),
        P("shard"),
        P("shard", None),
        P("shard", None),
        P("shard", None),
        P(None, "shard"),
        P("shard"),
        P("shard", None),
        P(None, "shard", None),
        P(None, "shard", None),
        P(None, "shard", None),
    )
    return jax.shard_map(
        functools.partial(per_device, hi, yx, n),
        mesh=split,
        in_specs=placed,
        out_specs=(
            P(rows, None),
            P(rows, None),
            P("shard"),
            P("shard", None),
            P("shard", None),
            P("shard", None),
            P(None, "shard"),
            P("shard"),
            P("shard", None),
            P(None, "shard", None),
            P(None, "shard", None),
            P(None, "shard", None),
        ),
        check_vma=False,
    )
```

```python
import functools
import math

import jax
import jax.numpy as jnp
from jax import lax
from jax.experimental import pallas as pl
from jax.experimental.pallas import tpu as pltpu
from jax.sharding import Mesh
from jax.sharding import PartitionSpec as P

QUERY_HEADS = 16
KEY_VALUE_HEADS = 8
HEAD = 64
LANES = 128
MIX_LOW = 64
SCALE = 0.02

EPS = 1e-06
ROPE_BASE = 10000.0
MASKED = -1e30
F32 = jnp.float32
BF16 = jnp.bfloat16
NT = (((1,), (1,)), ((), ()))
TN = (((0,), (0,)), ((), ()))
VMEM_LIMIT = 60 * 1024 * 1024


def dot(a, b):
    return jnp.dot(a, b, preferred_element_type=F32)


def dot_nt(a, b):
    return lax.dot_general(a, b, NT, preferred_element_type=F32)


def dot_tn(a, b):
    return lax.dot_general(a, b, TN, preferred_element_type=F32)


def split_hi_lo(value):
    high = value.astype(BF16)
    return high, (value - high.astype(F32)).astype(BF16)


def inverse_rms(value):
    return lax.rsqrt(jnp.mean(value * value, axis=-1, keepdims=True) + EPS)


def swap_halves(value):
    width = value.shape[1]
    lane = lax.broadcasted_iota(jnp.int32, value.shape, 1)
    up = pltpu.roll(value, width - HEAD // 2, 1)
    down = pltpu.roll(value, HEAD // 2, 1)
    return jnp.where(lane % HEAD < HEAD // 2, up, down)


def rotate(value, cosine, sine):
    copies = value.shape[1] // LANES
    cosine = jnp.concatenate([cosine] * copies, axis=1)
    sine = jnp.concatenate([sine] * copies, axis=1)
    return value * cosine + swap_halves(value) * sine


def allowed_pairs(seg_col, seg_row, row0, count):
    rows = seg_col.shape[0]
    row = row0 + lax.broadcasted_iota(jnp.int32, (rows, count), 0)
    col = lax.broadcasted_iota(jnp.int32, (rows, count), 1)
    return (seg_col == seg_row) & (col <= row)


def ring_chunk(z, k, parts):
    return lax.rem(z - k + parts, parts)


def chunk_of(index, size):
    return pl.ds(pl.multiple_of(index * size, size), size)


def peer(place_ref, c, j):
    return lax.bitwise_xor(place_ref[2], jnp.int32(j)) * 2 + lax.bitwise_xor(place_ref[3], jnp.int32(c))


def front_kernel(
    block, heads, kv_heads, place_ref, x_ref, gain_ref, mine_ref, mate_ref, cos_ref, sin_ref, segc_ref, segr_ref,
    w_ref, normed_ref, q_ref, k_ref, v_ref, att_ref, lse_ref, out_s,
):
    seq = x_ref.shape[0]
    blocks = seq // block
    group = heads // kv_heads
    qw, kw = heads * HEAD, kv_heads * HEAD
    z = place_ref[0]
    slab = w_ref.shape[0] // blocks
    part = slab // (2 * mine_ref.shape[0])
    for c, piece_ref in enumerate((mine_ref, mate_ref)):
        for j in range(piece_ref.shape[0]):
            at = peer(place_ref, c, j) * part
            for i in range(blocks):
                start = pl.multiple_of(ring_chunk(z, i, blocks) * slab + at, part)
                w_ref[pl.ds(start, part), :] = piece_ref[j, i, :part, :]

    def project(i, carry):
        rows = pl.ds(pl.multiple_of(i * block, block), block)
        x = x_ref[rows, :].astype(F32)
        normed = (x * inverse_rms(x) * gain_ref[...]).astype(BF16)
        normed_ref[rows, :] = normed
        qkv = dot(normed, w_ref[...])
        turned = rotate(qkv[:, : qw + kw], cos_ref[rows, :], sin_ref[rows, :])
        for h in range(heads):
            q_ref[h, rows, :] = turned[:, h * HEAD : (h + 1) * HEAD].astype(BF16)
        for h in range(kv_heads):
            k_ref[h, rows, :] = turned[:, qw + h * HEAD : qw + (h + 1) * HEAD].astype(BF16)
            v_ref[h, rows, :] = qkv[:, qw + kw + h * HEAD : qw + kw + (h + 1) * HEAD].astype(BF16)
        return carry

    lax.fori_loop(0, blocks, project, 0)

    def one_head(h, carry):
        kv = h // group
        for i in range(blocks):
            count = (i + 1) * block
            rows = slice(i * block, (i + 1) * block)
            q = q_ref[h, rows, :] * jnp.asarray(0.125, BF16)
            k = k_ref[kv, :count, :]
            v = v_ref[kv, :count, :]
            allowed = allowed_pairs(segc_ref[rows, :], segr_ref[:, :count], i * block, count)
            s = jnp.where(allowed, dot_nt(q, k), MASKED)
            top = jnp.max(s, axis=-1, keepdims=True)
            e = jnp.exp(s - top)
            total = jnp.sum(e, axis=-1, keepdims=True)
            lse_ref[h, rows, :] = top + jnp.log(total)
            p = (e * (1.0 / total)).astype(BF16)
            out_s[h, rows, :] = dot(p, v)
        return carry

    lax.fori_loop(0, heads, one_head, 0)
    for i in range(blocks):
        k = lax.rem(i - z + blocks, blocks)
        for h in range(heads):
            att_ref[k, :, h * HEAD : (h + 1) * HEAD] = out_s[h, i * block : (i + 1) * block, :].astype(BF16)


def back_kernel(
    block, heads, kv_heads, q_ref, k_ref, v_ref, lse_ref, segc_ref, segr_ref, do_ref,
    raw_ref, do_s, dq_s, dk_s, dv_s,
):
    seq = q_ref.shape[1]
    blocks = seq // block
    group = heads // kv_heads
    qw, kw = heads * HEAD, kv_heads * HEAD
    for k in range(blocks):
        at = slice(k * block, (k + 1) * block)
        for h in range(heads):
            do_s[h, at, :] = do_ref[k, :, h * HEAD : (h + 1) * HEAD]
    dk_s[...] = jnp.zeros_like(dk_s)
    dv_s[...] = jnp.zeros_like(dv_s)

    def one_head(h, carry):
        kv = h // group
        for i in range(blocks):
            count = (i + 1) * block
            rows = slice(i * block, (i + 1) * block)
            q = q_ref[h, rows, :] * jnp.asarray(0.125, BF16)
            k = k_ref[kv, :count, :]
            v = v_ref[kv, :count, :]
            do = do_s[h, rows, :]
            allowed = allowed_pairs(segc_ref[rows, :], segr_ref[:, :count], i * block, count)
            s = jnp.where(allowed, dot_nt(q, k), MASKED)
            prob = jnp.exp(s - lse_ref[h, rows, :])
            grad = dot_nt(do, v)
            inner = jnp.sum(prob * grad, axis=-1, keepdims=True)
            ds = (prob * (grad - inner)).astype(BF16)
            dq_s[h, rows, :] = dot(ds, k) * 0.125
            dk_s[kv, :count, :] += dot_tn(ds, q)
            dv_s[kv, :count, :] += dot_tn(prob.astype(BF16), do)
        return carry

    lax.fori_loop(0, heads, one_head, 0)
    for h in range(heads):
        raw_ref[:, h * HEAD : (h + 1) * HEAD] = dq_s[h]
    for h in range(kv_heads):
        raw_ref[:, qw + h * HEAD : qw + (h + 1) * HEAD] = dk_s[h]
        raw_ref[:, qw + kw + h * HEAD : qw + kw + (h + 1) * HEAD] = dv_s[h]


def finish_kernel(
    block, turned, raw_ref, x_ref, normed_ref, w_ref, cos_ref, sin_ref, ng_ref, dw_ref, gain_ref, g_s,
):
    seq = x_ref.shape[0]
    blocks = seq // block
    gain_ref[...] = jnp.zeros_like(gain_ref)

    def finish(i, carry):
        rows = pl.ds(pl.multiple_of(i * block, block), block)
        g_s[rows, :turned] = rotate(raw_ref[rows, :turned], cos_ref[rows, :], -sin_ref[rows, :]).astype(BF16)
        g_s[rows, turned:] = raw_ref[rows, turned:].astype(BF16)
        ng = dot_nt(g_s[rows, :], w_ref[...])
        x = x_ref[rows, :].astype(F32)
        gain_ref[...] += jnp.sum(ng * (x * inverse_rms(x)), axis=0, keepdims=True)
        ng_ref[rows, :] = ng.astype(BF16)
        return carry

    lax.fori_loop(0, blocks, finish, 0)
    width = normed_ref.shape[1]
    for c in range(0, width, 256):
        dw_ref[c : c + 256, :] = dot_tn(normed_ref[:, c : c + 256], g_s[...]).astype(BF16)


def softmax_gates(logits, mask):
    shown = jnp.where(mask > 0.0, logits, MASKED)
    e = jnp.where(mask > 0.0, jnp.exp(shown - jnp.max(shown, axis=-1, keepdims=True)), 0.0)
    return e * (1.0 / jnp.sum(e, axis=-1, keepdims=True))


def mid_kernel(
    place_ref, x_ref, mine_ref, mate_ref, gain_ref, router_ref, mask_ref, *refs
):
    hidden_ref, normed_ref, gates_ref, ow_ref = refs[-4:]
    att_refs = refs[:-4]
    parts, width = ow_ref.shape[0], ow_ref.shape[2]
    share = ow_ref.shape[1] // (2 * mine_ref.shape[0])
    fold = mine_ref.shape[3] // width
    lines = share // fold
    skip = ow_ref.shape[0] * width // (2 * parts * mine_ref.shape[0])
    for c, piece_ref in enumerate((mine_ref, mate_ref)):
        for j in range(piece_ref.shape[0]):
            at = peer(place_ref, c, j) * share
            for k in range(parts):
                for f in range(fold):
                    start = pl.multiple_of(at + f * lines, lines)
                    ow_ref[k, pl.ds(start, lines), :] = piece_ref[j, k, skip : skip + lines, f * width : (f + 1) * width]
    depth = att_refs[0].shape[1]
    for j in range(parts):
        cols = chunk_of(ring_chunk(place_ref[0], j, parts), width)
        total = x_ref[:, cols].astype(F32)
        for i in range(parts):
            at = chunk_of(ring_chunk(place_ref[0], i, parts), depth)
            total = total + dot(att_refs[i][...], ow_ref[j, at, :])
        hidden_ref[:, cols] = total
    hidden = hidden_ref[...]
    normed = (hidden * inverse_rms(hidden) * gain_ref[...]).astype(BF16)
    normed_ref[...] = normed
    gates_ref[...] = softmax_gates(dot(normed, router_ref[...]), mask_ref[...])


def mid_back_kernel(
    place_ref, hidden_ref, dy_ref, gates_ref, normed_ref, router_ref, gain_ref, ow_ref, *refs
):
    hg_ref, ag_ref, owg_ref, fg_ref, rg_ref, aog_s = refs[-6:]
    att_refs = refs[: ow_ref.shape[0]]
    nb_refs = refs[ow_ref.shape[0] : -6]
    gates = gates_ref[...]
    width_all = hidden_ref.shape[1]
    nb = sum(ref[...].astype(F32) for ref in nb_refs)
    mix = nb[:, width_all:]
    mix = mix + pltpu.roll(mix, LANES - MIX_LOW, 1)
    lg = gates * (mix - jnp.sum(gates * mix, axis=-1, keepdims=True))
    high, low = split_hi_lo(lg)
    normed = normed_ref[...]
    rg_ref[...] = dot_tn(high, normed) + dot_tn(low, normed)
    router = router_ref[...]
    ng = nb[:, :width_all] + dot_nt(high, router) + dot_nt(low, router)
    hidden = hidden_ref[...]
    inv = inverse_rms(hidden)
    scaled = hidden * inv
    fg_ref[...] = jnp.sum(ng * scaled, axis=0, keepdims=True)
    w = ng * gain_ref[...]
    hg = dy_ref[...].astype(F32) + inv * (w - scaled * jnp.mean(w * scaled, axis=-1, keepdims=True))
    hg_ref[...] = hg
    aog_s[...] = hg.astype(BF16)
    parts, width = ow_ref.shape[0], ow_ref.shape[2]
    depth = att_refs[0].shape[1]
    for i in range(parts):
        group = ring_chunk(place_ref[0], i, parts)
        rows = chunk_of(group, depth)
        total = None
        for j in range(parts):
            chunk = ring_chunk(place_ref[0], j, parts)
            part = dot_nt(aog_s[:, chunk_of(chunk, width)], ow_ref[j, rows, :])
            total = part if total is None else total + part
        ag_ref[group] = total.astype(BF16)
        for j in range(parts):
            owg_ref[j, rows, :] = dot_tn(att_refs[i][...], aog_s[:, j * width : (j + 1) * width]).astype(BF16)


def expert_kernel(parts, e, place_ref, n2_ref, dyx_ref, router_ref, w_ref, *refs):
    previous = refs[:2] if e else ()
    moe_ref, nb_ref, g_ref, inner_ref, gg_ref, ug_ref, wg_s, wu_s, wd_s, sems = refs[len(previous) :]
    width, ff = wg_s.shape
    slab, ff_slab = width // parts, ff // parts

    first_step = pl.program_id(0) == 0

    def move(start, count, target, sem):
        return pltpu.make_async_copy(w_ref.at[start : start + count, :], target, sems.at[sem])

    gate_copies, up_copies, down_copies = [], [], []
    for k in range(parts):
        start = k * 3 * slab
        rows = slice(k * slab, (k + 1) * slab)
        gate_copies.append(move(start, slab, wg_s.at[rows, :], k))
        up_copies.append(move(start + slab, slab, wu_s.at[rows, :], parts + k))
        for c in range(width // ff):
            at = start + 2 * slab + c * ff_slab
            target = wd_s.at[k * ff_slab : (k + 1) * ff_slab, c * ff : (c + 1) * ff]
            down_copies.append(move(at, ff_slab, target, (2 + c) * parts + k))

    @pl.when(first_step)
    def load():
        for copy in gate_copies + up_copies + down_copies:
            copy.start()

    def ready(copies):
        @pl.when(first_step)
        def wait():
            for copy in copies:
                copy.wait()

    x = n2_ref[...]
    dy = dyx_ref[:, :width].astype(F32)
    gates = softmax_gates(dot(x, router_ref[...]), dyx_ref[:, width:].astype(F32))
    lane = lax.broadcasted_iota(jnp.int32, gates.shape, 1)
    at = place_ref[1] + e
    g = jnp.sum(jnp.where(lane == at, gates, 0.0), axis=-1, keepdims=True)
    ready(gate_copies)
    ga = dot(x, wg_s[...])
    ready(up_copies)
    ua = dot(x, wu_s[...])
    sg = jax.nn.sigmoid(ga)
    act = ga * sg
    inner = (act * ua).astype(BF16)
    inner_ref[...] = inner
    ready(down_copies)
    eo = dot(inner, wd_s[...]).astype(BF16).astype(F32)
    moe = g * eo
    high, low = split_hi_lo(jnp.sum(dy * eo, axis=-1, keepdims=True))
    mix = jnp.where(lane == at, high.astype(F32), 0.0) + jnp.where(lane == MIX_LOW + at, low.astype(F32), 0.0)
    g_ref[...] = jnp.where(lane == 0, g, 0.0)
    ig = dot_nt((g * dy).astype(BF16), wd_s[...])
    gg = (ig * ua * sg * (1.0 + ga * (1.0 - sg))).astype(BF16)
    ug = (ig * act).astype(BF16)
    gg_ref[...] = gg
    ug_ref[...] = ug
    nb = dot_nt(gg, wg_s[...]) + dot_nt(ug, wu_s[...])
    if e:
        moe = moe + previous[0][...].astype(F32)
        nb = nb + previous[1][:, :width].astype(F32)
        mix = mix + previous[1][:, width:].astype(F32)
    moe_ref[...] = moe.astype(BF16)
    nb_ref[:, :width] = nb.astype(BF16)
    nb_ref[:, width:] = mix.astype(BF16)


def expert_grad_kernel(parts, half, *refs):
    halves = (refs[:6], refs[6:12])
    out_ref, g_s, u_s, d_s = refs[12:]
    step = pl.program_id(0)
    width, ff = g_s.shape
    slab, ff_slab = width // parts, ff // parts

    @pl.when(step == 0)
    def clear():
        g_s[...] = jnp.zeros_like(g_s)
        u_s[...] = jnp.zeros_like(u_s)
        d_s[...] = jnp.zeros_like(d_s)

    def add(n2_ref, dyx_ref, g_ref, inner_ref, gg_ref, ug_ref):
        x = n2_ref[...]
        g = jnp.sum(g_ref[...], axis=-1, keepdims=True)
        og = (g * dyx_ref[:, :width].astype(F32)).astype(BF16)
        g_s[...] += dot_tn(x, gg_ref[...])
        u_s[...] += dot_tn(x, ug_ref[...])
        d_s[...] += dot_tn(inner_ref[...], og)

    pl.when(step < half)(lambda: add(*halves[0]))
    pl.when(step >= half)(lambda: add(*halves[1]))

    @pl.when(step == pl.num_programs(0) - 1)
    def store():
        for k in range(parts):
            start = k * 3 * slab
            out_ref[start : start + slab, :] = g_s[k * slab : (k + 1) * slab, :].astype(BF16)
            out_ref[start + slab : start + 2 * slab, :] = u_s[k * slab : (k + 1) * slab, :].astype(BF16)
            for c in range(width // ff):
                at = start + 2 * slab + c * ff_slab
                out_ref[at : at + ff_slab, :] = d_s[k * ff_slab : (k + 1) * ff_slab, c * ff : (c + 1) * ff].astype(BF16)


def share_kernel(count, place_ref, *refs):
    gate_ref, up_ref, down_ref = refs[-3:]
    _, _, slab, ff = gate_ref.shape
    ff_slab, width = down_ref.shape[2:]
    for i in range(count):

        @pl.when(pl.program_id(0) == i)
        def copy(piece_ref=refs[i]):
            gate_ref[0, 0] = piece_ref[:slab, :].astype(F32)
            up_ref[0, 0] = piece_ref[slab : 2 * slab, :].astype(F32)
            for c in range(width // ff):
                at = 2 * slab + c * ff_slab
                down_ref[0, 0, :, c * ff : (c + 1) * ff] = piece_ref[at : at + ff_slab, :].astype(F32)


def sds(shape, dtype):
    return jax.ShapeDtypeStruct(shape, dtype)


def params():
    return pltpu.CompilerParams(vmem_limit_bytes=VMEM_LIMIT)


def cost(flops, traffic):
    return pl.CostEstimate(flops=int(flops * SCALE), bytes_accessed=int(traffic * SCALE), transcendentals=0)


def per_device(
    hi, yx, n, tokens, cotangent, segment_ids, routes, attn_gain, query_weight, key_matrix, value_weight,
    out_weight, ffn_gain, router_weight, gate_weight, up_weight, down_weight,
):
    rows, width = tokens.shape
    seq = rows * n
    experts = gate_weight.shape[0]
    ep = yx * 2
    own = experts // ep
    heads, kv_heads = QUERY_HEADS // n, KEY_VALUE_HEADS // n
    qw, kw = heads * HEAD, kv_heads * HEAD
    cols = qw + 2 * kw
    slab = width // n
    ff = gate_weight.shape[2]
    z = lax.axis_index("shard").astype(jnp.int32)
    core = lax.axis_index("cr").astype(jnp.int32)
    chip = lax.axis_index("yx").astype(jnp.int32)
    r = chip * 2 + core
    place = jnp.stack([z, r * own, chip, core])
    smem = pl.BlockSpec(memory_space=pltpu.SMEM)
    vmem = pl.BlockSpec(memory_space=pltpu.VMEM)
    hbm = pl.BlockSpec(memory_space=pl.ANY)

    def shift(value, k=1):
        return lax.ppermute(value, "shard", [(i, (i + k) % n) for i in range(n)])

    def swap(value):
        return lax.ppermute(value, "cr", [(0, 1), (1, 0)])

    def flip(value, j):
        return lax.ppermute(value, "yx", [(i, i ^ j) for i in range(yx)])

    def pick(value, index, axis):
        return lax.dynamic_index_in_dim(value, index, axis, keepdims=False)

    def absolute(parts):
        stacked = jnp.stack(parts)
        return jnp.stack([pick(stacked, lax.rem(z - j + n, n), 0) for j in range(n)])

    def plus(one, other):
        return (one.astype(F32) + other.astype(F32)).astype(BF16)

    def around(value):
        return across_too(value, flip(value, 1), flip(value, 2))

    def across_too(value, by_x, by_y):
        half = value.shape[0] // 2
        across = jnp.concatenate([flip(by_x[:half], 2), flip(by_y[half:], 1)], axis=0)
        return [value, by_x, by_y, across]

    def to_owners(blocks):
        return [blocks[0]] + [flip(blocks[j], j) for j in range(1, yx)]

    x_all = lax.all_gather(tokens, "shard", axis=0, tiled=True)

    pack = jnp.concatenate(
        [attn_gain[None], ffn_gain[None], segment_ids.astype(BF16)[None], router_weight.T], axis=0
    )
    pack_rows = 16
    pack = jnp.pad(pack, ((0, 2 * pack_rows - pack.shape[0]), (0, 0)))
    pack = jnp.concatenate([pack[:pack_rows], pack[pack_rows:]], axis=1)
    part_rows = slab // ep
    by_dest = jnp.concatenate(
        [
            lax.dynamic_slice_in_dim(w, r * part_rows, part_rows, axis=0).reshape(part_rows, n, -1)
            for w in (query_weight, key_matrix, value_weight)
        ],
        axis=2,
    )
    ow_rows = out_weight.shape[0] // ep
    fold = cols // slab
    ow_mine = lax.dynamic_slice_in_dim(out_weight, r * ow_rows, ow_rows, axis=0)
    ow_mine = ow_mine.reshape(fold, ow_rows // fold, slab).transpose(1, 0, 2).reshape(ow_rows // fold, cols)

    def piece(k):
        return jnp.concatenate([pick(by_dest, lax.rem(z + k, n), 1), ow_mine, pack], axis=0)

    dense_mine = [piece(0)] + [shift(piece(k), k) for k in range(1, n)]
    ids = jnp.arange(experts, dtype=jnp.int32)
    routed = jnp.any(routes[:, :, None] == ids[None, None, :], axis=1)
    mask_own = jnp.pad(routed.astype(F32), ((0, 0), (0, LANES - experts)))
    dyx_mine = around(jnp.concatenate([cotangent, mask_own.astype(BF16)], axis=1))

    folds = width // ff
    packed = []
    for e in range(own):
        gate, up, down = (pick(w, r * own + e, 0) for w in (gate_weight, up_weight, down_weight))
        down = [down[:, c * ff : (c + 1) * ff] for c in range(folds)]
        packed.append(jnp.concatenate([gate, up] + down, axis=0))
    packed, dense_mine = lax.optimization_barrier((packed, dense_mine))
    weights = [lax.all_gather(w, "shard", axis=0, tiled=True) for w in packed]

    packs = absolute([p[-pack_rows:] for p in dense_mine])
    packs = jnp.concatenate([packs[:, :, :slab], packs[:, :, slab : 2 * slab]], axis=1)
    dense_mine = jnp.stack(around(jnp.stack([p[:-pack_rows] for p in dense_mine])))
    dense_mate = swap(dense_mine)
    gain1 = packs[:, 0, :].reshape(1, width).astype(F32)
    gain2 = packs[:, 1, :].reshape(1, width).astype(F32)
    segments = packs[:, 2, :].reshape(seq).astype(F32)
    seg_col, seg_row = segments[:, None], segments[None, :]
    router = jnp.pad(packs[:, 3 : 3 + experts, :].transpose(0, 2, 1).reshape(width, experts), ((0, 0), (0, LANES - experts)))


    positions = jnp.arange(seq, dtype=jnp.int32).astype(F32)
    frequency = ROPE_BASE ** (-jnp.arange(HEAD // 2, dtype=F32) / (HEAD // 2))
    angles = positions[:, None] * frequency[None, :]
    cosine, sine = jnp.cos(angles), jnp.sin(angles)
    cosine = jnp.concatenate([cosine] * 4, axis=1)
    sine = jnp.concatenate([-sine, sine] * 2, axis=1)

    x_all, dyx_mine = lax.optimization_barrier((x_all, dyx_mine))
    dyx_mine = jnp.concatenate(dyx_mine, axis=0)
    dyx_mate = swap(dyx_mine)
    w_qkv, normed, q, k, v, att, lse = pl.pallas_call(
        functools.partial(front_kernel, rows, heads, kv_heads),
        in_specs=[smem] + [vmem] * 8,
        out_shape=(
            sds((width, cols), BF16),
            sds((seq, width), BF16),
            sds((heads, seq, HEAD), BF16),
            sds((kv_heads, seq, HEAD), BF16),
            sds((kv_heads, seq, HEAD), BF16),
            sds((n, rows, qw), BF16),
            sds((heads, seq, 1), F32),
        ),
        scratch_shapes=[pltpu.VMEM((heads, seq, HEAD), F32)],
        compiler_params=params(),
        cost_estimate=cost(2 * seq * width * cols, 60e6),
        name="front",
    )(place, x_all, gain1, dense_mine, dense_mate, cosine, sine, seg_col, seg_row)

    att = [att[0]] + [shift(att[k], k) for k in range(1, n)]
    hidden, normed2, gates_own, ow = pl.pallas_call(
        mid_kernel,
        in_specs=[smem] + [vmem] * (6 + n),
        out_shape=(
            sds((rows, width), F32),
            sds((rows, width), BF16),
            sds((rows, LANES), F32),
            sds((n, ep * ow_rows, slab), BF16),
        ),
        compiler_params=params(),
        cost_estimate=cost(2 * rows * width * width, 14e6),
        name="mid",
    )(place, tokens, dense_mine, dense_mate, gain2, router, mask_own, *att)

    n2_mine = jnp.concatenate(around(normed2), axis=0)
    n2_mate = swap(n2_mine)

    total = yx * rows
    block = min(512, total)
    steps = total // block

    def by_block(size):
        return pl.BlockSpec((block, size), lambda i: (i, 0))

    def run_expert(e, n2, dyx, previous):
        return pl.pallas_call(
            functools.partial(expert_kernel, n, e),
            grid=(steps,),
            in_specs=[
                smem,
                by_block(width),
                by_block(width + LANES),
                pl.BlockSpec((width, LANES), lambda i: (0, 0)),
                hbm,
            ]
            + ([by_block(width), by_block(width + LANES)] if e else []),
            out_specs=(
                by_block(width),
                by_block(width + LANES),
                by_block(LANES),
                by_block(ff),
                by_block(ff),
                by_block(ff),
            ),
            out_shape=(
                sds((total, width), BF16),
                sds((total, width + LANES), BF16),
                sds((total, LANES), F32),
                sds((total, ff), BF16),
                sds((total, ff), BF16),
                sds((total, ff), BF16),
            ),
            scratch_shapes=[
                pltpu.VMEM((width, ff), BF16),
                pltpu.VMEM((width, ff), BF16),
                pltpu.VMEM((ff, width), BF16),
                pltpu.SemaphoreType.DMA(((2 + folds) * n,)),
            ],
            compiler_params=params(),
            cost_estimate=cost(12 * total * width * ff, 36e6),
            name="expert",
        )(place, n2, dyx, router, weights[e], *previous)

    def half_specs(at):
        sizes = (width, width + LANES, LANES, ff, ff, ff)
        return [pl.BlockSpec((block, size), lambda i: (at(i), 0)) for size in sizes]

    def weight_grads(mate, mine):
        return pl.pallas_call(
            functools.partial(expert_grad_kernel, n, steps),
            grid=(2 * steps,),
            in_specs=half_specs(lambda i: jnp.minimum(i, steps - 1))
            + half_specs(lambda i: jnp.maximum(i - steps, 0)),
            out_specs=pl.BlockSpec((3 * width, ff), lambda i: (0, 0)),
            out_shape=sds((3 * width, ff), BF16),
            scratch_shapes=[
                pltpu.VMEM((width, ff), F32),
                pltpu.VMEM((width, ff), F32),
                pltpu.VMEM((ff, width), F32),
            ],
            compiler_params=params(),
            cost_estimate=cost(12 * total * width * ff, 40e6),
            name="expert_grads",
        )(n2_mate, dyx_mate, *mate, n2_mine, dyx_mine, *mine)

    def spread(value):
        return [value[j * rows : (j + 1) * rows] for j in range(yx)]

    previous_mate = previous_mine = ()
    owned = []
    for e in range(own):
        *previous_mate, g_mate, in_mate, gg_mate, ug_mate = run_expert(e, n2_mate, dyx_mate, previous_mate)
        if e == own - 1:
            moe_got, nb_got = swap(previous_mate[0]), swap(previous_mate[1])
        *previous_mine, g_mine, in_mine, gg_mine, ug_mine = run_expert(e, n2_mine, dyx_mine, previous_mine)
        grads = weight_grads((g_mate, in_mate, gg_mate, ug_mate), (g_mine, in_mine, gg_mine, ug_mine))
        if e < own - 1:
            grads, weights[e + 1] = lax.optimization_barrier((grads, weights[e + 1]))
        else:
            nb_parts = to_owners(spread(plus(previous_mine[1], nb_got)))
            moe_sum = plus(previous_mine[0], moe_got)
            nb_parts, moe_sum, grads, owned = lax.optimization_barrier((nb_parts, moe_sum, grads, owned))
        grads = lax.psum_scatter(grads, "shard", scatter_dimension=0, tiled=True)
        if hi > 1:
            grads = lax.psum(grads.astype(F32), "hi").astype(BF16)
        owned.append(grads)

    hidden_grad, att_grad, ow_grad, ffn_grad, router_grad = pl.pallas_call(
        mid_back_kernel,
        in_specs=[smem] + [vmem] * (7 + n + yx),
        out_shape=(
            sds((rows, width), F32),
            sds((n, rows, qw), BF16),
            sds((n, n * qw, slab), BF16),
            sds((1, width), F32),
            sds((LANES, width), F32),
        ),
        scratch_shapes=[pltpu.VMEM((rows, width), BF16)],
        compiler_params=params(),
        cost_estimate=cost(4 * rows * width * width, 20e6),
        name="mid_back",
    )(place, hidden, cotangent, gates_own, normed2, router, gain2, ow, *att, *nb_parts)

    kvw = 2 * kw
    wide = max(slab, qw, kvw)
    small_rows = 16

    def widen(part):
        return jnp.pad(part, ((0, 0),) * 3 + ((0, wide - part.shape[3]),))

    def rows_of(small):
        small = jnp.pad(small, ((0, ep * small_rows - small.shape[0]), (0, 0)))
        return widen(small.reshape(ep, small_rows, n, slab).transpose(2, 0, 1, 3).astype(BF16))

    def dense_sum(pieces, beside=()):
        dense = jnp.concatenate(pieces, axis=2)
        depth = dense.shape[2]
        dense = dense.reshape(n, yx, 2, depth, wide).transpose(2, 1, 0, 3, 4)
        got, beside = lax.optimization_barrier((swap(pick(dense, 1 - core, 0)), beside))
        dense = plus(pick(dense, core, 0), got)
        parts = to_owners([pick(dense, lax.bitwise_xor(chip, jnp.int32(j)), 0) for j in range(yx)])
        return sum(p.astype(F32) for p in parts).astype(BF16), beside

    moe_parts = to_owners(spread(moe_sum))
    att_grad, moe_parts = lax.optimization_barrier((att_grad, moe_parts))
    att_grad = lax.all_to_all(att_grad, "shard", 0, 0)
    early = (owned[0], flip(owned[0], 1), flip(owned[0], 2))
    att_grad, early = lax.optimization_barrier((att_grad, early))
    early = across_too(*early)
    def with_mate(mine):
        return [p for one in mine for p in (one, swap(one))]

    def share(e, pieces, shared):
        def out_index(j, place_ref):
            return (peer(place_ref, j % 2, j // 2), e, 0, 0)

        return pl.pallas_call(
            functools.partial(share_kernel, ep),
            grid_spec=pltpu.PrefetchScalarGridSpec(
                num_scalar_prefetch=1,
                grid=(ep,),
                in_specs=[pl.BlockSpec((3 * slab, ff), lambda j, place_ref: (0, 0))] * ep + [hbm] * len(shared),
                out_specs=(
                    pl.BlockSpec((1, 1, slab, ff), out_index),
                    pl.BlockSpec((1, 1, slab, ff), out_index),
                    pl.BlockSpec((1, 1, ff // n, width), out_index),
                ),
            ),
            out_shape=(
                sds((ep, own, slab, ff), F32),
                sds((ep, own, slab, ff), F32),
                sds((ep, own, ff // n, width), F32),
            ),
            input_output_aliases={1 + ep + i: i for i in range(len(shared))},
            compiler_params=params(),
            cost_estimate=cost(0, 20e6),
            name="share",
        )(place, *pieces, *shared)

    raw = pl.pallas_call(
        functools.partial(back_kernel, rows, heads, kv_heads),
        out_shape=sds((seq, cols), F32),
        scratch_shapes=[
            pltpu.VMEM((heads, seq, HEAD), BF16),
            pltpu.VMEM((heads, seq, HEAD), F32),
            pltpu.VMEM((kv_heads, seq, HEAD), F32),
            pltpu.VMEM((kv_heads, seq, HEAD), F32),
        ],
        compiler_params=params(),
        cost_estimate=cost(2 * seq * width * cols, 52e6),
        name="back",
    )(q, k, v, lse, seg_col, seg_row, att_grad)
    raw, owned, early = lax.optimization_barrier((raw, owned, early))
    ng, qkv_grad, gain_grad = pl.pallas_call(
        functools.partial(finish_kernel, rows, qw + kw),
        out_shape=(sds((seq, width), BF16), sds((width, cols), BF16), sds((1, width), F32)),
        scratch_shapes=[pltpu.VMEM((seq, cols), BF16)],
        compiler_params=params(),
        cost_estimate=cost(0, 60e6 / SCALE),
        name="finish",
    )(raw, x_all, normed, w_qkv, cosine, sine)
    qkv_rows = qkv_grad.reshape(n, ep, part_rows, cols)
    shared = share(0, with_mate(early), ())
    part = lax.psum_scatter(ng, "shard", scatter_dimension=0, tiled=True).astype(F32)
    by_x = [flip(value, 1) for value in owned[1:]]
    qkv_rows, by_x = lax.optimization_barrier((qkv_rows, by_x))
    last = [(value, one, flip(value, 2)) for value, one in zip(owned[1:], by_x)]
    small = rows_of(jnp.concatenate([gain_grad, ffn_grad, router_grad[:experts]], axis=0))
    ow_grad = widen(ow_grad.reshape(n, ep, ow_rows, slab))
    dense, last = dense_sum([ow_grad, small, widen(qkv_rows[..., :qw]), widen(qkv_rows[..., qw:])], last)
    last = [with_mate(across_too(*parts)) for parts in last]
    if hi > 1:
        dense = lax.psum(dense.astype(F32), "hi").astype(BF16)
    dense, last, shared, part = lax.optimization_barrier((dense, last, shared, part))
    for e in range(1, own):
        shared = share(e, last[e - 1], shared)
    output = (hidden + sum(p.astype(F32) for p in moe_parts)).astype(BF16)


    dense = [pick(dense, z, 0)] + [shift(pick(dense, lax.rem(z + k, n), 0), k) for k in range(1, n)]
    cut = ow_rows + small_rows
    summed = sum(p[:cut].astype(F32) for p in dense).astype(BF16)
    kept = absolute([p[cut:] for p in dense]).reshape(n * 2 * part_rows, wide)
    mine = jnp.concatenate([summed, kept], axis=0)
    mine = [mine] + [flip(mine, j) for j in range(1, yx)]
    mine = jnp.stack(mine)
    x = tokens.astype(F32)
    inv = inverse_rms(x)
    scaled = x * inv
    w1 = part * gain1
    input_grad = hidden_grad + inv * (w1 - scaled * jnp.mean(w1 * scaled, axis=-1, keepdims=True))

    both = jnp.stack([mine, swap(mine)], axis=1).reshape((ep,) + mine.shape[1:])
    full = jnp.stack([pick(both, lax.bitwise_xor(r, jnp.int32(i)), 0) for i in range(ep)])
    ow_full = full[:, :ow_rows, :slab].reshape(-1, slab).astype(F32)
    small_full = full[:, ow_rows:cut, :slab].reshape(-1, slab).astype(F32)
    kept = full[:, cut:].reshape(ep, n, 2, part_rows, wide)

    gate_grad, up_grad, down_grad = (g.reshape((experts,) + g.shape[2:]) for g in shared)

    def columns(which, start, size):
        part = kept[:, :, which, :, start : start + size]
        return part.transpose(0, 2, 1, 3).reshape(slab, n * size).astype(F32)

    return (
        output,
        input_grad,
        small_full[0],
        columns(0, 0, qw),
        columns(1, 0, kw),
        columns(1, kw, kw),
        ow_full,
        small_full[1],
        small_full[2 : 2 + experts].T,
        gate_grad,
        up_grad,
        down_grad,
    )


def solution(mesh):
    rep, n = mesh.shape["rep"], mesh.shape["shard"]
    yx = math.gcd(rep // 2, 4)
    hi = rep // (2 * yx)
    split = Mesh(mesh.devices.reshape(hi, yx, 2, n), ("hi", "yx", "cr", "shard"))
    rows = ("hi", "yx", "cr", "shard")
    placed = (
        P(rows, None),
        P(rows, None),
        P(rows),
        P(rows, None),
        P("shard"),
        P("shard", None),
        P("shard", None),
        P("shard", None),
        P(None, "shard"),
        P("shard"),
        P("shard", None),
        P(None, "shard", None),
        P(None, "shard", None),
        P(None, "shard", None),
    )
    return jax.shard_map(
        functools.partial(per_device, hi, yx, n),
        mesh=split,
        in_specs=placed,
        out_specs=(
            P(rows, None),
            P(rows, None),
            P("shard"),
            P("shard", None),
            P("shard", None),
            P("shard", None),
            P(None, "shard"),
            P("shard"),
            P("shard", None),
            P(None, "shard", None),
            P(None, "shard", None),
            P(None, "shard", None),
        ),
        check_vma=False,
    )
```

```python
import functools
import math

import jax
import jax.numpy as jnp
from jax import lax
from jax.experimental import pallas as pl
from jax.experimental.pallas import tpu as pltpu
from jax.sharding import Mesh
from jax.sharding import PartitionSpec as P

QUERY_HEADS = 16
KEY_VALUE_HEADS = 8
HEAD = 64
LANES = 128
MIX_LOW = 64
SCALE = 0.02

EPS = 1e-06
ROPE_BASE = 10000.0
MASKED = -1e30
F32 = jnp.float32
BF16 = jnp.bfloat16
NT = (((1,), (1,)), ((), ()))
TN = (((0,), (0,)), ((), ()))
VMEM_LIMIT = 60 * 1024 * 1024


def dot(a, b):
    return jnp.dot(a, b, preferred_element_type=F32)


def dot_nt(a, b):
    return lax.dot_general(a, b, NT, preferred_element_type=F32)


def dot_tn(a, b):
    return lax.dot_general(a, b, TN, preferred_element_type=F32)


def split_hi_lo(value):
    high = value.astype(BF16)
    return high, (value - high.astype(F32)).astype(BF16)


def inverse_rms(value):
    return lax.rsqrt(jnp.mean(value * value, axis=-1, keepdims=True) + EPS)


def swap_halves(value):
    width = value.shape[1]
    lane = lax.broadcasted_iota(jnp.int32, value.shape, 1)
    up = pltpu.roll(value, width - HEAD // 2, 1)
    down = pltpu.roll(value, HEAD // 2, 1)
    return jnp.where(lane % HEAD < HEAD // 2, up, down)


def rotate(value, cosine, sine):
    copies = value.shape[1] // LANES
    cosine = jnp.concatenate([cosine] * copies, axis=1)
    sine = jnp.concatenate([sine] * copies, axis=1)
    return value * cosine + swap_halves(value) * sine


def allowed_pairs(seg_col, seg_row, row0, count):
    rows = seg_col.shape[0]
    row = row0 + lax.broadcasted_iota(jnp.int32, (rows, count), 0)
    col = lax.broadcasted_iota(jnp.int32, (rows, count), 1)
    return (seg_col == seg_row) & (col <= row)


def ring_chunk(z, k, parts):
    return lax.rem(z - k + parts, parts)


def chunk_of(index, size):
    return pl.ds(pl.multiple_of(index * size, size), size)


def peer(place_ref, c, j):
    return lax.bitwise_xor(place_ref[2], jnp.int32(j)) * 2 + lax.bitwise_xor(place_ref[3], jnp.int32(c))


def front_kernel(
    block, heads, kv_heads, place_ref, x_ref, gain_ref, mine_ref, mate_ref, cos_ref, sin_ref, segc_ref, segr_ref,
    w_ref, normed_ref, q_ref, k_ref, v_ref, att_ref, lse_ref, out_s,
):
    seq = x_ref.shape[0]
    blocks = seq // block
    group = heads // kv_heads
    qw, kw = heads * HEAD, kv_heads * HEAD
    z = place_ref[0]
    slab = w_ref.shape[0] // blocks
    part = slab // (2 * mine_ref.shape[0])
    for c, piece_ref in enumerate((mine_ref, mate_ref)):
        for j in range(piece_ref.shape[0]):
            at = peer(place_ref, c, j) * part
            for i in range(blocks):
                start = pl.multiple_of(ring_chunk(z, i, blocks) * slab + at, part)
                w_ref[pl.ds(start, part), :] = piece_ref[j, i, :part, :]

    def project(i, carry):
        rows = pl.ds(pl.multiple_of(i * block, block), block)
        x = x_ref[rows, :].astype(F32)
        normed = (x * inverse_rms(x) * gain_ref[...]).astype(BF16)
        normed_ref[rows, :] = normed
        qkv = dot(normed, w_ref[...])
        turned = rotate(qkv[:, : qw + kw], cos_ref[rows, :], sin_ref[rows, :])
        for h in range(heads):
            q_ref[h, rows, :] = turned[:, h * HEAD : (h + 1) * HEAD].astype(BF16)
        for h in range(kv_heads):
            k_ref[h, rows, :] = turned[:, qw + h * HEAD : qw + (h + 1) * HEAD].astype(BF16)
            v_ref[h, rows, :] = qkv[:, qw + kw + h * HEAD : qw + kw + (h + 1) * HEAD].astype(BF16)
        return carry

    lax.fori_loop(0, blocks, project, 0)

    def one_head(h, carry):
        kv = h // group
        for i in range(blocks):
            count = (i + 1) * block
            rows = slice(i * block, (i + 1) * block)
            q = q_ref[h, rows, :] * jnp.asarray(0.125, BF16)
            k = k_ref[kv, :count, :]
            v = v_ref[kv, :count, :]
            allowed = allowed_pairs(segc_ref[rows, :], segr_ref[:, :count], i * block, count)
            s = jnp.where(allowed, dot_nt(q, k), MASKED)
            top = jnp.max(s, axis=-1, keepdims=True)
            e = jnp.exp(s - top)
            total = jnp.sum(e, axis=-1, keepdims=True)
            lse_ref[h, rows, :] = top + jnp.log(total)
            p = (e * (1.0 / total)).astype(BF16)
            out_s[h, rows, :] = dot(p, v)
        return carry

    lax.fori_loop(0, heads, one_head, 0)
    for i in range(blocks):
        k = lax.rem(i - z + blocks, blocks)
        for h in range(heads):
            att_ref[k, :, h * HEAD : (h + 1) * HEAD] = out_s[h, i * block : (i + 1) * block, :].astype(BF16)


def back_kernel(
    block, heads, kv_heads, q_ref, k_ref, v_ref, lse_ref, segc_ref, segr_ref, do_ref,
    raw_ref, do_s, dq_s, dk_s, dv_s,
):
    seq = q_ref.shape[1]
    blocks = seq // block
    group = heads // kv_heads
    qw, kw = heads * HEAD, kv_heads * HEAD
    for k in range(blocks):
        at = slice(k * block, (k + 1) * block)
        for h in range(heads):
            do_s[h, at, :] = do_ref[k, :, h * HEAD : (h + 1) * HEAD]
    dk_s[...] = jnp.zeros_like(dk_s)
    dv_s[...] = jnp.zeros_like(dv_s)

    def one_head(h, carry):
        kv = h // group
        for i in range(blocks):
            count = (i + 1) * block
            rows = slice(i * block, (i + 1) * block)
            q = q_ref[h, rows, :] * jnp.asarray(0.125, BF16)
            k = k_ref[kv, :count, :]
            v = v_ref[kv, :count, :]
            do = do_s[h, rows, :]
            allowed = allowed_pairs(segc_ref[rows, :], segr_ref[:, :count], i * block, count)
            s = jnp.where(allowed, dot_nt(q, k), MASKED)
            prob = jnp.exp(s - lse_ref[h, rows, :])
            grad = dot_nt(do, v)
            inner = jnp.sum(prob * grad, axis=-1, keepdims=True)
            ds = (prob * (grad - inner)).astype(BF16)
            dq_s[h, rows, :] = dot(ds, k) * 0.125
            dk_s[kv, :count, :] += dot_tn(ds, q)
            dv_s[kv, :count, :] += dot_tn(prob.astype(BF16), do)
        return carry

    lax.fori_loop(0, heads, one_head, 0)
    for h in range(heads):
        raw_ref[:, h * HEAD : (h + 1) * HEAD] = dq_s[h]
    for h in range(kv_heads):
        raw_ref[:, qw + h * HEAD : qw + (h + 1) * HEAD] = dk_s[h]
        raw_ref[:, qw + kw + h * HEAD : qw + kw + (h + 1) * HEAD] = dv_s[h]


def finish_kernel(
    block, turned, raw_ref, x_ref, normed_ref, w_ref, cos_ref, sin_ref, ng_ref, dw_ref, gain_ref, g_s,
):
    seq = x_ref.shape[0]
    blocks = seq // block
    gain_ref[...] = jnp.zeros_like(gain_ref)

    def finish(i, carry):
        rows = pl.ds(pl.multiple_of(i * block, block), block)
        g_s[rows, :turned] = rotate(raw_ref[rows, :turned], cos_ref[rows, :], -sin_ref[rows, :]).astype(BF16)
        g_s[rows, turned:] = raw_ref[rows, turned:].astype(BF16)
        ng = dot_nt(g_s[rows, :], w_ref[...])
        x = x_ref[rows, :].astype(F32)
        gain_ref[...] += jnp.sum(ng * (x * inverse_rms(x)), axis=0, keepdims=True)
        ng_ref[rows, :] = ng.astype(BF16)
        return carry

    lax.fori_loop(0, blocks, finish, 0)
    width = normed_ref.shape[1]
    for c in range(0, width, 256):
        dw_ref[c : c + 256, :] = dot_tn(normed_ref[:, c : c + 256], g_s[...]).astype(BF16)


def softmax_gates(logits, mask):
    shown = jnp.where(mask > 0.0, logits, MASKED)
    e = jnp.where(mask > 0.0, jnp.exp(shown - jnp.max(shown, axis=-1, keepdims=True)), 0.0)
    return e * (1.0 / jnp.sum(e, axis=-1, keepdims=True))


def mid_kernel(
    place_ref, x_ref, mine_ref, mate_ref, gain_ref, router_ref, mask_ref, *refs
):
    hidden_ref, normed_ref, gates_ref, ow_ref = refs[-4:]
    att_refs = refs[:-4]
    parts, width = ow_ref.shape[0], ow_ref.shape[2]
    share = ow_ref.shape[1] // (2 * mine_ref.shape[0])
    fold = mine_ref.shape[3] // width
    lines = share // fold
    skip = ow_ref.shape[0] * width // (2 * parts * mine_ref.shape[0])
    for c, piece_ref in enumerate((mine_ref, mate_ref)):
        for j in range(piece_ref.shape[0]):
            at = peer(place_ref, c, j) * share
            for k in range(parts):
                for f in range(fold):
                    start = pl.multiple_of(at + f * lines, lines)
                    ow_ref[k, pl.ds(start, lines), :] = piece_ref[j, k, skip : skip + lines, f * width : (f + 1) * width]
    depth = att_refs[0].shape[1]
    for j in range(parts):
        cols = chunk_of(ring_chunk(place_ref[0], j, parts), width)
        total = x_ref[:, cols].astype(F32)
        for i in range(parts):
            at = chunk_of(ring_chunk(place_ref[0], i, parts), depth)
            total = total + dot(att_refs[i][...], ow_ref[j, at, :])
        hidden_ref[:, cols] = total
    hidden = hidden_ref[...]
    normed = (hidden * inverse_rms(hidden) * gain_ref[...]).astype(BF16)
    normed_ref[...] = normed
    gates_ref[...] = softmax_gates(dot(normed, router_ref[...]), mask_ref[...])


def mid_back_kernel(
    place_ref, hidden_ref, dy_ref, gates_ref, normed_ref, router_ref, gain_ref, ow_ref, *refs
):
    hg_ref, ag_ref, owg_ref, fg_ref, rg_ref, aog_s = refs[-6:]
    att_refs = refs[: ow_ref.shape[0]]
    nb_refs = refs[ow_ref.shape[0] : -6]
    gates = gates_ref[...]
    width_all = hidden_ref.shape[1]
    nb = sum(ref[...].astype(F32) for ref in nb_refs)
    mix = nb[:, width_all:]
    mix = mix + pltpu.roll(mix, LANES - MIX_LOW, 1)
    lg = gates * (mix - jnp.sum(gates * mix, axis=-1, keepdims=True))
    high, low = split_hi_lo(lg)
    normed = normed_ref[...]
    rg_ref[...] = dot_tn(high, normed) + dot_tn(low, normed)
    router = router_ref[...]
    ng = nb[:, :width_all] + dot_nt(high, router) + dot_nt(low, router)
    hidden = hidden_ref[...]
    inv = inverse_rms(hidden)
    scaled = hidden * inv
    fg_ref[...] = jnp.sum(ng * scaled, axis=0, keepdims=True)
    w = ng * gain_ref[...]
    hg = dy_ref[...].astype(F32) + inv * (w - scaled * jnp.mean(w * scaled, axis=-1, keepdims=True))
    hg_ref[...] = hg
    aog_s[...] = hg.astype(BF16)
    parts, width = ow_ref.shape[0], ow_ref.shape[2]
    depth = att_refs[0].shape[1]
    for i in range(parts):
        group = ring_chunk(place_ref[0], i, parts)
        rows = chunk_of(group, depth)
        total = None
        for j in range(parts):
            chunk = ring_chunk(place_ref[0], j, parts)
            part = dot_nt(aog_s[:, chunk_of(chunk, width)], ow_ref[j, rows, :])
            total = part if total is None else total + part
        ag_ref[group] = total.astype(BF16)
        for j in range(parts):
            owg_ref[j, rows, :] = dot_tn(att_refs[i][...], aog_s[:, j * width : (j + 1) * width]).astype(BF16)


def expert_kernel(parts, e, place_ref, n2_ref, dyx_ref, router_ref, w_ref, *refs):
    previous = refs[:2] if e else ()
    moe_ref, nb_ref, g_ref, inner_ref, gg_ref, ug_ref, wg_s, wu_s, wd_s, sems = refs[len(previous) :]
    width, ff = wg_s.shape
    slab, ff_slab = width // parts, ff // parts

    first_step = pl.program_id(0) == 0

    def move(start, count, target, sem):
        return pltpu.make_async_copy(w_ref.at[start : start + count, :], target, sems.at[sem])

    gate_copies, up_copies, down_copies = [], [], []
    for k in range(parts):
        start = k * 3 * slab
        rows = slice(k * slab, (k + 1) * slab)
        gate_copies.append(move(start, slab, wg_s.at[rows, :], k))
        up_copies.append(move(start + slab, slab, wu_s.at[rows, :], parts + k))
        for c in range(width // ff):
            at = start + 2 * slab + c * ff_slab
            target = wd_s.at[k * ff_slab : (k + 1) * ff_slab, c * ff : (c + 1) * ff]
            down_copies.append(move(at, ff_slab, target, (2 + c) * parts + k))

    @pl.when(first_step)
    def load():
        for copy in gate_copies + up_copies + down_copies:
            copy.start()

    def ready(copies):
        @pl.when(first_step)
        def wait():
            for copy in copies:
                copy.wait()

    x = n2_ref[...]
    dy = dyx_ref[:, :width].astype(F32)
    gates = softmax_gates(dot(x, router_ref[...]), dyx_ref[:, width:].astype(F32))
    lane = lax.broadcasted_iota(jnp.int32, gates.shape, 1)
    at = place_ref[1] + e
    g = jnp.sum(jnp.where(lane == at, gates, 0.0), axis=-1, keepdims=True)
    ready(gate_copies)
    ga = dot(x, wg_s[...])
    ready(up_copies)
    ua = dot(x, wu_s[...])
    sg = jax.nn.sigmoid(ga)
    act = ga * sg
    inner = (act * ua).astype(BF16)
    inner_ref[...] = inner
    ready(down_copies)
    eo = dot(inner, wd_s[...]).astype(BF16).astype(F32)
    moe = g * eo
    high, low = split_hi_lo(jnp.sum(dy * eo, axis=-1, keepdims=True))
    mix = jnp.where(lane == at, high.astype(F32), 0.0) + jnp.where(lane == MIX_LOW + at, low.astype(F32), 0.0)
    g_ref[...] = jnp.where(lane == 0, g, 0.0)
    ig = dot_nt((g * dy).astype(BF16), wd_s[...])
    gg = (ig * ua * sg * (1.0 + ga * (1.0 - sg))).astype(BF16)
    ug = (ig * act).astype(BF16)
    gg_ref[...] = gg
    ug_ref[...] = ug
    nb = dot_nt(gg, wg_s[...]) + dot_nt(ug, wu_s[...])
    if e:
        moe = moe + previous[0][...].astype(F32)
        nb = nb + previous[1][:, :width].astype(F32)
        mix = mix + previous[1][:, width:].astype(F32)
    moe_ref[...] = moe.astype(BF16)
    nb_ref[:, :width] = nb.astype(BF16)
    nb_ref[:, width:] = mix.astype(BF16)


def expert_grad_kernel(parts, half, *refs):
    halves = (refs[:6], refs[6:12])
    out_ref, g_s, u_s, d_s = refs[12:]
    step = pl.program_id(0)
    width, ff = g_s.shape
    slab, ff_slab = width // parts, ff // parts

    @pl.when(step == 0)
    def clear():
        g_s[...] = jnp.zeros_like(g_s)
        u_s[...] = jnp.zeros_like(u_s)
        d_s[...] = jnp.zeros_like(d_s)

    def add(n2_ref, dyx_ref, g_ref, inner_ref, gg_ref, ug_ref):
        x = n2_ref[...]
        g = jnp.sum(g_ref[...], axis=-1, keepdims=True)
        og = (g * dyx_ref[:, :width].astype(F32)).astype(BF16)
        g_s[...] += dot_tn(x, gg_ref[...])
        u_s[...] += dot_tn(x, ug_ref[...])
        d_s[...] += dot_tn(inner_ref[...], og)

    pl.when(step < half)(lambda: add(*halves[0]))
    pl.when(step >= half)(lambda: add(*halves[1]))

    @pl.when(step == pl.num_programs(0) - 1)
    def store():
        for k in range(parts):
            start = k * 3 * slab
            out_ref[start : start + slab, :] = g_s[k * slab : (k + 1) * slab, :].astype(BF16)
            out_ref[start + slab : start + 2 * slab, :] = u_s[k * slab : (k + 1) * slab, :].astype(BF16)
            for c in range(width // ff):
                at = start + 2 * slab + c * ff_slab
                out_ref[at : at + ff_slab, :] = d_s[k * ff_slab : (k + 1) * ff_slab, c * ff : (c + 1) * ff].astype(BF16)


def share_kernel(count, place_ref, *refs):
    gate_ref, up_ref, down_ref = refs[-3:]
    _, _, slab, ff = gate_ref.shape
    ff_slab, width = down_ref.shape[2:]
    for i in range(count):

        @pl.when(pl.program_id(0) == i)
        def copy(piece_ref=refs[i]):
            gate_ref[0, 0] = piece_ref[:slab, :].astype(F32)
            up_ref[0, 0] = piece_ref[slab : 2 * slab, :].astype(F32)
            for c in range(width // ff):
                at = 2 * slab + c * ff_slab
                down_ref[0, 0, :, c * ff : (c + 1) * ff] = piece_ref[at : at + ff_slab, :].astype(F32)


def sds(shape, dtype):
    return jax.ShapeDtypeStruct(shape, dtype)


def params():
    return pltpu.CompilerParams(vmem_limit_bytes=VMEM_LIMIT)


def cost(flops, traffic):
    return pl.CostEstimate(flops=int(flops * SCALE), bytes_accessed=int(traffic * SCALE), transcendentals=0)


def per_device(
    hi, yx, n, tokens, cotangent, segment_ids, routes, attn_gain, query_weight, key_matrix, value_weight,
    out_weight, ffn_gain, router_weight, gate_weight, up_weight, down_weight,
):
    rows, width = tokens.shape
    seq = rows * n
    experts = gate_weight.shape[0]
    ep = yx * 2
    own = experts // ep
    heads, kv_heads = QUERY_HEADS // n, KEY_VALUE_HEADS // n
    qw, kw = heads * HEAD, kv_heads * HEAD
    cols = qw + 2 * kw
    slab = width // n
    ff = gate_weight.shape[2]
    z = lax.axis_index("shard").astype(jnp.int32)
    core = lax.axis_index("cr").astype(jnp.int32)
    chip = lax.axis_index("yx").astype(jnp.int32)
    r = chip * 2 + core
    place = jnp.stack([z, r * own, chip, core])
    smem = pl.BlockSpec(memory_space=pltpu.SMEM)
    vmem = pl.BlockSpec(memory_space=pltpu.VMEM)
    hbm = pl.BlockSpec(memory_space=pl.ANY)

    def shift(value, k=1):
        return lax.ppermute(value, "shard", [(i, (i + k) % n) for i in range(n)])

    def swap(value):
        return lax.ppermute(value, "cr", [(0, 1), (1, 0)])

    def flip(value, j):
        return lax.ppermute(value, "yx", [(i, i ^ j) for i in range(yx)])

    def pick(value, index, axis):
        return lax.dynamic_index_in_dim(value, index, axis, keepdims=False)

    def absolute(parts):
        stacked = jnp.stack(parts)
        return jnp.stack([pick(stacked, lax.rem(z - j + n, n), 0) for j in range(n)])

    def plus(one, other):
        return (one.astype(F32) + other.astype(F32)).astype(BF16)

    def around(value):
        return across_too(value, flip(value, 1), flip(value, 2))

    def across_too(value, by_x, by_y):
        half = value.shape[0] // 2
        across = jnp.concatenate([flip(by_x[:half], 2), flip(by_y[half:], 1)], axis=0)
        return [value, by_x, by_y, across]

    def to_owners(blocks):
        return [blocks[0]] + [flip(blocks[j], j) for j in range(1, yx)]

    x_all = lax.all_gather(tokens, "shard", axis=0, tiled=True)

    pack = jnp.concatenate(
        [attn_gain[None], ffn_gain[None], segment_ids.astype(BF16)[None], router_weight.T], axis=0
    )
    pack_rows = 16
    pack = jnp.pad(pack, ((0, 2 * pack_rows - pack.shape[0]), (0, 0)))
    pack = jnp.concatenate([pack[:pack_rows], pack[pack_rows:]], axis=1)
    part_rows = slab // ep
    by_dest = jnp.concatenate(
        [
            lax.dynamic_slice_in_dim(w, r * part_rows, part_rows, axis=0).reshape(part_rows, n, -1)
            for w in (query_weight, key_matrix, value_weight)
        ],
        axis=2,
    )
    ow_rows = out_weight.shape[0] // ep
    fold = cols // slab
    ow_mine = lax.dynamic_slice_in_dim(out_weight, r * ow_rows, ow_rows, axis=0)
    ow_mine = ow_mine.reshape(fold, ow_rows // fold, slab).transpose(1, 0, 2).reshape(ow_rows // fold, cols)

    def piece(k):
        return jnp.concatenate([pick(by_dest, lax.rem(z + k, n), 1), ow_mine, pack], axis=0)

    dense_mine = [piece(0)] + [shift(piece(k), k) for k in range(1, n)]
    ids = jnp.arange(experts, dtype=jnp.int32)
    routed = jnp.any(routes[:, :, None] == ids[None, None, :], axis=1)
    mask_own = jnp.pad(routed.astype(F32), ((0, 0), (0, LANES - experts)))
    dyx_mine = around(jnp.concatenate([cotangent, mask_own.astype(BF16)], axis=1))

    folds = width // ff
    packed = []
    for e in range(own):
        gate, up, down = (pick(w, r * own + e, 0) for w in (gate_weight, up_weight, down_weight))
        down = [down[:, c * ff : (c + 1) * ff] for c in range(folds)]
        packed.append(jnp.concatenate([gate, up] + down, axis=0))
    packed, dense_mine = lax.optimization_barrier((packed, dense_mine))
    weights = [lax.all_gather(w, "shard", axis=0, tiled=True) for w in packed]

    packs = absolute([p[-pack_rows:] for p in dense_mine])
    packs = jnp.concatenate([packs[:, :, :slab], packs[:, :, slab : 2 * slab]], axis=1)
    dense_mine = jnp.stack(around(jnp.stack([p[:-pack_rows] for p in dense_mine])))
    dense_mate = swap(dense_mine)
    gain1 = packs[:, 0, :].reshape(1, width).astype(F32)
    gain2 = packs[:, 1, :].reshape(1, width).astype(F32)
    segments = packs[:, 2, :].reshape(seq).astype(F32)
    seg_col, seg_row = segments[:, None], segments[None, :]
    router = jnp.pad(packs[:, 3 : 3 + experts, :].transpose(0, 2, 1).reshape(width, experts), ((0, 0), (0, LANES - experts)))


    positions = jnp.arange(seq, dtype=jnp.int32).astype(F32)
    frequency = ROPE_BASE ** (-jnp.arange(HEAD // 2, dtype=F32) / (HEAD // 2))
    angles = positions[:, None] * frequency[None, :]
    cosine, sine = jnp.cos(angles), jnp.sin(angles)
    cosine = jnp.concatenate([cosine] * 4, axis=1)
    sine = jnp.concatenate([-sine, sine] * 2, axis=1)

    x_all, dyx_mine = lax.optimization_barrier((x_all, dyx_mine))
    dyx_mine = jnp.concatenate(dyx_mine, axis=0)
    dyx_mate = swap(dyx_mine)
    w_qkv, normed, q, k, v, att, lse = pl.pallas_call(
        functools.partial(front_kernel, rows, heads, kv_heads),
        in_specs=[smem] + [vmem] * 8,
        out_shape=(
            sds((width, cols), BF16),
            sds((seq, width), BF16),
            sds((heads, seq, HEAD), BF16),
            sds((kv_heads, seq, HEAD), BF16),
            sds((kv_heads, seq, HEAD), BF16),
            sds((n, rows, qw), BF16),
            sds((heads, seq, 1), F32),
        ),
        scratch_shapes=[pltpu.VMEM((heads, seq, HEAD), F32)],
        compiler_params=params(),
        cost_estimate=cost(2 * seq * width * cols, 60e6),
        name="front",
    )(place, x_all, gain1, dense_mine, dense_mate, cosine, sine, seg_col, seg_row)

    att = [att[0]] + [shift(att[k], k) for k in range(1, n)]
    hidden, normed2, gates_own, ow = pl.pallas_call(
        mid_kernel,
        in_specs=[smem] + [vmem] * (6 + n),
        out_shape=(
            sds((rows, width), F32),
            sds((rows, width), BF16),
            sds((rows, LANES), F32),
            sds((n, ep * ow_rows, slab), BF16),
        ),
        compiler_params=params(),
        cost_estimate=cost(2 * rows * width * width, 14e6),
        name="mid",
    )(place, tokens, dense_mine, dense_mate, gain2, router, mask_own, *att)

    n2_mine = jnp.concatenate(around(normed2), axis=0)
    n2_mate = swap(n2_mine)

    total = yx * rows
    block = min(512, total)
    steps = total // block

    def by_block(size):
        return pl.BlockSpec((block, size), lambda i: (i, 0))

    def run_expert(e, n2, dyx, previous):
        return pl.pallas_call(
            functools.partial(expert_kernel, n, e),
            grid=(steps,),
            in_specs=[
                smem,
                by_block(width),
                by_block(width + LANES),
                pl.BlockSpec((width, LANES), lambda i: (0, 0)),
                hbm,
            ]
            + ([by_block(width), by_block(width + LANES)] if e else []),
            out_specs=(
                by_block(width),
                by_block(width + LANES),
                by_block(LANES),
                by_block(ff),
                by_block(ff),
                by_block(ff),
            ),
            out_shape=(
                sds((total, width), BF16),
                sds((total, width + LANES), BF16),
                sds((total, LANES), F32),
                sds((total, ff), BF16),
                sds((total, ff), BF16),
                sds((total, ff), BF16),
            ),
            scratch_shapes=[
                pltpu.VMEM((width, ff), BF16),
                pltpu.VMEM((width, ff), BF16),
                pltpu.VMEM((ff, width), BF16),
                pltpu.SemaphoreType.DMA(((2 + folds) * n,)),
            ],
            compiler_params=params(),
            cost_estimate=cost(12 * total * width * ff, 36e6),
            name="expert",
        )(place, n2, dyx, router, weights[e], *previous)

    def half_specs(at):
        sizes = (width, width + LANES, LANES, ff, ff, ff)
        return [pl.BlockSpec((block, size), lambda i: (at(i), 0)) for size in sizes]

    def weight_grads(mate, mine):
        return pl.pallas_call(
            functools.partial(expert_grad_kernel, n, steps),
            grid=(2 * steps,),
            in_specs=half_specs(lambda i: jnp.minimum(i, steps - 1))
            + half_specs(lambda i: jnp.maximum(i - steps, 0)),
            out_specs=pl.BlockSpec((3 * width, ff), lambda i: (0, 0)),
            out_shape=sds((3 * width, ff), BF16),
            scratch_shapes=[
                pltpu.VMEM((width, ff), F32),
                pltpu.VMEM((width, ff), F32),
                pltpu.VMEM((ff, width), F32),
            ],
            compiler_params=params(),
            cost_estimate=cost(12 * total * width * ff, 40e6),
            name="expert_grads",
        )(n2_mate, dyx_mate, *mate, n2_mine, dyx_mine, *mine)

    def over_groups(grads):
        grads = lax.psum_scatter(grads, "shard", scatter_dimension=0, tiled=True)
        return lax.psum(grads.astype(F32), "hi").astype(BF16) if hi > 1 else grads

    def spread(value):
        return [value[j * rows : (j + 1) * rows] for j in range(yx)]

    previous_mate = previous_mine = ()
    owned = []
    for e in range(own):
        *previous_mate, g_mate, in_mate, gg_mate, ug_mate = run_expert(e, n2_mate, dyx_mate, previous_mate)
        if e == own - 1:
            moe_got, nb_got = swap(previous_mate[0]), swap(previous_mate[1])
        *previous_mine, g_mine, in_mine, gg_mine, ug_mine = run_expert(e, n2_mine, dyx_mine, previous_mine)
        grads = weight_grads((g_mate, in_mate, gg_mate, ug_mate), (g_mine, in_mine, gg_mine, ug_mine))
        if e < own - 1:
            grads, weights[e + 1] = lax.optimization_barrier((grads, weights[e + 1]))
        else:
            nb_parts = to_owners(spread(plus(previous_mine[1], nb_got)))
            moe_sum = plus(previous_mine[0], moe_got)
            nb_parts, moe_sum, grads, owned = lax.optimization_barrier((nb_parts, moe_sum, grads, owned))
        if e < own - 1:
            owned.append(over_groups(grads))

    hidden_grad, att_grad, ow_grad, ffn_grad, router_grad = pl.pallas_call(
        mid_back_kernel,
        in_specs=[smem] + [vmem] * (7 + n + yx),
        out_shape=(
            sds((rows, width), F32),
            sds((n, rows, qw), BF16),
            sds((n, n * qw, slab), BF16),
            sds((1, width), F32),
            sds((LANES, width), F32),
        ),
        scratch_shapes=[pltpu.VMEM((rows, width), BF16)],
        compiler_params=params(),
        cost_estimate=cost(4 * rows * width * width, 20e6),
        name="mid_back",
    )(place, hidden, cotangent, gates_own, normed2, router, gain2, ow, *att, *nb_parts)

    kvw = 2 * kw
    wide = max(slab, qw, kvw)
    small_rows = 16

    def widen(part):
        return jnp.pad(part, ((0, 0),) * 3 + ((0, wide - part.shape[3]),))

    def rows_of(small):
        small = jnp.pad(small, ((0, ep * small_rows - small.shape[0]), (0, 0)))
        return widen(small.reshape(ep, small_rows, n, slab).transpose(2, 0, 1, 3).astype(BF16))

    def dense_sum(pieces):
        dense = jnp.concatenate(pieces, axis=2)
        depth = dense.shape[2]
        dense = dense.reshape(n, yx, 2, depth, wide).transpose(2, 1, 0, 3, 4)
        dense = plus(pick(dense, core, 0), swap(pick(dense, 1 - core, 0)))
        parts = to_owners([pick(dense, lax.bitwise_xor(chip, jnp.int32(j)), 0) for j in range(yx)])
        return sum(p.astype(F32) for p in parts).astype(BF16)

    moe_parts = to_owners(spread(moe_sum))
    att_grad = lax.all_to_all(att_grad, "shard", 0, 0)
    early = (owned[0], flip(owned[0], 1), flip(owned[0], 2))
    att_grad, grads = lax.optimization_barrier((att_grad, grads))
    owned.append(over_groups(grads))
    def with_mate(mine):
        return [p for one in mine for p in (one, swap(one))]

    def share(e, pieces, shared):
        def out_index(j, place_ref):
            return (peer(place_ref, j % 2, j // 2), e, 0, 0)

        return pl.pallas_call(
            functools.partial(share_kernel, ep),
            grid_spec=pltpu.PrefetchScalarGridSpec(
                num_scalar_prefetch=1,
                grid=(ep,),
                in_specs=[pl.BlockSpec((3 * slab, ff), lambda j, place_ref: (0, 0))] * ep + [hbm] * len(shared),
                out_specs=(
                    pl.BlockSpec((1, 1, slab, ff), out_index),
                    pl.BlockSpec((1, 1, slab, ff), out_index),
                    pl.BlockSpec((1, 1, ff // n, width), out_index),
                ),
            ),
            out_shape=(
                sds((ep, own, slab, ff), F32),
                sds((ep, own, slab, ff), F32),
                sds((ep, own, ff // n, width), F32),
            ),
            input_output_aliases={1 + ep + i: i for i in range(len(shared))},
            compiler_params=params(),
            cost_estimate=cost(0, 20e6),
            name="share",
        )(place, *pieces, *shared)

    raw = pl.pallas_call(
        functools.partial(back_kernel, rows, heads, kv_heads),
        out_shape=sds((seq, cols), F32),
        scratch_shapes=[
            pltpu.VMEM((heads, seq, HEAD), BF16),
            pltpu.VMEM((heads, seq, HEAD), F32),
            pltpu.VMEM((kv_heads, seq, HEAD), F32),
            pltpu.VMEM((kv_heads, seq, HEAD), F32),
        ],
        compiler_params=params(),
        cost_estimate=cost(2 * seq * width * cols, 52e6),
        name="back",
    )(q, k, v, lse, seg_col, seg_row, att_grad)
    raw, early = lax.optimization_barrier((raw, early))
    early = across_too(*early)
    ng, qkv_grad, gain_grad = pl.pallas_call(
        functools.partial(finish_kernel, rows, qw + kw),
        out_shape=(sds((seq, width), BF16), sds((width, cols), BF16), sds((1, width), F32)),
        scratch_shapes=[pltpu.VMEM((seq, cols), BF16)],
        compiler_params=params(),
        cost_estimate=cost(4 * seq * width * cols, 30e6),
        name="finish",
    )(raw, x_all, normed, w_qkv, cosine, sine)
    qkv_rows = qkv_grad.reshape(n, ep, part_rows, cols)
    shared = share(0, with_mate(early), ())
    part = lax.psum_scatter(ng, "shard", scatter_dimension=0, tiled=True).astype(F32)
    qkv_rows, moe_parts = lax.optimization_barrier((qkv_rows, moe_parts))
    small = rows_of(jnp.concatenate([gain_grad, ffn_grad, router_grad[:experts]], axis=0))
    ow_grad = widen(ow_grad.reshape(n, ep, ow_rows, slab))
    dense = dense_sum([ow_grad, small, widen(qkv_rows[..., :qw]), widen(qkv_rows[..., qw:])])
    if hi > 1:
        dense = lax.psum(dense.astype(F32), "hi").astype(BF16)
    dense, last, shared = lax.optimization_barrier((dense, owned[1:], shared))
    last = [with_mate(around(value)) for value in last]
    for e in range(1, own):
        shared = share(e, last[e - 1], shared)
    output = (hidden + sum(p.astype(F32) for p in moe_parts)).astype(BF16)


    dense = [pick(dense, z, 0)] + [shift(pick(dense, lax.rem(z + k, n), 0), k) for k in range(1, n)]
    cut = ow_rows + small_rows
    summed = sum(p[:cut].astype(F32) for p in dense).astype(BF16)
    kept = absolute([p[cut:] for p in dense]).reshape(n * 2 * part_rows, wide)
    mine = jnp.concatenate([summed, kept], axis=0)
    mine = [mine] + [flip(mine, j) for j in range(1, yx)]
    part, mine, shared = lax.optimization_barrier((part, mine, shared))
    mine = jnp.stack(mine)
    x = tokens.astype(F32)
    inv = inverse_rms(x)
    scaled = x * inv
    w1 = part * gain1
    input_grad = hidden_grad + inv * (w1 - scaled * jnp.mean(w1 * scaled, axis=-1, keepdims=True))

    both = jnp.stack([mine, swap(mine)], axis=1).reshape((ep,) + mine.shape[1:])
    full = jnp.stack([pick(both, lax.bitwise_xor(r, jnp.int32(i)), 0) for i in range(ep)])
    ow_full = full[:, :ow_rows, :slab].reshape(-1, slab).astype(F32)
    small_full = full[:, ow_rows:cut, :slab].reshape(-1, slab).astype(F32)
    kept = full[:, cut:].reshape(ep, n, 2, part_rows, wide)

    gate_grad, up_grad, down_grad = (g.reshape((experts,) + g.shape[2:]) for g in shared)

    def columns(which, start, size):
        part = kept[:, :, which, :, start : start + size]
        return part.transpose(0, 2, 1, 3).reshape(slab, n * size).astype(F32)

    return (
        output,
        input_grad,
        small_full[0],
        columns(0, 0, qw),
        columns(1, 0, kw),
        columns(1, kw, kw),
        ow_full,
        small_full[1],
        small_full[2 : 2 + experts].T,
        gate_grad,
        up_grad,
        down_grad,
    )


def solution(mesh):
    rep, n = mesh.shape["rep"], mesh.shape["shard"]
    yx = math.gcd(rep // 2, 4)
    hi = rep // (2 * yx)
    split = Mesh(mesh.devices.reshape(hi, yx, 2, n), ("hi", "yx", "cr", "shard"))
    rows = ("hi", "yx", "cr", "shard")
    placed = (
        P(rows, None),
        P(rows, None),
        P(rows),
        P(rows, None),
        P("shard"),
        P("shard", None),
        P("shard", None),
        P("shard", None),
        P(None, "shard"),
        P("shard"),
        P("shard", None),
        P(None, "shard", None),
        P(None, "shard", None),
        P(None, "shard", None),
    )
    return jax.shard_map(
        functools.partial(per_device, hi, yx, n),
        mesh=split,
        in_specs=placed,
        out_specs=(
            P(rows, None),
            P(rows, None),
            P("shard"),
            P("shard", None),
            P("shard", None),
            P("shard", None),
            P(None, "shard"),
            P("shard"),
            P("shard", None),
            P(None, "shard", None),
            P(None, "shard", None),
            P(None, "shard", None),
        ),
        check_vma=False,
    )
```

```python
import functools
import math

import jax
import jax.numpy as jnp
from jax import lax
from jax.experimental import pallas as pl
from jax.experimental.pallas import tpu as pltpu
from jax.sharding import Mesh
from jax.sharding import PartitionSpec as P

QUERY_HEADS = 16
KEY_VALUE_HEADS = 8
HEAD = 64
LANES = 128
MIX_LOW = 64
SCALE = 0.02

EPS = 1e-06
ROPE_BASE = 10000.0
MASKED = -1e30
F32 = jnp.float32
BF16 = jnp.bfloat16
NT = (((1,), (1,)), ((), ()))
TN = (((0,), (0,)), ((), ()))
VMEM_LIMIT = 60 * 1024 * 1024


def dot(a, b):
    return jnp.dot(a, b, preferred_element_type=F32)


def dot_nt(a, b):
    return lax.dot_general(a, b, NT, preferred_element_type=F32)


def dot_tn(a, b):
    return lax.dot_general(a, b, TN, preferred_element_type=F32)


def split_hi_lo(value):
    high = value.astype(BF16)
    return high, (value - high.astype(F32)).astype(BF16)


def inverse_rms(value):
    return lax.rsqrt(jnp.mean(value * value, axis=-1, keepdims=True) + EPS)


def swap_halves(value):
    width = value.shape[1]
    lane = lax.broadcasted_iota(jnp.int32, value.shape, 1)
    up = pltpu.roll(value, width - HEAD // 2, 1)
    down = pltpu.roll(value, HEAD // 2, 1)
    return jnp.where(lane % HEAD < HEAD // 2, up, down)


def rotate(value, cosine, sine):
    copies = value.shape[1] // LANES
    cosine = jnp.concatenate([cosine] * copies, axis=1)
    sine = jnp.concatenate([sine] * copies, axis=1)
    return value * cosine + swap_halves(value) * sine


def allowed_pairs(seg_col, seg_row, row0, count):
    rows = seg_col.shape[0]
    row = row0 + lax.broadcasted_iota(jnp.int32, (rows, count), 0)
    col = lax.broadcasted_iota(jnp.int32, (rows, count), 1)
    return (seg_col == seg_row) & (col <= row)


def ring_chunk(z, k, parts):
    return lax.rem(z - k + parts, parts)


def chunk_of(index, size):
    return pl.ds(pl.multiple_of(index * size, size), size)


def peer(place_ref, c, j):
    return lax.bitwise_xor(place_ref[2], jnp.int32(j)) * 2 + lax.bitwise_xor(place_ref[3], jnp.int32(c))


def front_kernel(
    block, heads, kv_heads, place_ref, x_ref, gain_ref, mine_ref, mate_ref, cos_ref, sin_ref, segc_ref, segr_ref,
    w_ref, normed_ref, q_ref, k_ref, v_ref, att_ref, lse_ref, out_s,
):
    seq = x_ref.shape[0]
    blocks = seq // block
    group = heads // kv_heads
    qw, kw = heads * HEAD, kv_heads * HEAD
    z = place_ref[0]
    slab = w_ref.shape[0] // blocks
    part = slab // (2 * mine_ref.shape[0])
    for c, piece_ref in enumerate((mine_ref, mate_ref)):
        for j in range(piece_ref.shape[0]):
            at = peer(place_ref, c, j) * part
            for i in range(blocks):
                start = pl.multiple_of(ring_chunk(z, i, blocks) * slab + at, part)
                w_ref[pl.ds(start, part), :] = piece_ref[j, i, :part, :]

    def project(i, carry):
        rows = pl.ds(pl.multiple_of(i * block, block), block)
        x = x_ref[rows, :].astype(F32)
        normed = (x * inverse_rms(x) * gain_ref[...]).astype(BF16)
        normed_ref[rows, :] = normed
        qkv = dot(normed, w_ref[...])
        turned = rotate(qkv[:, : qw + kw], cos_ref[rows, :], sin_ref[rows, :])
        for h in range(heads):
            q_ref[h, rows, :] = turned[:, h * HEAD : (h + 1) * HEAD].astype(BF16)
        for h in range(kv_heads):
            k_ref[h, rows, :] = turned[:, qw + h * HEAD : qw + (h + 1) * HEAD].astype(BF16)
            v_ref[h, rows, :] = qkv[:, qw + kw + h * HEAD : qw + kw + (h + 1) * HEAD].astype(BF16)
        return carry

    lax.fori_loop(0, blocks, project, 0)

    def one_head(h, carry):
        kv = h // group
        for i in range(blocks):
            count = (i + 1) * block
            rows = slice(i * block, (i + 1) * block)
            q = q_ref[h, rows, :] * jnp.asarray(0.125, BF16)
            k = k_ref[kv, :count, :]
            v = v_ref[kv, :count, :]
            allowed = allowed_pairs(segc_ref[rows, :], segr_ref[:, :count], i * block, count)
            s = jnp.where(allowed, dot_nt(q, k), MASKED)
            top = jnp.max(s, axis=-1, keepdims=True)
            e = jnp.exp(s - top)
            total = jnp.sum(e, axis=-1, keepdims=True)
            lse_ref[h, rows, :] = top + jnp.log(total)
            p = (e * (1.0 / total)).astype(BF16)
            out_s[h, rows, :] = dot(p, v)
        return carry

    lax.fori_loop(0, heads, one_head, 0)
    for i in range(blocks):
        k = lax.rem(i - z + blocks, blocks)
        for h in range(heads):
            att_ref[k, :, h * HEAD : (h + 1) * HEAD] = out_s[h, i * block : (i + 1) * block, :].astype(BF16)


def back_kernel(
    block, heads, kv_heads, place_ref, q_ref, k_ref, v_ref, lse_ref, segc_ref, segr_ref, *refs
):
    seq = q_ref.shape[1]
    blocks = seq // block
    raw_ref, do_s, dq_s, dk_s, dv_s = refs[blocks:]
    group = heads // kv_heads
    qw, kw = heads * HEAD, kv_heads * HEAD
    for k in range(blocks):
        at = chunk_of(lax.rem(place_ref[0] + k, blocks), block)
        for h in range(heads):
            do_s[h, at, :] = refs[k][:, h * HEAD : (h + 1) * HEAD]
    dk_s[...] = jnp.zeros_like(dk_s)
    dv_s[...] = jnp.zeros_like(dv_s)

    def one_head(h, carry):
        kv = h // group
        for i in range(blocks):
            count = (i + 1) * block
            rows = slice(i * block, (i + 1) * block)
            q = q_ref[h, rows, :] * jnp.asarray(0.125, BF16)
            k = k_ref[kv, :count, :]
            v = v_ref[kv, :count, :]
            do = do_s[h, rows, :]
            allowed = allowed_pairs(segc_ref[rows, :], segr_ref[:, :count], i * block, count)
            s = jnp.where(allowed, dot_nt(q, k), MASKED)
            prob = jnp.exp(s - lse_ref[h, rows, :])
            grad = dot_nt(do, v)
            inner = jnp.sum(prob * grad, axis=-1, keepdims=True)
            ds = (prob * (grad - inner)).astype(BF16)
            dq_s[h, rows, :] = dot(ds, k) * 0.125
            dk_s[kv, :count, :] += dot_tn(ds, q)
            dv_s[kv, :count, :] += dot_tn(prob.astype(BF16), do)
        return carry

    lax.fori_loop(0, heads, one_head, 0)
    for h in range(heads):
        raw_ref[:, h * HEAD : (h + 1) * HEAD] = dq_s[h]
    for h in range(kv_heads):
        raw_ref[:, qw + h * HEAD : qw + (h + 1) * HEAD] = dk_s[h]
        raw_ref[:, qw + kw + h * HEAD : qw + kw + (h + 1) * HEAD] = dv_s[h]


def finish_kernel(
    block, turned, raw_ref, x_ref, normed_ref, w_ref, cos_ref, sin_ref, ng_ref, dw_ref, gain_ref, g_s,
):
    seq = x_ref.shape[0]
    blocks = seq // block
    gain_ref[...] = jnp.zeros_like(gain_ref)

    def finish(i, carry):
        rows = pl.ds(pl.multiple_of(i * block, block), block)
        g_s[rows, :turned] = rotate(raw_ref[rows, :turned], cos_ref[rows, :], -sin_ref[rows, :]).astype(BF16)
        g_s[rows, turned:] = raw_ref[rows, turned:].astype(BF16)
        ng = dot_nt(g_s[rows, :], w_ref[...])
        x = x_ref[rows, :].astype(F32)
        gain_ref[...] += jnp.sum(ng * (x * inverse_rms(x)), axis=0, keepdims=True)
        ng_ref[rows, :] = ng.astype(BF16)
        return carry

    lax.fori_loop(0, blocks, finish, 0)
    width = normed_ref.shape[1]
    for c in range(0, width, 256):
        dw_ref[c : c + 256, :] = dot_tn(normed_ref[:, c : c + 256], g_s[...]).astype(BF16)


def softmax_gates(logits, mask):
    shown = jnp.where(mask > 0.0, logits, MASKED)
    e = jnp.where(mask > 0.0, jnp.exp(shown - jnp.max(shown, axis=-1, keepdims=True)), 0.0)
    return e * (1.0 / jnp.sum(e, axis=-1, keepdims=True))


def mid_kernel(
    place_ref, x_ref, mine_ref, mate_ref, gain_ref, router_ref, mask_ref, *refs
):
    hidden_ref, normed_ref, gates_ref, ow_ref = refs[-4:]
    att_refs = refs[:-4]
    parts, width = ow_ref.shape[0], ow_ref.shape[2]
    share = ow_ref.shape[1] // (2 * mine_ref.shape[0])
    fold = mine_ref.shape[3] // width
    lines = share // fold
    skip = ow_ref.shape[0] * width // (2 * parts * mine_ref.shape[0])
    for c, piece_ref in enumerate((mine_ref, mate_ref)):
        for j in range(piece_ref.shape[0]):
            at = peer(place_ref, c, j) * share
            for k in range(parts):
                for f in range(fold):
                    start = pl.multiple_of(at + f * lines, lines)
                    ow_ref[k, pl.ds(start, lines), :] = piece_ref[j, k, skip : skip + lines, f * width : (f + 1) * width]
    depth = att_refs[0].shape[1]
    for j in range(parts):
        cols = chunk_of(ring_chunk(place_ref[0], j, parts), width)
        total = x_ref[:, cols].astype(F32)
        for i in range(parts):
            at = chunk_of(ring_chunk(place_ref[0], i, parts), depth)
            total = total + dot(att_refs[i][...], ow_ref[j, at, :])
        hidden_ref[:, cols] = total
    hidden = hidden_ref[...]
    normed = (hidden * inverse_rms(hidden) * gain_ref[...]).astype(BF16)
    normed_ref[...] = normed
    gates_ref[...] = softmax_gates(dot(normed, router_ref[...]), mask_ref[...])


def mid_back_kernel(
    place_ref, hidden_ref, dy_ref, gates_ref, normed_ref, router_ref, gain_ref, ow_ref, *refs
):
    hg_ref, ag_ref, owg_ref, fg_ref, rg_ref, aog_s = refs[-6:]
    att_refs = refs[: ow_ref.shape[0]]
    nb_refs = refs[ow_ref.shape[0] : -6]
    gates = gates_ref[...]
    width_all = hidden_ref.shape[1]
    nb = sum(ref[...].astype(F32) for ref in nb_refs)
    mix = nb[:, width_all:]
    mix = mix + pltpu.roll(mix, LANES - MIX_LOW, 1)
    lg = gates * (mix - jnp.sum(gates * mix, axis=-1, keepdims=True))
    high, low = split_hi_lo(lg)
    normed = normed_ref[...]
    rg_ref[...] = dot_tn(high, normed) + dot_tn(low, normed)
    router = router_ref[...]
    ng = nb[:, :width_all] + dot_nt(high, router) + dot_nt(low, router)
    hidden = hidden_ref[...]
    inv = inverse_rms(hidden)
    scaled = hidden * inv
    fg_ref[...] = jnp.sum(ng * scaled, axis=0, keepdims=True)
    w = ng * gain_ref[...]
    hg = dy_ref[...].astype(F32) + inv * (w - scaled * jnp.mean(w * scaled, axis=-1, keepdims=True))
    hg_ref[...] = hg
    aog_s[...] = hg.astype(BF16)
    parts, width = ow_ref.shape[0], ow_ref.shape[2]
    depth = att_refs[0].shape[1]
    for i in range(parts):
        group = ring_chunk(place_ref[0], i, parts)
        rows = chunk_of(group, depth)
        total = None
        for j in range(parts):
            chunk = ring_chunk(place_ref[0], j, parts)
            part = dot_nt(aog_s[:, chunk_of(chunk, width)], ow_ref[j, rows, :])
            total = part if total is None else total + part
        ag_ref[i] = total.astype(BF16)
        for j in range(parts):
            owg_ref[j, rows, :] = dot_tn(att_refs[i][...], aog_s[:, j * width : (j + 1) * width]).astype(BF16)


def expert_kernel(parts, e, place_ref, n2_ref, dyx_ref, router_ref, w_ref, *refs):
    previous = refs[:2] if e else ()
    moe_ref, nb_ref, g_ref, inner_ref, gg_ref, ug_ref, wg_s, wu_s, wd_s, sems = refs[len(previous) :]
    width, ff = wg_s.shape
    slab, ff_slab = width // parts, ff // parts

    first_step = pl.program_id(0) == 0

    def move(start, count, target, sem):
        return pltpu.make_async_copy(w_ref.at[start : start + count, :], target, sems.at[sem])

    gate_copies, up_copies, down_copies = [], [], []
    for k in range(parts):
        start = k * 3 * slab
        rows = slice(k * slab, (k + 1) * slab)
        gate_copies.append(move(start, slab, wg_s.at[rows, :], k))
        up_copies.append(move(start + slab, slab, wu_s.at[rows, :], parts + k))
        for c in range(width // ff):
            at = start + 2 * slab + c * ff_slab
            target = wd_s.at[k * ff_slab : (k + 1) * ff_slab, c * ff : (c + 1) * ff]
            down_copies.append(move(at, ff_slab, target, (2 + c) * parts + k))

    @pl.when(first_step)
    def load():
        for copy in gate_copies + up_copies + down_copies:
            copy.start()

    def ready(copies):
        @pl.when(first_step)
        def wait():
            for copy in copies:
                copy.wait()

    x = n2_ref[...]
    dy = dyx_ref[:, :width].astype(F32)
    gates = softmax_gates(dot(x, router_ref[...]), dyx_ref[:, width:].astype(F32))
    lane = lax.broadcasted_iota(jnp.int32, gates.shape, 1)
    at = place_ref[1] + e
    g = jnp.sum(jnp.where(lane == at, gates, 0.0), axis=-1, keepdims=True)
    ready(gate_copies)
    ga = dot(x, wg_s[...])
    ready(up_copies)
    ua = dot(x, wu_s[...])
    sg = jax.nn.sigmoid(ga)
    act = ga * sg
    inner = (act * ua).astype(BF16)
    inner_ref[...] = inner
    ready(down_copies)
    eo = dot(inner, wd_s[...]).astype(BF16).astype(F32)
    moe = g * eo
    high, low = split_hi_lo(jnp.sum(dy * eo, axis=-1, keepdims=True))
    mix = jnp.where(lane == at, high.astype(F32), 0.0) + jnp.where(lane == MIX_LOW + at, low.astype(F32), 0.0)
    g_ref[...] = jnp.where(lane == 0, g, 0.0)
    ig = dot_nt((g * dy).astype(BF16), wd_s[...])
    gg = (ig * ua * sg * (1.0 + ga * (1.0 - sg))).astype(BF16)
    ug = (ig * act).astype(BF16)
    gg_ref[...] = gg
    ug_ref[...] = ug
    nb = dot_nt(gg, wg_s[...]) + dot_nt(ug, wu_s[...])
    if e:
        moe = moe + previous[0][...].astype(F32)
        nb = nb + previous[1][:, :width].astype(F32)
        mix = mix + previous[1][:, width:].astype(F32)
    moe_ref[...] = moe.astype(BF16)
    nb_ref[:, :width] = nb.astype(BF16)
    nb_ref[:, width:] = mix.astype(BF16)


def expert_grad_kernel(parts, half, *refs):
    halves = (refs[:6], refs[6:12])
    out_ref, g_s, u_s, d_s = refs[12:]
    step = pl.program_id(0)
    width, ff = g_s.shape
    slab, ff_slab = width // parts, ff // parts

    @pl.when(step == 0)
    def clear():
        g_s[...] = jnp.zeros_like(g_s)
        u_s[...] = jnp.zeros_like(u_s)
        d_s[...] = jnp.zeros_like(d_s)

    def add(n2_ref, dyx_ref, g_ref, inner_ref, gg_ref, ug_ref):
        x = n2_ref[...]
        g = jnp.sum(g_ref[...], axis=-1, keepdims=True)
        og = (g * dyx_ref[:, :width].astype(F32)).astype(BF16)
        g_s[...] += dot_tn(x, gg_ref[...])
        u_s[...] += dot_tn(x, ug_ref[...])
        d_s[...] += dot_tn(inner_ref[...], og)

    pl.when(step < half)(lambda: add(*halves[0]))
    pl.when(step >= half)(lambda: add(*halves[1]))

    @pl.when(step == pl.num_programs(0) - 1)
    def store():
        for k in range(parts):
            start = k * 3 * slab
            out_ref[start : start + slab, :] = g_s[k * slab : (k + 1) * slab, :].astype(BF16)
            out_ref[start + slab : start + 2 * slab, :] = u_s[k * slab : (k + 1) * slab, :].astype(BF16)
            for c in range(width // ff):
                at = start + 2 * slab + c * ff_slab
                out_ref[at : at + ff_slab, :] = d_s[k * ff_slab : (k + 1) * ff_slab, c * ff : (c + 1) * ff].astype(BF16)


def share_kernel(count, place_ref, *refs):
    gate_ref, up_ref, down_ref = refs[-3:]
    _, _, slab, ff = gate_ref.shape
    ff_slab, width = down_ref.shape[2:]
    for i in range(count):

        @pl.when(pl.program_id(0) == i)
        def copy(piece_ref=refs[i]):
            gate_ref[0, 0] = piece_ref[:slab, :].astype(F32)
            up_ref[0, 0] = piece_ref[slab : 2 * slab, :].astype(F32)
            for c in range(width // ff):
                at = 2 * slab + c * ff_slab
                down_ref[0, 0, :, c * ff : (c + 1) * ff] = piece_ref[at : at + ff_slab, :].astype(F32)


def sds(shape, dtype):
    return jax.ShapeDtypeStruct(shape, dtype)


def params():
    return pltpu.CompilerParams(vmem_limit_bytes=VMEM_LIMIT)


def cost(flops, traffic):
    return pl.CostEstimate(flops=int(flops * SCALE), bytes_accessed=int(traffic * SCALE), transcendentals=0)


def per_device(
    hi, yx, n, tokens, cotangent, segment_ids, routes, attn_gain, query_weight, key_matrix, value_weight,
    out_weight, ffn_gain, router_weight, gate_weight, up_weight, down_weight,
):
    rows, width = tokens.shape
    seq = rows * n
    experts = gate_weight.shape[0]
    ep = yx * 2
    own = experts // ep
    heads, kv_heads = QUERY_HEADS // n, KEY_VALUE_HEADS // n
    qw, kw = heads * HEAD, kv_heads * HEAD
    cols = qw + 2 * kw
    slab = width // n
    ff = gate_weight.shape[2]
    z = lax.axis_index("shard").astype(jnp.int32)
    core = lax.axis_index("cr").astype(jnp.int32)
    chip = lax.axis_index("yx").astype(jnp.int32)
    r = chip * 2 + core
    place = jnp.stack([z, r * own, chip, core])
    smem = pl.BlockSpec(memory_space=pltpu.SMEM)
    vmem = pl.BlockSpec(memory_space=pltpu.VMEM)
    hbm = pl.BlockSpec(memory_space=pl.ANY)

    def shift(value, k=1):
        return lax.ppermute(value, "shard", [(i, (i + k) % n) for i in range(n)])

    def swap(value):
        return lax.ppermute(value, "cr", [(0, 1), (1, 0)])

    def flip(value, j):
        return lax.ppermute(value, "yx", [(i, i ^ j) for i in range(yx)])

    def pick(value, index, axis):
        return lax.dynamic_index_in_dim(value, index, axis, keepdims=False)

    def absolute(parts):
        stacked = jnp.stack(parts)
        return jnp.stack([pick(stacked, lax.rem(z - j + n, n), 0) for j in range(n)])

    def plus(one, other):
        return (one.astype(F32) + other.astype(F32)).astype(BF16)

    def around(value):
        return across_too(value, flip(value, 1), flip(value, 2))

    def across_too(value, by_x, by_y):
        half = value.shape[0] // 2
        across = jnp.concatenate([flip(by_x[:half], 2), flip(by_y[half:], 1)], axis=0)
        return [value, by_x, by_y, across]

    def to_owners(blocks):
        return [blocks[0]] + [flip(blocks[j], j) for j in range(1, yx)]

    x_all = lax.all_gather(tokens, "shard", axis=0, tiled=True)

    pack = jnp.concatenate(
        [attn_gain[None], ffn_gain[None], segment_ids.astype(BF16)[None], router_weight.T], axis=0
    )
    pack_rows = 16
    pack = jnp.pad(pack, ((0, 2 * pack_rows - pack.shape[0]), (0, 0)))
    pack = jnp.concatenate([pack[:pack_rows], pack[pack_rows:]], axis=1)
    part_rows = slab // ep
    by_dest = jnp.concatenate(
        [
            lax.dynamic_slice_in_dim(w, r * part_rows, part_rows, axis=0).reshape(part_rows, n, -1)
            for w in (query_weight, key_matrix, value_weight)
        ],
        axis=2,
    )
    ow_rows = out_weight.shape[0] // ep
    fold = cols // slab
    ow_mine = lax.dynamic_slice_in_dim(out_weight, r * ow_rows, ow_rows, axis=0)
    ow_mine = ow_mine.reshape(fold, ow_rows // fold, slab).transpose(1, 0, 2).reshape(ow_rows // fold, cols)

    def piece(k):
        return jnp.concatenate([pick(by_dest, lax.rem(z + k, n), 1), ow_mine, pack], axis=0)

    dense_mine = [piece(0)] + [shift(piece(k), k) for k in range(1, n)]
    ids = jnp.arange(experts, dtype=jnp.int32)
    routed = jnp.any(routes[:, :, None] == ids[None, None, :], axis=1)
    mask_own = jnp.pad(routed.astype(F32), ((0, 0), (0, LANES - experts)))
    dyx_mine = around(jnp.concatenate([cotangent, mask_own.astype(BF16)], axis=1))

    folds = width // ff
    packed = []
    for e in range(own):
        gate, up, down = (pick(w, r * own + e, 0) for w in (gate_weight, up_weight, down_weight))
        down = [down[:, c * ff : (c + 1) * ff] for c in range(folds)]
        packed.append(jnp.concatenate([gate, up] + down, axis=0))
    packed, dense_mine = lax.optimization_barrier((packed, dense_mine))
    weights = [lax.all_gather(w, "shard", axis=0, tiled=True) for w in packed]

    packs = absolute([p[-pack_rows:] for p in dense_mine])
    packs = jnp.concatenate([packs[:, :, :slab], packs[:, :, slab : 2 * slab]], axis=1)
    dense_mine = jnp.stack(around(jnp.stack([p[:-pack_rows] for p in dense_mine])))
    dense_mate = swap(dense_mine)
    gain1 = packs[:, 0, :].reshape(1, width).astype(F32)
    gain2 = packs[:, 1, :].reshape(1, width).astype(F32)
    segments = packs[:, 2, :].reshape(seq).astype(F32)
    seg_col, seg_row = segments[:, None], segments[None, :]
    router = jnp.pad(packs[:, 3 : 3 + experts, :].transpose(0, 2, 1).reshape(width, experts), ((0, 0), (0, LANES - experts)))


    positions = jnp.arange(seq, dtype=jnp.int32).astype(F32)
    frequency = ROPE_BASE ** (-jnp.arange(HEAD // 2, dtype=F32) / (HEAD // 2))
    angles = positions[:, None] * frequency[None, :]
    cosine, sine = jnp.cos(angles), jnp.sin(angles)
    cosine = jnp.concatenate([cosine] * 4, axis=1)
    sine = jnp.concatenate([-sine, sine] * 2, axis=1)

    x_all, dyx_mine = lax.optimization_barrier((x_all, dyx_mine))
    dyx_mine = jnp.concatenate(dyx_mine, axis=0)
    dyx_mate = swap(dyx_mine)
    w_qkv, normed, q, k, v, att, lse = pl.pallas_call(
        functools.partial(front_kernel, rows, heads, kv_heads),
        in_specs=[smem] + [vmem] * 8,
        out_shape=(
            sds((width, cols), BF16),
            sds((seq, width), BF16),
            sds((heads, seq, HEAD), BF16),
            sds((kv_heads, seq, HEAD), BF16),
            sds((kv_heads, seq, HEAD), BF16),
            sds((n, rows, qw), BF16),
            sds((heads, seq, 1), F32),
        ),
        scratch_shapes=[pltpu.VMEM((heads, seq, HEAD), F32)],
        compiler_params=params(),
        cost_estimate=cost(2 * seq * width * cols, 60e6),
        name="front",
    )(place, x_all, gain1, dense_mine, dense_mate, cosine, sine, seg_col, seg_row)

    att = [att[0]] + [shift(att[k], k) for k in range(1, n)]
    hidden, normed2, gates_own, ow = pl.pallas_call(
        mid_kernel,
        in_specs=[smem] + [vmem] * (6 + n),
        out_shape=(
            sds((rows, width), F32),
            sds((rows, width), BF16),
            sds((rows, LANES), F32),
            sds((n, ep * ow_rows, slab), BF16),
        ),
        compiler_params=params(),
        cost_estimate=cost(2 * rows * width * width, 14e6),
        name="mid",
    )(place, tokens, dense_mine, dense_mate, gain2, router, mask_own, *att)

    n2_mine = jnp.concatenate(around(normed2), axis=0)
    n2_mate = swap(n2_mine)

    total = yx * rows
    block = min(512, total)
    steps = total // block

    def by_block(size):
        return pl.BlockSpec((block, size), lambda i: (i, 0))

    def run_expert(e, n2, dyx, previous):
        return pl.pallas_call(
            functools.partial(expert_kernel, n, e),
            grid=(steps,),
            in_specs=[
                smem,
                by_block(width),
                by_block(width + LANES),
                pl.BlockSpec((width, LANES), lambda i: (0, 0)),
                hbm,
            ]
            + ([by_block(width), by_block(width + LANES)] if e else []),
            out_specs=(
                by_block(width),
                by_block(width + LANES),
                by_block(LANES),
                by_block(ff),
                by_block(ff),
                by_block(ff),
            ),
            out_shape=(
                sds((total, width), BF16),
                sds((total, width + LANES), BF16),
                sds((total, LANES), F32),
                sds((total, ff), BF16),
                sds((total, ff), BF16),
                sds((total, ff), BF16),
            ),
            scratch_shapes=[
                pltpu.VMEM((width, ff), BF16),
                pltpu.VMEM((width, ff), BF16),
                pltpu.VMEM((ff, width), BF16),
                pltpu.SemaphoreType.DMA(((2 + folds) * n,)),
            ],
            compiler_params=params(),
            cost_estimate=cost(12 * total * width * ff, 36e6),
            name="expert",
        )(place, n2, dyx, router, weights[e], *previous)

    def half_specs(at):
        sizes = (width, width + LANES, LANES, ff, ff, ff)
        return [pl.BlockSpec((block, size), lambda i: (at(i), 0)) for size in sizes]

    def weight_grads(mate, mine):
        return pl.pallas_call(
            functools.partial(expert_grad_kernel, n, steps),
            grid=(2 * steps,),
            in_specs=half_specs(lambda i: jnp.minimum(i, steps - 1))
            + half_specs(lambda i: jnp.maximum(i - steps, 0)),
            out_specs=pl.BlockSpec((3 * width, ff), lambda i: (0, 0)),
            out_shape=sds((3 * width, ff), BF16),
            scratch_shapes=[
                pltpu.VMEM((width, ff), F32),
                pltpu.VMEM((width, ff), F32),
                pltpu.VMEM((ff, width), F32),
            ],
            compiler_params=params(),
            cost_estimate=cost(12 * total * width * ff, 40e6),
            name="expert_grads",
        )(n2_mate, dyx_mate, *mate, n2_mine, dyx_mine, *mine)

    def over_groups(grads):
        grads = lax.psum_scatter(grads, "shard", scatter_dimension=0, tiled=True)
        return lax.psum(grads.astype(F32), "hi").astype(BF16) if hi > 1 else grads

    def spread(value):
        return [value[j * rows : (j + 1) * rows] for j in range(yx)]

    previous_mate = previous_mine = ()
    owned = []
    for e in range(own):
        *previous_mate, g_mate, in_mate, gg_mate, ug_mate = run_expert(e, n2_mate, dyx_mate, previous_mate)
        if e == own - 1:
            moe_got, nb_got = swap(previous_mate[0]), swap(previous_mate[1])
        *previous_mine, g_mine, in_mine, gg_mine, ug_mine = run_expert(e, n2_mine, dyx_mine, previous_mine)
        grads = weight_grads((g_mate, in_mate, gg_mate, ug_mate), (g_mine, in_mine, gg_mine, ug_mine))
        if e < own - 1:
            grads, weights[e + 1] = lax.optimization_barrier((grads, weights[e + 1]))
        else:
            nb_parts = to_owners(spread(plus(previous_mine[1], nb_got)))
            moe_sum = plus(previous_mine[0], moe_got)
            nb_parts, moe_sum, grads, owned = lax.optimization_barrier((nb_parts, moe_sum, grads, owned))
        if e < own - 1:
            owned.append(over_groups(grads))

    hidden_grad, att_grad, ow_grad, ffn_grad, router_grad = pl.pallas_call(
        mid_back_kernel,
        in_specs=[smem] + [vmem] * (7 + n + yx),
        out_shape=(
            sds((rows, width), F32),
            sds((n, rows, qw), BF16),
            sds((n, n * qw, slab), BF16),
            sds((1, width), F32),
            sds((LANES, width), F32),
        ),
        scratch_shapes=[pltpu.VMEM((rows, width), BF16)],
        compiler_params=params(),
        cost_estimate=cost(4 * rows * width * width, 20e6),
        name="mid_back",
    )(place, hidden, cotangent, gates_own, normed2, router, gain2, ow, *att, *nb_parts)

    kvw = 2 * kw
    wide = max(slab, qw, kvw)
    small_rows = 16

    def widen(part):
        return jnp.pad(part, ((0, 0),) * 3 + ((0, wide - part.shape[3]),))

    def rows_of(small):
        small = jnp.pad(small, ((0, ep * small_rows - small.shape[0]), (0, 0)))
        return widen(small.reshape(ep, small_rows, n, slab).transpose(2, 0, 1, 3).astype(BF16))

    def dense_sum(pieces):
        dense = jnp.concatenate(pieces, axis=2)
        depth = dense.shape[2]
        dense = dense.reshape(n, yx, 2, depth, wide).transpose(2, 1, 0, 3, 4)
        dense = plus(pick(dense, core, 0), swap(pick(dense, 1 - core, 0)))
        parts = to_owners([pick(dense, lax.bitwise_xor(chip, jnp.int32(j)), 0) for j in range(yx)])
        return sum(p.astype(F32) for p in parts).astype(BF16)

    moe_parts = to_owners(spread(moe_sum))
    att_grad = [att_grad[0]] + [shift(att_grad[k], n - k) for k in range(1, n)]
    early = (owned[0], flip(owned[0], 1), flip(owned[0], 2))
    att_grad, grads = lax.optimization_barrier((att_grad, grads))
    owned.append(over_groups(grads))
    def with_mate(mine):
        return [p for one in mine for p in (one, swap(one))]

    def share(e, pieces, shared):
        def out_index(j, place_ref):
            return (peer(place_ref, j % 2, j // 2), e, 0, 0)

        return pl.pallas_call(
            functools.partial(share_kernel, ep),
            grid_spec=pltpu.PrefetchScalarGridSpec(
                num_scalar_prefetch=1,
                grid=(ep,),
                in_specs=[pl.BlockSpec((3 * slab, ff), lambda j, place_ref: (0, 0))] * ep + [hbm] * len(shared),
                out_specs=(
                    pl.BlockSpec((1, 1, slab, ff), out_index),
                    pl.BlockSpec((1, 1, slab, ff), out_index),
                    pl.BlockSpec((1, 1, ff // n, width), out_index),
                ),
            ),
            out_shape=(
                sds((ep, own, slab, ff), F32),
                sds((ep, own, slab, ff), F32),
                sds((ep, own, ff // n, width), F32),
            ),
            input_output_aliases={1 + ep + i: i for i in range(len(shared))},
            compiler_params=params(),
            cost_estimate=cost(0, 20e6),
            name="share",
        )(place, *pieces, *shared)

    raw = pl.pallas_call(
        functools.partial(back_kernel, rows, heads, kv_heads),
        in_specs=[smem] + [vmem] * (6 + n),
        out_shape=sds((seq, cols), F32),
        scratch_shapes=[
            pltpu.VMEM((heads, seq, HEAD), BF16),
            pltpu.VMEM((heads, seq, HEAD), F32),
            pltpu.VMEM((kv_heads, seq, HEAD), F32),
            pltpu.VMEM((kv_heads, seq, HEAD), F32),
        ],
        compiler_params=params(),
        cost_estimate=cost(2 * seq * width * cols, 52e6),
        name="back",
    )(place, q, k, v, lse, seg_col, seg_row, *att_grad)
    raw, early = lax.optimization_barrier((raw, early))
    early = across_too(*early)
    ng, qkv_grad, gain_grad = pl.pallas_call(
        functools.partial(finish_kernel, rows, qw + kw),
        out_shape=(sds((seq, width), BF16), sds((width, cols), BF16), sds((1, width), F32)),
        scratch_shapes=[pltpu.VMEM((seq, cols), BF16)],
        compiler_params=params(),
        cost_estimate=cost(4 * seq * width * cols, 30e6),
        name="finish",
    )(raw, x_all, normed, w_qkv, cosine, sine)
    qkv_rows = qkv_grad.reshape(n, ep, part_rows, cols)
    shared = share(0, with_mate(early), ())
    part = lax.psum_scatter(ng, "shard", scatter_dimension=0, tiled=True).astype(F32)
    qkv_rows, moe_parts = lax.optimization_barrier((qkv_rows, moe_parts))
    small = rows_of(jnp.concatenate([gain_grad, ffn_grad, router_grad[:experts]], axis=0))
    ow_grad = widen(ow_grad.reshape(n, ep, ow_rows, slab))
    dense = dense_sum([ow_grad, small, widen(qkv_rows[..., :qw]), widen(qkv_rows[..., qw:])])
    if hi > 1:
        dense = lax.psum(dense.astype(F32), "hi").astype(BF16)
    dense, last, shared = lax.optimization_barrier((dense, owned[1:], shared))
    last = [with_mate(around(value)) for value in last]
    for e in range(1, own):
        shared = share(e, last[e - 1], shared)
    output = (hidden + sum(p.astype(F32) for p in moe_parts)).astype(BF16)


    dense = [pick(dense, z, 0)] + [shift(pick(dense, lax.rem(z + k, n), 0), k) for k in range(1, n)]
    cut = ow_rows + small_rows
    summed = sum(p[:cut].astype(F32) for p in dense).astype(BF16)
    kept = absolute([p[cut:] for p in dense]).reshape(n * 2 * part_rows, wide)
    mine = jnp.concatenate([summed, kept], axis=0)
    mine = [mine] + [flip(mine, j) for j in range(1, yx)]
    part, mine, shared = lax.optimization_barrier((part, mine, shared))
    mine = jnp.stack(mine)
    x = tokens.astype(F32)
    inv = inverse_rms(x)
    scaled = x * inv
    w1 = part * gain1
    input_grad = hidden_grad + inv * (w1 - scaled * jnp.mean(w1 * scaled, axis=-1, keepdims=True))

    both = jnp.stack([mine, swap(mine)], axis=1).reshape((ep,) + mine.shape[1:])
    full = jnp.stack([pick(both, lax.bitwise_xor(r, jnp.int32(i)), 0) for i in range(ep)])
    ow_full = full[:, :ow_rows, :slab].reshape(-1, slab).astype(F32)
    small_full = full[:, ow_rows:cut, :slab].reshape(-1, slab).astype(F32)
    kept = full[:, cut:].reshape(ep, n, 2, part_rows, wide)

    gate_grad, up_grad, down_grad = (g.reshape((experts,) + g.shape[2:]) for g in shared)

    def columns(which, start, size):
        part = kept[:, :, which, :, start : start + size]
        return part.transpose(0, 2, 1, 3).reshape(slab, n * size).astype(F32)

    return (
        output,
        input_grad,
        small_full[0],
        columns(0, 0, qw),
        columns(1, 0, kw),
        columns(1, kw, kw),
        ow_full,
        small_full[1],
        small_full[2 : 2 + experts].T,
        gate_grad,
        up_grad,
        down_grad,
    )


def solution(mesh):
    rep, n = mesh.shape["rep"], mesh.shape["shard"]
    yx = math.gcd(rep // 2, 4)
    hi = rep // (2 * yx)
    split = Mesh(mesh.devices.reshape(hi, yx, 2, n), ("hi", "yx", "cr", "shard"))
    rows = ("hi", "yx", "cr", "shard")
    placed = (
        P(rows, None),
        P(rows, None),
        P(rows),
        P(rows, None),
        P("shard"),
        P("shard", None),
        P("shard", None),
        P("shard", None),
        P(None, "shard"),
        P("shard"),
        P("shard", None),
        P(None, "shard", None),
        P(None, "shard", None),
        P(None, "shard", None),
    )
    return jax.shard_map(
        functools.partial(per_device, hi, yx, n),
        mesh=split,
        in_specs=placed,
        out_specs=(
            P(rows, None),
            P(rows, None),
            P("shard"),
            P("shard", None),
            P("shard", None),
            P("shard", None),
            P(None, "shard"),
            P("shard"),
            P("shard", None),
            P(None, "shard", None),
            P(None, "shard", None),
            P(None, "shard", None),
        ),
        check_vma=False,
    )
```
